128 devices in a mesh: gx: 8 (over z, core), gy: 16 (over x, y).
Axes of the slice: x: 4, y: 4, z: 4, core: 2. Of those that a mesh axis runs over, the one named last changes fastest.
Arguments:
- sources: float32 [2, 2048, 2048], P(None, 'gx', 'gy'), may hold values from -4 to 4
- metric: float32 [2048, 2048], P('gx', 'gy'), may hold values from 0.6 to 1.5
- helm: float32 [2048, 2048], P('gx', 'gy'), may hold values from 0.002 to 0.02
Outputs:
- solution: float32 [2, 2048, 2048], P(None, 'gx', 'gy')
- resid: float32 [2, 2048, 2048], P(None, 'gx', 'gy')
The draws below stay inside these ranges and needn't reach their ends.
All inputs are finite; a program needn't handle non-finite values.
Results may differ from the reference program's by a relative error of at most 0.0009.
Values sent between devices are 32-bit elements; how exact they have to be, the bound alone decides.
No kernel may reach another device: no remote copies, remote signals or barrier semaphores. Data moves between devices by JAX's collectives and lax.ppermute only.
A program may use at most 128 MiB of HBM per device.

```python
import math
import jax
import jax.numpy as jnp
from jax import lax

LEVELS = 1
ITERS = 2
NX = 2048
NY = 2048


def draw_sources(key, part):
    key = jax.random.fold_in(key, 7)
    across = jnp.arange(NX, dtype=jnp.float32) / NX
    down = jnp.arange(NY, dtype=jnp.float32) / NY
    ramp = 1.0 + across[:, None] + down[None, :]
    shape = (2 * LEVELS, NX, NY)
    return 0.3 * jnp.clip(jax.random.normal(key, shape, jnp.float32), -4.0, 4.0) * ramp


def levels(key, extent, pieces, least, high):
    gain = 1.0
    for dim, blocks in pieces:
        steps = jax.random.uniform(jax.random.fold_in(jax.random.fold_in(key, 6), dim), (blocks,), jnp.float32, least / len(pieces), high / len(pieces))
        gain = gain * jnp.repeat(jnp.exp(steps), extent[dim] // blocks).reshape((-1,) + (1,) * (len(extent) - 1 - dim))
    return gain


def setup_inputs(seed: int = 0) -> dict:
    key_list = jax.random.split(jax.random.key(seed), 4)
    return {
        "sources": draw_sources(jax.random.fold_in(key_list[3], 71), 0),
        "metric": jnp.clip(jnp.exp(math.log(1.5) - 0.9162907 * jax.random.uniform(key_list[1], (NX, NY), jnp.float32) ** levels(key_list[1], (NX, NY), ((0, 8), (1, 16)), -0.2, 0.2)), 0.6, 1.5),
        "helm": jnp.clip(jnp.exp(math.log(0.02) - 2.30258502 * jax.random.uniform(key_list[2], (NX, NY), jnp.float32) ** levels(key_list[2], (NX, NY), ((0, 8), (1, 16)), -0.2, 0.2)), 0.002, 0.02),
    }


shift = 0.001

def cosine_table(freq, space, length):
    phase = freq * (2 * space + 1) % (4 * length)
    angle = phase.astype(jnp.float32) * (math.pi / (2 * length))
    scale = jnp.where(freq == 0, math.sqrt(1.0 / length), math.sqrt(2.0 / length))
    return (scale * jnp.cos(angle)).astype(jnp.float32)

def eigen(index, length):
    return 2.0 - 2.0 * jnp.cos(index.astype(jnp.float32) * (math.pi / length))

def precondition(resid, metric):
    rows = jnp.arange(NX, dtype=jnp.int32)
    cols = jnp.arange(NY, dtype=jnp.int32)
    table_x = cosine_table(rows[:, None], rows[None, :], NX)
    table_y = cosine_table(cols[:, None], cols[None, :], NY)
    exact = lax.Precision.HIGHEST
    scaled = resid / metric
    first = jnp.einsum('kx,fxy->fky', table_x, scaled, precision=exact)
    second = jnp.einsum('fky,ly->fkl', first, table_y, precision=exact)
    denom = eigen(rows, NX)[:, None] + eigen(cols, NY)[None, :] + shift
    third = second / denom
    fourth = jnp.einsum('fkl,ly->fky', third, table_y, precision=exact)
    fifth = jnp.einsum('kx,fky->fxy', table_x, fourth, precision=exact)
    return fifth / metric

def operate(field, metric, helm):
    weighted = metric * field
    padded = jnp.pad(weighted, ((0, 0), (1, 1), (1, 1)))
    beside = padded[:, 2:, 1:-1] + padded[:, :-2, 1:-1]
    beside = beside + padded[:, 1:-1, 2:] + padded[:, 1:-1, :-2]
    rows = jnp.arange(NX, dtype=jnp.int32)
    cols = jnp.arange(NY, dtype=jnp.int32)
    edge_x = jnp.where(rows == 0, 1.0, 0.0) + jnp.where(rows == NX - 1, 1.0, 0.0)
    edge_y = jnp.where(cols == 0, 1.0, 0.0) + jnp.where(cols == NY - 1, 1.0, 0.0)
    degree = 4.0 - edge_x[:, None] - edge_y[None, :]
    return metric * (degree * weighted - beside) + helm * field

def reference(sources, metric, helm):
    solution = jnp.zeros_like(sources)
    resid = sources
    direct = precondition(resid, metric)
    search = direct
    gamma = lax.optimization_barrier(jnp.sum(resid * direct, axis=(1, 2)))
    for step in range(ITERS):
        image = operate(search, metric, helm)
        alpha = gamma / lax.optimization_barrier(jnp.sum(search * image, axis=(1, 2)))
        solution = solution + alpha[:, None, None] * search
        resid = resid - alpha[:, None, None] * image
        if step + 1 < ITERS:
            direct = precondition(resid, metric)
            fresh = lax.optimization_barrier(jnp.sum(resid * direct, axis=(1, 2)))
            search = direct + (fresh / gamma)[:, None, None] * search
            gamma = fresh
    return (solution, resid)
```

```python
import functools
import math

import jax
import jax.numpy as jnp
import ml_dtypes
import numpy as np
from jax import lax
from jax.experimental import pallas as pl
from jax.experimental.pallas import tpu as pltpu
from jax.sharding import PartitionSpec as P

SHIFT = 0.001
ROWS = 16
LANES = 128
LENGTH = ROWS * LANES


def frequency():
    t = np.arange(16)[:, None]
    k2 = np.arange(64)[None, :]
    first = t + 32 * k2
    second = np.where(t == 0, 16, 32 - t) + 32 * k2
    return np.concatenate([first, second], axis=1)


def tables():
    freq = frequency()
    b = np.arange(LANES)
    phase = (freq[:, None, :] * (2 * b[None, :, None] + 1)) % (4 * LENGTH)
    angle = phase * (math.pi / (2 * LENGTH))
    scale = np.where(freq == 0, math.sqrt(1.0 / LENGTH), math.sqrt(2.0 / LENGTH))[:, None, :]
    even, odd = scale * np.cos(angle), scale * np.sin(angle)
    sign = np.where(np.arange(LANES) < 64, -1.0, 1.0)
    full = np.concatenate([even, odd * sign], axis=1)
    full[0, :LANES, 64:] = 0.0
    full[0, LANES:, :64] = 0.0
    full[0, LANES:, 64:] = even[0, :, 64:]
    beside = np.concatenate([full[:, :LANES], full[:, LANES:]], axis=2)
    full = np.concatenate([np.swapaxes(full, 1, 2), beside], axis=1)
    high = full.astype(ml_dtypes.bfloat16)
    low = (full - high.astype(np.float64)).astype(ml_dtypes.bfloat16)
    lam = 4.0 * np.sin(math.pi * freq / (2 * LENGTH)) ** 2
    return np.stack([high, low], axis=1), lam.astype(np.float32)


def cos16(n):
    return float(math.cos(math.pi * n / 16))


def sin16(n):
    return float(math.sin(math.pi * n / 16))


def combine(terms):
    total = None
    for c, v in terms:
        if abs(c) < 1e-12:
            continue
        if abs(abs(c) - 1.0) < 1e-12:
            if total is None:
                total = v if c > 0 else -v
            else:
                total = total + v if c > 0 else total - v
        else:
            total = c * v if total is None else total + c * v
    return total


def first_stage(x):
    p = {a: x[a] + x[16 - a] for a in range(1, 8)}
    m = {a: x[a] - x[16 - a] for a in range(1, 8)}
    R, S = {}, {}
    for j in range(1, 8):
        c, s = (m, p) if j % 2 else (p, m)
        ev = combine([(1.0, x[0])] + [(cos16(j * a), c[a]) for a in (2, 4, 6)] + [(cos16(8 * j), x[8])])
        od = combine([(cos16(j * a), c[a]) for a in (1, 3, 5, 7)])
        R[j], R[16 - j] = ev + od, ev - od
        ev = combine([(sin16(j * a), s[a]) for a in (2, 4, 6)] + [(sin16(8 * j), x[8])])
        od = combine([(sin16(j * a), s[a]) for a in (1, 3, 5, 7)])
        S[j], S[16 - j] = od + ev, od - ev
    outer, inner = x[0] + x[8], p[2] + p[6]
    R[8] = outer + p[4] - inner
    S[8] = (m[1] + m[5]) - (m[3] + m[7])
    even, odd = outer + p[4] + inner, (p[1] + p[7]) + (p[3] + p[5])
    R[0], R[16] = even + odd, even - odd
    return R, S


def first_stage_transposed(R, S):
    rp = {j: R[j] + R[16 - j] for j in range(1, 8)}
    rm = {j: R[j] - R[16 - j] for j in range(1, 8)}
    sp = {j: S[j] + S[16 - j] for j in range(1, 8)}
    sm = {j: S[j] - S[16 - j] for j in range(1, 8)}
    ends, wide = R[0] + R[16], R[0] - R[16]
    x = {}
    for a in range(1, 8):
        r, s = (rm, sp) if a % 2 else (rp, sm)
        ce = combine([(1.0, wide if a % 2 else ends), (cos16(8 * a), R[8])] + [(cos16(j * a), r[j]) for j in (2, 4, 6)])
        co = combine([(cos16(j * a), r[j]) for j in (1, 3, 5, 7)])
        se = combine([(sin16(8 * a), S[8])] + [(sin16(j * a), s[j]) for j in (2, 4, 6)])
        so = combine([(sin16(j * a), s[j]) for j in (1, 3, 5, 7)])
        x[a], x[16 - a] = (ce + so) + (co + se), (ce + so) - (co + se)
    even = ends + R[8] + rp[2] + rp[4] + rp[6]
    x[0] = even + (rp[1] + rp[7]) + (rp[3] + rp[5])
    x[8] = ends + R[8] - rp[2] + rp[4] - rp[6] + (sm[1] - sm[3]) + (sm[5] - sm[7])
    return x


def split_dot(value, high_table, low_table):
    rows = value.shape[0]
    high = value.astype(jnp.bfloat16)
    low = (value - high.astype(jnp.float32)).astype(jnp.bfloat16)
    both = jnp.dot(jnp.concatenate([high, low], axis=0), high_table, preferred_element_type=jnp.float32)
    third = jnp.dot(high, low_table, preferred_element_type=jnp.float32)
    return both[:rows] + (both[rows:] + third)


def forward_dot(value, table, t):
    halves = [[table[t, n, LANES:, LANES * k : LANES * (k + 1)] for k in range(2)] for n in range(2)]
    return split_dot(value, *[jnp.concatenate(pair, axis=0) for pair in halves])


def backward_dot(value, table, t):
    return split_dot(value, table[t, 0, :LANES, :], table[t, 1, :LANES, :])


def put_first(R, S, rs, chunk):
    rows = pl.ds(8 * chunk, 8)
    for t in range(16):
        rs[t, rows, 0:LANES] = R[t]
        rs[t, rows, LANES : 2 * LANES] = R[16] if t == 0 else S[t]


def get_first(rs, chunk):
    rows = pl.ds(8 * chunk, 8)
    R = {t: rs[t, rows, 0:LANES] for t in range(16)}
    S = {t: rs[t, rows, LANES : 2 * LANES] for t in range(1, 16)}
    R[16] = rs[0, rows, LANES : 2 * LANES]
    return R, S


def leave_block(
    sources, metric, helm, table, lam, columns, here, fields, weights, factors, source_here, metric_here, helm_here, arrived
):
    moves = [(metric, metric_here), (sources.at[0], source_here.at[0]), (sources.at[1], source_here.at[1]), (helm, helm_here)]
    copies = [pltpu.make_async_copy(a, b, arrived.at[n]) for n, (a, b) in enumerate(moves)]
    for copy in copies:
        copy.start()
    lane = lax.broadcasted_iota(jnp.int32, (32, LANES), 1)
    mine = jnp.sum(jnp.where(lane == here[...], columns[...], 0.0), axis=1, keepdims=True)
    for t in range(16):
        factors[t] = 1.0 / (mine + (lam[pl.ds(t, 1), :] + SHIFT))
    copies[0].wait()
    inverse = 1.0 / metric_here[...]
    for f in range(2):
        copies[1 + f].wait()
        field = source_here[f] * inverse
        for h in range(2):
            across = field[LANES * h : LANES * (h + 1), :].T
            for peer in range(8):
                fields[pl.ds(64 * peer + 32 * f + h, 16, stride=2), :] = across[16 * peer : 16 * (peer + 1)]
    copies[3].wait()
    weight = helm_here[...] * (inverse * inverse) - SHIFT
    for h in range(2):
        across = weight[LANES * h : LANES * (h + 1), :].T
        for g in range(2):
            weights[pl.ds(2 * g + h, 64, stride=4), :] = across[64 * g : 64 * (g + 1)]


def pencil_x_first(fields, own, table, sent, rs, flat):
    for chunk in range(4):
        x = [fields[pl.ds(64 * (a // 2) + 16 * chunk + a % 2, 8, stride=2), :] for a in range(16)]
        put_first(*first_stage(x), rs, chunk)
    for n in range(4):
        weight = own[pl.ds(n, 64, stride=4), :]
        for f in range(2):
            sent[pl.ds(512 * f + 2 * n + 1, 64, stride=8), :] = weight
    forward_along_x(table, rs, flat)
    for f in range(2):
        for u in range(2):
            across = flat[pl.ds(256 * f + LANES * u, LANES), :].T
            for s in range(2):
                sent[pl.ds(512 * f + 2 * (2 * s + u), 64, stride=8), :] = across[64 * s : 64 * (s + 1)]


def forward_along_x(table, rs, flat):
    for t in range(16):
        lines = forward_dot(rs[t], table, t)
        for g in range(2):
            flat[pl.ds(256 * g + 16 * t, 16), :] = lines[16 * g : 16 * (g + 1)]


def along_y(table, factors, sent, rs, flat):
    for chunk in range(4):
        x = [flat[pl.ds(LANES * chunk + a, 8, stride=16), :] for a in range(16)]
        put_first(*first_stage(x), rs, chunk)
    total = jnp.zeros((32, LANES), jnp.float32)
    for t in range(16):
        spectrum = forward_dot(rs[t], table, t)
        scaled = spectrum * factors[t]
        total += spectrum * scaled
        rs[t] = backward_dot(scaled, table, t)
    for chunk in range(4):
        x = first_stage_transposed(*get_first(rs, chunk))
        for a in range(16):
            flat[pl.ds(LANES * chunk + a, 8, stride=16), :] = x[a]
    for r in range(4):
        across = flat[pl.ds(LANES * r, LANES), :].T
        for g in range(2):
            sent[pl.ds(4 * g + r, 64, stride=8), :] = across[64 * g : 64 * (g + 1)]
    return (total[0:8] + total[8:16]) + (total[16:24] + total[24:32])


def pencil_y_first(received, table, factors, sent, total, rs, flat):
    lane = lax.broadcasted_iota(jnp.int32, (8, LANES), 1)
    for pair in range(8):
        v = [received[pl.ds((16 * i + 2 * pair) * 8, 8, stride=2), :] for i in range(8)]
        for step in (4, 2, 1):
            upper = (lane // (16 * step)) % 2 == 1
            w = list(v)
            for i in range(8):
                if not i & step:
                    w[i] = jnp.where(upper, pltpu.roll(v[i + step], 16 * step, 1), v[i])
                    w[i + step] = jnp.where(upper, v[i + step], pltpu.roll(v[i], LANES - 16 * step, 1))
            v = w
        for n in range(8):
            for m in range(2):
                flat[pl.ds(16 * n + 2 * pair + m, 4, stride=LANES), :] = v[n][4 * m : 4 * (m + 1)]
    total[...] = along_y(table, factors, sent, rs, flat)


def pencil_y_second(received, table, factors, sent, rs, flat):
    for r in range(4):
        lines = [received[pl.ds(4 * g + r, 64, stride=8), :] for g in range(2)]
        flat[pl.ds(LANES * r, LANES), :] = jnp.concatenate(lines, axis=0).T
    along_y(table, factors, sent, rs, flat)


def weight_at(weights, a, chunk):
    g, half = chunk // 2, chunk % 2
    start = (16 * (a // 2) + 8 * half) * 8 + 2 * (2 * g + a % 2) + 1
    return weights[pl.ds(start, 8, stride=8), :]


def back_along_x(received, table, rs, flat):
    for g in range(2):
        for u in range(2):
            lines = [received[pl.ds(4 * g + 2 * s + u, 64, stride=8), :] for s in range(2)]
            flat[pl.ds(256 * g + LANES * u, LANES), :] = jnp.concatenate(lines, axis=0).T
    for t in range(16):
        both = [flat[pl.ds(256 * g + 16 * t, 16), :] for g in range(2)]
        rs[t] = backward_dot(jnp.concatenate(both, axis=0), table, t)


def pencil_x_middle(received, weights, table, sent, kept, rs, flat):
    back_along_x(received, table, rs, flat)
    for chunk in range(4):
        x = first_stage_transposed(*get_first(rs, chunk))
        for a in range(16):
            kept[a, pl.ds(8 * chunk, 8), :] = x[a]
        x = [x[a] * weight_at(weights, a, chunk) for a in range(16)]
        put_first(*first_stage(x), rs, chunk)
    forward_along_x(table, rs, flat)
    for g in range(2):
        for u in range(2):
            across = flat[pl.ds(256 * g + LANES * u, LANES), :].T
            for s in range(2):
                sent[pl.ds(4 * g + 2 * s + u, 64, stride=8), :] = across[64 * s : 64 * (s + 1)]


def pencil_x_last(received, weights, kept, total, table, sent, rs, flat):
    back_along_x(received, table, rs, flat)
    sums = [total[...]] + [jnp.zeros((8, LANES), jnp.float32) for _ in range(3)]
    for chunk in range(4):
        x = first_stage_transposed(*get_first(rs, chunk))
        for a in range(16):
            old, new = kept[a, pl.ds(8 * chunk, 8), :], x[a]
            weight = weight_at(weights, a, chunk)
            scaled = weight * old
            sums[1] += scaled * old
            sums[2] += scaled * new
            sums[3] += weight * new * new
            place = ((a // 2) * 16 + 8 * (chunk % 2)) * 9 + 2 * (chunk // 2) + a % 2
            sent[pl.ds(place, 8, stride=9), :] = old
            sent[pl.ds(place + 4, 8, stride=9), :] = new
    lane = lax.broadcasted_iota(jnp.int32, (1, LANES), 1)
    line = jnp.zeros((1, LANES), jnp.float32)
    for q in range(4):
        line = jnp.where(lane == q, jnp.sum(sums[q]), line)
    sent[pl.ds(8, LANES, stride=9), :] = jnp.broadcast_to(line, (LANES, LANES))


def enter_block(received, sources, metric, helm, solution, resid):
    lane = lax.broadcasted_iota(jnp.int32, (1, LANES), 1)
    m = metric[...]
    inverse = 1.0 / m
    weight = helm[...] * inverse - SHIFT * m
    for f in range(2):
        totals = jnp.sum(received[pl.ds(64 * 9 * f + 8, 64, stride=9), :], axis=0, keepdims=True)
        n0, n1, n2, n3 = [
            jnp.sum(jnp.where(lane == q, totals, 0.0), axis=1, keepdims=True) for q in range(4)
        ]
        delta = n0 + n1
        alpha = n0 / delta
        rest = n1 / delta
        gamma = n0 * rest * rest - 2.0 * alpha * rest * n1 + alpha * alpha * n2
        beta = gamma / n0
        p, q = rest + beta, -alpha
        second = gamma / (p * p * delta + 2.0 * p * q * (n1 + n2) + q * q * (n2 + n3))
        c0, c1 = alpha + second * p, second * q
        for h in range(2):
            pair = []
            for field in range(2):
                lines = [
                    received[pl.ds(64 * 9 * f + 4 * field + 2 * g + h, 64, stride=9), :] for g in range(2)
                ]
                pair.append(jnp.concatenate(lines, axis=0).T)
            old, new = pair
            rows = slice(LANES * h, LANES * (h + 1))
            solution[f, rows, :] = (c0 * old + c1 * new) * inverse[rows]
            resid[f, rows, :] = (1.0 - c0) * sources[f, rows, :] - ((c0 + c1) * old + c1 * new) * weight[rows]


RS = pltpu.VMEM((16, 32, 2 * LANES), jnp.float32)
FLAT = pltpu.VMEM((512, LANES), jnp.float32)


def call(kernel, outs, scratch=(RS, FLAT), **more):
    return pl.pallas_call(
        kernel,
        out_shape=[jax.ShapeDtypeStruct(s, jnp.float32) if isinstance(s, tuple) else s for s in outs],
        scratch_shapes=scratch,
        compiler_params=pltpu.CompilerParams(vmem_limit_bytes=32 * 1024 * 1024),
        **more,
    )


def far(*arrays):
    return [pltpu.with_memory_space_constraint(a, pltpu.HBM) for a in arrays]


def exchange(flat, axes, *shape):
    moved = lax.all_to_all(flat.reshape(*shape, LANES), axes, 0, 0, tiled=True)
    return moved.reshape(flat.shape)


def per_device(sources, metric, helm):
    pair, eigen = tables()
    group = ("quarter", "gy")
    here = lax.axis_index("quarter") * lax.axis_size("gy") + lax.axis_index("gy")
    columns = np.zeros((32, LANES), np.float32)
    columns[:, :64] = eigen.reshape(16, 2, 64).transpose(1, 0, 2).reshape(32, 64)

    block = pltpu.VMEM(metric.shape, metric.dtype)
    hbm, vmem = pl.BlockSpec(memory_space=pl.ANY), pl.BlockSpec(memory_space=pltpu.VMEM)
    table = jnp.asarray(pair)
    fields, own, factors = call(
        leave_block,
        [(512, LANES), (256, LANES), (16, 32, LANES)],
        [pltpu.VMEM(sources.shape, sources.dtype), block, block, pltpu.SemaphoreType.DMA((4,))],
        in_specs=[hbm] * 4 + [vmem] * 3,
    )(
        *far(sources, metric, helm, table),
        jnp.asarray(eigen),
        jnp.asarray(columns),
        jnp.full((1, LANES), here, jnp.int32),
    )
    fields = exchange(fields, ("half", "quarter"), 8, 64)
    (sent,) = call(pencil_x_first, [(1024, LANES)])(fields, own, table)
    weights = exchange(sent, ("half", "quarter", "gy"), LANES, 8)
    sent, total = call(pencil_y_first, [(512, LANES), (8, LANES)])(weights, table, factors)
    received = exchange(sent, group, 64, 8)
    sent, kept = call(pencil_x_middle, [(512, LANES), (16, 32, LANES)])(received, weights, table)
    received = exchange(sent, group, 64, 8)
    (sent,) = call(pencil_y_second, [(512, LANES)])(received, table, factors)
    received = exchange(sent, group, 64, 8)
    (sent,) = call(pencil_x_last, [(9 * LANES, LANES)])(received, weights, kept, total, table)
    received = exchange(sent, ("half", "quarter", "gy"), LANES, 9, 1)
    return tuple(call(enter_block, [sources.shape] * 2, ())(received, sources, metric, helm))


def solution(mesh):
    devices = mesh.devices.reshape(2, 4, 16)
    finer = jax.sharding.Mesh(devices, ("half", "quarter", "gy"))
    line = ("half", "quarter")
    in_specs = (P(None, line, "gy"), P(line, "gy"), P(line, "gy"))
    out_specs = (P(None, line, "gy"), P(None, line, "gy"))
    return jax.shard_map(
        per_device, mesh=finer, in_specs=in_specs, out_specs=out_specs, check_vma=False
    )
```

```python
import functools
import math

import jax
import jax.numpy as jnp
import ml_dtypes
import numpy as np
from jax import lax
from jax.experimental import pallas as pl
from jax.experimental.pallas import tpu as pltpu
from jax.sharding import PartitionSpec as P

SHIFT = 0.001
ROWS = 16
BLOCK = 32
BLOCKS = 64
LANES = 128
LENGTH = ROWS * LANES


def frequency():
    t = np.arange(16)[:, None]
    k2 = np.arange(64)[None, :]
    first = t + 32 * k2
    second = np.where(t == 0, 16, 32 - t) + 32 * k2
    return np.concatenate([first, second], axis=1)


def tables():
    freq = frequency()
    b = np.arange(LANES)
    phase = (freq[:, None, :] * (2 * b[None, :, None] + 1)) % (4 * LENGTH)
    angle = phase * (math.pi / (2 * LENGTH))
    scale = np.where(freq == 0, math.sqrt(1.0 / LENGTH), math.sqrt(2.0 / LENGTH))[:, None, :]
    even, odd = scale * np.cos(angle), scale * np.sin(angle)
    sign = np.where(np.arange(LANES) < 64, -1.0, 1.0)
    full = np.concatenate([even, odd * sign], axis=1)
    full[0, :LANES, 64:] = 0.0
    full[0, LANES:, :64] = 0.0
    full[0, LANES:, 64:] = even[0, :, 64:]
    high = full.astype(ml_dtypes.bfloat16)
    low = (full - high.astype(np.float64)).astype(ml_dtypes.bfloat16)
    forward = np.concatenate([high, low], axis=2)
    sigma = 4.0 * np.sin(math.pi * freq / (2 * LENGTH)) ** 2 + SHIFT
    mu = 2.0 * np.arcsinh(np.sqrt(sigma) / 2.0)
    waves = [np.exp(-mu), BLOCK * mu, 0.5 / np.sinh(mu), 1.0 / (1.0 - np.exp(-2.0 * BLOCK * BLOCKS * mu))]
    return np.stack([forward, np.swapaxes(forward, 1, 2)], axis=1), np.stack(waves).astype(np.float32)


def cos16(n):
    return float(math.cos(math.pi * n / 16))


def sin16(n):
    return float(math.sin(math.pi * n / 16))


def combine(terms):
    total = None
    for c, v in terms:
        if abs(c) < 1e-12:
            continue
        if abs(abs(c) - 1.0) < 1e-12:
            if total is None:
                total = v if c > 0 else -v
            else:
                total = total + v if c > 0 else total - v
        else:
            total = c * v if total is None else total + c * v
    return total


def first_stage(x):
    p = {a: x[a] + x[16 - a] for a in range(1, 8)}
    m = {a: x[a] - x[16 - a] for a in range(1, 8)}
    R, S = {}, {}
    for j in range(1, 8):
        c, s = (m, p) if j % 2 else (p, m)
        ev = combine([(1.0, x[0])] + [(cos16(j * a), c[a]) for a in (2, 4, 6)] + [(cos16(8 * j), x[8])])
        od = combine([(cos16(j * a), c[a]) for a in (1, 3, 5, 7)])
        R[j], R[16 - j] = ev + od, ev - od
        ev = combine([(sin16(j * a), s[a]) for a in (2, 4, 6)] + [(sin16(8 * j), x[8])])
        od = combine([(sin16(j * a), s[a]) for a in (1, 3, 5, 7)])
        S[j], S[16 - j] = od + ev, od - ev
    outer, inner = x[0] + x[8], p[2] + p[6]
    R[8] = outer + p[4] - inner
    S[8] = (m[1] + m[5]) - (m[3] + m[7])
    even, odd = outer + p[4] + inner, (p[1] + p[7]) + (p[3] + p[5])
    R[0], R[16] = even + odd, even - odd
    return R, S


def first_stage_transposed(R, S):
    rp = {j: R[j] + R[16 - j] for j in range(1, 8)}
    rm = {j: R[j] - R[16 - j] for j in range(1, 8)}
    sp = {j: S[j] + S[16 - j] for j in range(1, 8)}
    sm = {j: S[j] - S[16 - j] for j in range(1, 8)}
    ends, wide = R[0] + R[16], R[0] - R[16]
    x = {}
    for a in range(1, 8):
        r, s = (rm, sp) if a % 2 else (rp, sm)
        ce = combine([(1.0, wide if a % 2 else ends), (cos16(8 * a), R[8])] + [(cos16(j * a), r[j]) for j in (2, 4, 6)])
        co = combine([(cos16(j * a), r[j]) for j in (1, 3, 5, 7)])
        se = combine([(sin16(8 * a), S[8])] + [(sin16(j * a), s[j]) for j in (2, 4, 6)])
        so = combine([(sin16(j * a), s[j]) for j in (1, 3, 5, 7)])
        x[a], x[16 - a] = (ce + so) + (co + se), (ce + so) - (co + se)
    even = ends + R[8] + rp[2] + rp[4] + rp[6]
    x[0] = even + (rp[1] + rp[7]) + (rp[3] + rp[5])
    x[8] = ends + R[8] - rp[2] + rp[4] - rp[6] + (sm[1] - sm[3]) + (sm[5] - sm[7])
    return x


def split(value):
    high = value.astype(jnp.bfloat16)
    return high, (value - high.astype(jnp.float32)).astype(jnp.bfloat16)


def forward_dot(value, table, t):
    high, low = split(value)
    both = jnp.dot(jnp.concatenate([high, low], axis=0), table[t, 0, :, :LANES], preferred_element_type=jnp.float32)
    third = jnp.dot(high, table[t, 0, :, LANES:], preferred_element_type=jnp.float32)
    return both[:32] + (both[32:] + third)


def backward_dot(value, table, t):
    high, low = split(value)
    both = jnp.dot(jnp.concatenate([high, low], axis=0), table[t, 1, :LANES, :], preferred_element_type=jnp.float32)
    third = jnp.dot(high, table[t, 1, LANES:, :], preferred_element_type=jnp.float32)
    return both[:32] + (both[32:] + third)


def put_first(R, S, rs, chunk):
    rows = pl.ds(8 * chunk, 8)
    for t in range(16):
        rs[t, rows, 0:LANES] = R[t]
        rs[t, rows, LANES : 2 * LANES] = R[16] if t == 0 else S[t]


def get_first(rs, chunk):
    rows = pl.ds(8 * chunk, 8)
    R = {t: rs[t, rows, 0:LANES] for t in range(16)}
    S = {t: rs[t, rows, LANES : 2 * LANES] for t in range(1, 16)}
    R[16] = rs[0, rows, LANES : 2 * LANES]
    return R, S


def leave_block(sources, metric, helm, table, waves, here, sent, source_here, metric_here, helm_here, arrived):
    moves = [(metric, metric_here)]
    moves += [(sources.at[f], source_here.at[f]) for f in range(2)] + [(helm, helm_here)]
    copies = [pltpu.make_async_copy(a, b, arrived.at[n]) for n, (a, b) in enumerate(moves)]
    for copy in copies:
        copy.start()
    copies[0].wait()
    inverse = 1.0 / metric_here[...]
    for f in range(2):
        copies[1 + f].wait()
        field = source_here[f] * inverse
        for h in range(2):
            across = field[LANES * h : LANES * (h + 1), :].T
            for quarter in range(4):
                rows = pl.ds(LANES * (4 * f + quarter) + h, BLOCK, stride=2)
                sent[rows, :] = across[BLOCK * quarter : BLOCK * (quarter + 1)]
    copies[3].wait()
    weight = helm_here[...] * (inverse * inverse) - SHIFT
    for h in range(2):
        across = weight[LANES * h : LANES * (h + 1), :].T
        for quarter in range(4):
            for f in range(2):
                rows = pl.ds(LANES * (4 * f + quarter) + 64 + h, BLOCK, stride=2)
                sent[rows, :] = across[BLOCK * quarter : BLOCK * (quarter + 1)]


def from_block(blocks, a, chunk, field):
    return blocks[pl.ds(LANES * (a // 2) + 64 * field + 16 * chunk + a % 2, 8, stride=2), :]


def lines(spectrum, y):
    return spectrum[pl.ds(16 * y, 16), :]


def forward_x(table, rs, spectrum):
    for t in range(16):
        spectrum[pl.ds(t, BLOCK, stride=16), :] = forward_dot(rs[t], table, t)


def backward_x(spectrum, table, rs):
    for t in range(16):
        rs[t] = backward_dot(spectrum[pl.ds(t, BLOCK, stride=16), :], table, t)


def leave_lines(spectrum, waves, here, ends, sent):
    rho, decay = waves[0], waves[1]
    p = lines(spectrum, 0)
    q = lines(spectrum, BLOCK - 1)
    for y in range(1, BLOCK):
        p = rho * p + lines(spectrum, y)
        q = rho * q + lines(spectrum, BLOCK - 1 - y)
    ends[0], ends[1] = p, q
    b = here[...]
    above = p + jnp.exp(-decay * (2.0 * b + 1.0)) * q
    below = q + jnp.exp(-decay * (2.0 * (BLOCKS - 1.0 - b) + 1.0)) * p
    for n in range(BLOCKS):
        sent[pl.ds(16 * n, 16), :] = jnp.where(b < n, above, below)


def solve_lines(received, spectrum, waves, here, ends, solved):
    rho, decay, scale, rounds = waves[0], waves[1], waves[2], waves[3]
    whole = jnp.exp(-decay)
    b = here[...]
    low = jnp.zeros((16, LANES), jnp.float32)
    high = jnp.zeros((16, LANES), jnp.float32)
    for n in range(BLOCKS):
        low = jnp.where(b > n, received[pl.ds(16 * n, 16), :] + whole * low, low)
        m = BLOCKS - 1 - n
        high = jnp.where(b < m, received[pl.ds(16 * m, 16), :] + whole * high, high)
    p, q = ends[0], ends[1]
    left = jnp.exp(-decay * (2.0 * b))
    right = jnp.exp(-decay * (2.0 * (BLOCKS - 1.0 - b)))
    up = (low + left * (q + whole * (high + right * p))) * rounds
    down = high + right * (p + whole * up)
    for y in range(BLOCK):
        up = rho * up + lines(spectrum, y)
        solved[pl.ds(16 * y, 16), :] = up
    for y in range(BLOCK - 1, -1, -1):
        down = rho * down
        solved[pl.ds(16 * y, 16), :] = scale * (lines(solved, y) + down)
        down = down + lines(spectrum, y)


def pencil_first(blocks, table, waves, here, sent, spectrum, ends, rs):
    for chunk in range(4):
        x = [from_block(blocks, a, chunk, 0) for a in range(16)]
        put_first(*first_stage(x), rs, chunk)
    forward_x(table, rs, spectrum)
    leave_lines(spectrum, waves, here, ends, sent)


def pencil_middle(received, blocks, old, old_ends, table, waves, here, sent, spectrum, ends, kept, rs, solved):
    solve_lines(received, old, waves, here, old_ends, solved)
    backward_x(solved, table, rs)
    for chunk in range(4):
        x = first_stage_transposed(*get_first(rs, chunk))
        for a in range(16):
            kept[a, pl.ds(8 * chunk, 8), :] = x[a]
        x = [x[a] * from_block(blocks, a, chunk, 1) for a in range(16)]
        put_first(*first_stage(x), rs, chunk)
    forward_x(table, rs, spectrum)
    leave_lines(spectrum, waves, here, ends, sent)


def pencil_last(received, blocks, old, old_ends, kept, table, waves, here, sent, rs, solved):
    solve_lines(received, old, waves, here, old_ends, solved)
    backward_x(solved, table, rs)
    sums = [jnp.zeros((8, LANES), jnp.float32) for _ in range(4)]
    for chunk in range(4):
        x = first_stage_transposed(*get_first(rs, chunk))
        for a in range(16):
            before, new = kept[a, pl.ds(8 * chunk, 8), :], x[a]
            weight = from_block(blocks, a, chunk, 1)
            scaled = weight * before
            sums[0] += from_block(blocks, a, chunk, 0) * before
            sums[1] += scaled * before
            sums[2] += scaled * new
            sums[3] += weight * new * new
            place = 136 * (a // 2) + 16 * chunk + a % 2
            sent[pl.ds(place, 8, stride=2), :] = before
            sent[pl.ds(place + 64, 8, stride=2), :] = new
    lane = lax.broadcasted_iota(jnp.int32, (8, LANES), 1)
    line = jnp.zeros((8, LANES), jnp.float32)
    for q in range(4):
        line = jnp.where(lane == q, jnp.sum(sums[q]), line)
    for i in range(8):
        sent[pl.ds(136 * i + 128, 8), :] = line


def gather_sums(received, sent):
    for f in range(2):
        total = received[pl.ds(136 * 4 * f + 128, 1), :]
        for quarter in range(1, 4):
            total += received[pl.ds(136 * (4 * f + quarter) + 128, 1), :]
        sent[pl.ds(f, 16, stride=2), :] = jnp.broadcast_to(total, (16, LANES))


def enter_block(received, parts, sources, metric, helm, solution, resid, near, done):
    copies = []
    lane = lax.broadcasted_iota(jnp.int32, (1, LANES), 1)
    m = metric[...]
    inverse = 1.0 / m
    weight = helm[...] * inverse - SHIFT * m
    for f in range(2):
        totals = jnp.sum(parts[pl.ds(f, 16, stride=2), :], axis=0, keepdims=True)
        n0, n1, n2, n3 = [
            jnp.sum(jnp.where(lane == q, totals, 0.0), axis=1, keepdims=True) for q in range(4)
        ]
        delta = n0 + n1
        alpha = n0 / delta
        rest = n1 / delta
        gamma = n0 * rest * rest - 2.0 * alpha * rest * n1 + alpha * alpha * n2
        beta = gamma / n0
        p, q = rest + beta, -alpha
        second = gamma / (p * p * delta + 2.0 * p * q * (n1 + n2) + q * q * (n2 + n3))
        c0, c1 = alpha + second * p, second * q
        for h in range(2):
            pair = []
            for field in range(2):
                places = [136 * (4 * f + quarter) + 64 * field + h for quarter in range(4)]
                columns = [received[pl.ds(place, BLOCK, stride=2), :] for place in places]
                pair.append(jnp.concatenate(columns, axis=0).T)
            old, new = pair
            rows = slice(LANES * h, LANES * (h + 1))
            near[0, f, rows, :] = (c0 * old + c1 * new) * inverse[rows]
            near[1, f, rows, :] = (1.0 - c0) * sources[f, rows, :] - ((c0 + c1) * old + c1 * new) * weight[rows]
            for n, out in enumerate((solution, resid)):
                place = (f, pl.ds(LANES * h, LANES))
                copies.append(pltpu.make_async_copy(near.at[n, *place], out.at[*place], done.at[4 * n + 2 * f + h]))
                copies[-1].start()
    for copy in copies:
        copy.wait()


RS = pltpu.VMEM((16, 32, 2 * LANES), jnp.float32)
LINES = pltpu.VMEM((512, LANES), jnp.float32)
SENT, SPECTRUM, ENDS, KEPT = (1024, LANES), (512, LANES), (2, 16, LANES), (16, 32, LANES)


def call(kernel, outs, scratch, **more):
    return pl.pallas_call(
        kernel,
        out_shape=[jax.ShapeDtypeStruct(s, jnp.float32) for s in outs],
        scratch_shapes=scratch,
        compiler_params=pltpu.CompilerParams(vmem_limit_bytes=32 * 1024 * 1024),
        **more,
    )


def far(*arrays):
    return [pltpu.with_memory_space_constraint(a, pltpu.HBM) for a in arrays]


def exchange(flat, axes, *shape):
    moved = lax.all_to_all(flat.reshape(*shape, LANES), axes, 0, 0, tiled=True)
    return moved.reshape(flat.shape)


def per_device(sources, metric, helm):
    table, waves = (jnp.asarray(a) for a in tables())
    line, column = ("half", "quarter"), ("gy", "quarter")
    here = lax.axis_index("gy") * lax.axis_size("quarter") + lax.axis_index("quarter")
    here = jnp.full((1, LANES), here, jnp.float32)
    block = pltpu.VMEM(metric.shape, metric.dtype)
    hbm, vmem = pl.BlockSpec(memory_space=pl.ANY), pl.BlockSpec(memory_space=pltpu.VMEM)

    (sent,) = call(
        leave_block,
        [SENT],
        [pltpu.VMEM(sources.shape, sources.dtype), block, block, pltpu.SemaphoreType.DMA((4,))],
        in_specs=[hbm] * 5 + [vmem],
    )(*far(sources, metric, helm, table, waves), here)
    blocks = exchange(sent, line, 8, 128)
    sent, first, ends = call(pencil_first, [SENT, SPECTRUM, ENDS], [RS])(blocks, table, waves, here)
    received = exchange(sent, column, BLOCKS, 16)
    sent, second, more, kept = call(pencil_middle, [SENT, SPECTRUM, ENDS, KEPT], [RS, LINES])(
        received, blocks, first, ends, table, waves, here
    )
    received = exchange(sent, column, BLOCKS, 16)
    (sent,) = call(pencil_last, [(8 * 136, LANES)], [RS, LINES])(
        received, blocks, second, more, kept, table, waves, here
    )
    received = exchange(sent, line, 8, 136)
    (parts,) = call(gather_sums, [(32, LANES)], [])(received)
    parts = exchange(parts, "gy", 16, 2)
    outs = call(
        enter_block,
        [sources.shape] * 2,
        [pltpu.VMEM((2, *sources.shape), jnp.float32), pltpu.SemaphoreType.DMA((8,))],
        in_specs=[vmem] * 5,
        out_specs=[hbm] * 2,
    )(received, parts, sources, metric, helm)
    return tuple(outs)


def solution(mesh):
    devices = mesh.devices.reshape(2, 4, 16)
    finer = jax.sharding.Mesh(devices, ("half", "quarter", "gy"))
    line = ("half", "quarter")
    in_specs = (P(None, line, "gy"), P(line, "gy"), P(line, "gy"))
    out_specs = (P(None, line, "gy"), P(None, line, "gy"))
    return jax.shard_map(
        per_device, mesh=finer, in_specs=in_specs, out_specs=out_specs, check_vma=False
    )
```

```python
import functools
import math

import jax
import jax.numpy as jnp
import ml_dtypes
import numpy as np
from jax import lax
from jax.experimental import pallas as pl
from jax.experimental.pallas import tpu as pltpu
from jax.sharding import PartitionSpec as P

SHIFT = 0.001
ROWS = 16
BLOCK = 32
BLOCKS = 32
LANES = 128
LENGTH = ROWS * LANES


def frequency():
    t = np.arange(16)[:, None]
    k2 = np.arange(64)[None, :]
    first = t + 32 * k2
    second = np.where(t == 0, 16, 32 - t) + 32 * k2
    return np.concatenate([first, second], axis=1)


def tables():
    freq = frequency()
    b = np.arange(LANES)
    phase = (freq[:, None, :] * (2 * b[None, :, None] + 1)) % (4 * LENGTH)
    angle = phase * (math.pi / (2 * LENGTH))
    scale = np.where(freq == 0, math.sqrt(1.0 / LENGTH), math.sqrt(2.0 / LENGTH))[:, None, :]
    even, odd = scale * np.cos(angle), scale * np.sin(angle)
    sign = np.where(np.arange(LANES) < 64, -1.0, 1.0)
    full = np.concatenate([even, odd * sign], axis=1)
    full[0, :LANES, 64:] = 0.0
    full[0, LANES:, :64] = 0.0
    full[0, LANES:, 64:] = even[0, :, 64:]
    high = full.astype(ml_dtypes.bfloat16)
    low = (full - high.astype(np.float64)).astype(ml_dtypes.bfloat16)
    forward = np.concatenate([high, low], axis=2)
    sigma = 4.0 * np.sin(math.pi * freq / (2 * LENGTH)) ** 2 + SHIFT
    mu = 2.0 * np.arcsinh(np.sqrt(sigma) / 2.0)
    waves = [np.exp(-mu), BLOCK * mu, 0.5 / np.sinh(mu), 1.0 / (1.0 - np.exp(-4.0 * BLOCK * BLOCKS * mu))]
    return np.stack([forward, np.swapaxes(forward, 1, 2)], axis=1), np.stack(waves).astype(np.float32)


def cos16(n):
    return float(math.cos(math.pi * n / 16))


def sin16(n):
    return float(math.sin(math.pi * n / 16))


def combine(terms):
    total = None
    for c, v in terms:
        if abs(c) < 1e-12:
            continue
        if abs(abs(c) - 1.0) < 1e-12:
            if total is None:
                total = v if c > 0 else -v
            else:
                total = total + v if c > 0 else total - v
        else:
            total = c * v if total is None else total + c * v
    return total


def first_stage(x):
    p = {a: x[a] + x[16 - a] for a in range(1, 8)}
    m = {a: x[a] - x[16 - a] for a in range(1, 8)}
    R, S = {}, {}
    for j in range(1, 8):
        c, s = (m, p) if j % 2 else (p, m)
        ev = combine([(1.0, x[0])] + [(cos16(j * a), c[a]) for a in (2, 4, 6)] + [(cos16(8 * j), x[8])])
        od = combine([(cos16(j * a), c[a]) for a in (1, 3, 5, 7)])
        R[j], R[16 - j] = ev + od, ev - od
        ev = combine([(sin16(j * a), s[a]) for a in (2, 4, 6)] + [(sin16(8 * j), x[8])])
        od = combine([(sin16(j * a), s[a]) for a in (1, 3, 5, 7)])
        S[j], S[16 - j] = od + ev, od - ev
    outer, inner = x[0] + x[8], p[2] + p[6]
    R[8] = outer + p[4] - inner
    S[8] = (m[1] + m[5]) - (m[3] + m[7])
    even, odd = outer + p[4] + inner, (p[1] + p[7]) + (p[3] + p[5])
    R[0], R[16] = even + odd, even - odd
    return R, S


def first_stage_transposed(R, S):
    rp = {j: R[j] + R[16 - j] for j in range(1, 8)}
    rm = {j: R[j] - R[16 - j] for j in range(1, 8)}
    sp = {j: S[j] + S[16 - j] for j in range(1, 8)}
    sm = {j: S[j] - S[16 - j] for j in range(1, 8)}
    ends, wide = R[0] + R[16], R[0] - R[16]
    x = {}
    for a in range(1, 8):
        r, s = (rm, sp) if a % 2 else (rp, sm)
        ce = combine([(1.0, wide if a % 2 else ends), (cos16(8 * a), R[8])] + [(cos16(j * a), r[j]) for j in (2, 4, 6)])
        co = combine([(cos16(j * a), r[j]) for j in (1, 3, 5, 7)])
        se = combine([(sin16(8 * a), S[8])] + [(sin16(j * a), s[j]) for j in (2, 4, 6)])
        so = combine([(sin16(j * a), s[j]) for j in (1, 3, 5, 7)])
        x[a], x[16 - a] = (ce + so) + (co + se), (ce + so) - (co + se)
    even = ends + R[8] + rp[2] + rp[4] + rp[6]
    x[0] = even + (rp[1] + rp[7]) + (rp[3] + rp[5])
    x[8] = ends + R[8] - rp[2] + rp[4] - rp[6] + (sm[1] - sm[3]) + (sm[5] - sm[7])
    return x


def split(value):
    high = value.astype(jnp.bfloat16)
    return high, (value - high.astype(jnp.float32)).astype(jnp.bfloat16)


def forward_dot(value, table, t):
    high, low = split(value)
    both = jnp.dot(jnp.concatenate([high, low], axis=0), table[t, 0, :, :LANES], preferred_element_type=jnp.float32)
    third = jnp.dot(high, table[t, 0, :, LANES:], preferred_element_type=jnp.float32)
    return both[:32] + (both[32:] + third)


def backward_dot(value, table, t):
    high, low = split(value)
    both = jnp.dot(jnp.concatenate([high, low], axis=0), table[t, 1, :LANES, :], preferred_element_type=jnp.float32)
    third = jnp.dot(high, table[t, 1, LANES:, :], preferred_element_type=jnp.float32)
    return both[:32] + (both[32:] + third)


def put_first(R, S, rs, chunk):
    rows = pl.ds(8 * chunk, 8)
    for t in range(16):
        rs[t, rows, 0:LANES] = R[t]
        rs[t, rows, LANES : 2 * LANES] = R[16] if t == 0 else S[t]


def get_first(rs, chunk):
    rows = pl.ds(8 * chunk, 8)
    R = {t: rs[t, rows, 0:LANES] for t in range(16)}
    S = {t: rs[t, rows, LANES : 2 * LANES] for t in range(1, 16)}
    R[16] = rs[0, rows, LANES : 2 * LANES]
    return R, S


def leave_block(sources, metric, helm, table, waves, here, core, sent, source_here, metric_here, helm_here, arrived):
    moves = [(metric, metric_here)]
    moves += [(sources.at[f], source_here.at[f]) for f in range(2)] + [(helm, helm_here)]
    copies = [pltpu.make_async_copy(a, b, arrived.at[n]) for n, (a, b) in enumerate(moves)]
    for copy in copies:
        copy.start()
    copies[0].wait()
    inverse = 1.0 / metric_here[...]
    for f in range(2):
        copies[1 + f].wait()
        field = source_here[f] * inverse
        for h in range(2):
            across = field[LANES * h : LANES * (h + 1), :].T
            for quarter in range(4):
                rows = pl.ds(LANES * (4 * f + quarter) + h, BLOCK, stride=2)
                sent[rows, :] = across[BLOCK * quarter : BLOCK * (quarter + 1)]
    copies[3].wait()
    weight = helm_here[...] * (inverse * inverse) - SHIFT
    for h in range(2):
        across = weight[LANES * h : LANES * (h + 1), :].T
        for quarter in range(4):
            for f in range(2):
                rows = pl.ds(LANES * (4 * f + quarter) + 64 + h, BLOCK, stride=2)
                sent[rows, :] = across[BLOCK * quarter : BLOCK * (quarter + 1)]


def from_block(blocks, a, chunk, field):
    return blocks[pl.ds(LANES * (a // 2) + 64 * field + 16 * chunk + a % 2, 8, stride=2), :]


def lines(spectrum, y):
    return spectrum[pl.ds(16 * y, 16), :]


def forward_x(table, rs, spectrum):
    for t in range(16):
        spectrum[pl.ds(t, BLOCK, stride=16), :] = forward_dot(rs[t], table, t)


def backward_x(spectrum, table, rs):
    for t in range(16):
        rs[t] = backward_dot(spectrum[pl.ds(t, BLOCK, stride=16), :], table, t)


def local_sums(spectrum, waves, ends):
    rho = waves[0]
    p = lines(spectrum, 0)
    q = lines(spectrum, BLOCK - 1)
    for y in range(1, BLOCK):
        p = rho * p + lines(spectrum, y)
        q = rho * q + lines(spectrum, BLOCK - 1 - y)
    ends[0], ends[1] = p, q


def both_cores(ends, sibling, whole, upper):
    p = jnp.where(upper, ends[0] + whole * sibling[0], sibling[0] + whole * ends[0])
    q = jnp.where(upper, sibling[1] + whole * ends[1], ends[1] + whole * sibling[1])
    return p, q


def leave_lines(ends, sibling, waves, here, core, sent):
    decay = waves[1]
    upper = core[...] > 0
    p, q = both_cores(ends, sibling, jnp.exp(-decay), upper)
    b = here[...]
    above = p + jnp.exp(-decay * (4.0 * b + 2.0)) * q
    below = q + jnp.exp(-decay * (4.0 * (BLOCKS - 1.0 - b) + 2.0)) * p
    above = jnp.where(upper, above[8:], above[:8])
    below = jnp.where(upper, below[8:], below[:8])
    for n in range(BLOCKS):
        value = jnp.where(b < n, above, below)
        for twin in range(2):
            sent[pl.ds(16 * n + 8 * twin, 8), :] = value


def solve_lines(received, spectrum, waves, here, core, ends, sibling, solved):
    rho, decay, scale, rounds = waves[0], waves[1], waves[2], waves[3]
    whole, double = jnp.exp(-decay), jnp.exp(-2.0 * decay)
    b = here[...]
    low = jnp.zeros((16, LANES), jnp.float32)
    high = jnp.zeros((16, LANES), jnp.float32)
    for n in range(BLOCKS):
        low = jnp.where(b > n, received[pl.ds(16 * n, 16), :] + double * low, low)
        m = BLOCKS - 1 - n
        high = jnp.where(b < m, received[pl.ds(16 * m, 16), :] + double * high, high)
    upper = core[...] > 0
    p, q = both_cores(ends, sibling, whole, upper)
    left = jnp.exp(-decay * (4.0 * b))
    right = jnp.exp(-decay * (4.0 * (BLOCKS - 1.0 - b)))
    up = (low + left * (q + double * (high + right * p))) * rounds
    down = high + right * (p + double * up)
    up = jnp.where(upper, sibling[0] + whole * up, up)
    down = jnp.where(upper, down, sibling[1] + whole * down)
    for y in range(BLOCK):
        up = rho * up + lines(spectrum, y)
        solved[pl.ds(16 * y, 16), :] = up
    for y in range(BLOCK - 1, -1, -1):
        down = rho * down
        solved[pl.ds(16 * y, 16), :] = scale * (lines(solved, y) + down)
        down = down + lines(spectrum, y)


def pencil_first(blocks, table, waves, spectrum, ends, rs):
    for chunk in range(4):
        x = [from_block(blocks, a, chunk, 0) for a in range(16)]
        put_first(*first_stage(x), rs, chunk)
    forward_x(table, rs, spectrum)
    local_sums(spectrum, waves, ends)


def pencil_middle(
    received, blocks, old, old_ends, sibling, table, waves, here, core, spectrum, ends, kept, rs, solved
):
    solve_lines(received, old, waves, here, core, old_ends, sibling, solved)
    backward_x(solved, table, rs)
    for chunk in range(4):
        x = first_stage_transposed(*get_first(rs, chunk))
        for a in range(16):
            kept[a, pl.ds(8 * chunk, 8), :] = x[a]
        x = [x[a] * from_block(blocks, a, chunk, 1) for a in range(16)]
        put_first(*first_stage(x), rs, chunk)
    forward_x(table, rs, spectrum)
    local_sums(spectrum, waves, ends)


def pencil_last(received, blocks, old, old_ends, sibling, kept, table, waves, here, core, sent, rs, solved):
    solve_lines(received, old, waves, here, core, old_ends, sibling, solved)
    backward_x(solved, table, rs)
    sums = [jnp.zeros((8, LANES), jnp.float32) for _ in range(4)]
    for chunk in range(4):
        x = first_stage_transposed(*get_first(rs, chunk))
        for a in range(16):
            before, new = kept[a, pl.ds(8 * chunk, 8), :], x[a]
            weight = from_block(blocks, a, chunk, 1)
            scaled = weight * before
            sums[0] += from_block(blocks, a, chunk, 0) * before
            sums[1] += scaled * before
            sums[2] += scaled * new
            sums[3] += weight * new * new
            place = 136 * (a // 2) + 16 * chunk + a % 2
            sent[pl.ds(place, 8, stride=2), :] = before
            sent[pl.ds(place + 64, 8, stride=2), :] = new
    lane = lax.broadcasted_iota(jnp.int32, (8, LANES), 1)
    line = jnp.zeros((8, LANES), jnp.float32)
    for q in range(4):
        line = jnp.where(lane == q, jnp.sum(sums[q]), line)
    for i in range(8):
        sent[pl.ds(136 * i + 128, 8), :] = line


def gather_sums(received, sent):
    for f in range(2):
        total = received[pl.ds(136 * 4 * f + 128, 1), :]
        for quarter in range(1, 4):
            total += received[pl.ds(136 * (4 * f + quarter) + 128, 1), :]
        sent[pl.ds(f, 16, stride=2), :] = jnp.broadcast_to(total, (16, LANES))


def enter_block(received, parts, sources, metric, helm, solution, resid, near, done):
    copies = []
    lane = lax.broadcasted_iota(jnp.int32, (1, LANES), 1)
    m = metric[...]
    inverse = 1.0 / m
    weight = helm[...] * inverse - SHIFT * m
    for f in range(2):
        totals = jnp.sum(parts[pl.ds(f, 16, stride=2), :], axis=0, keepdims=True)
        n0, n1, n2, n3 = [
            jnp.sum(jnp.where(lane == q, totals, 0.0), axis=1, keepdims=True) for q in range(4)
        ]
        delta = n0 + n1
        alpha = n0 / delta
        rest = n1 / delta
        gamma = n0 * rest * rest - 2.0 * alpha * rest * n1 + alpha * alpha * n2
        beta = gamma / n0
        p, q = rest + beta, -alpha
        second = gamma / (p * p * delta + 2.0 * p * q * (n1 + n2) + q * q * (n2 + n3))
        c0, c1 = alpha + second * p, second * q
        for h in range(2):
            pair = []
            for field in range(2):
                places = [136 * (4 * f + quarter) + 64 * field + h for quarter in range(4)]
                columns = [received[pl.ds(place, BLOCK, stride=2), :] for place in places]
                pair.append(jnp.concatenate(columns, axis=0).T)
            old, new = pair
            rows = slice(LANES * h, LANES * (h + 1))
            near[0, f, rows, :] = (c0 * old + c1 * new) * inverse[rows]
            near[1, f, rows, :] = (1.0 - c0) * sources[f, rows, :] - ((c0 + c1) * old + c1 * new) * weight[rows]
            for n, out in enumerate((solution, resid)):
                place = (f, pl.ds(LANES * h, LANES))
                copies.append(pltpu.make_async_copy(near.at[n, *place], out.at[*place], done.at[4 * n + 2 * f + h]))
                copies[-1].start()
    for copy in copies:
        copy.wait()


RS = pltpu.VMEM((16, 32, 2 * LANES), jnp.float32)
LINES = pltpu.VMEM((512, LANES), jnp.float32)
BLOCKS_SENT, SENT, SPECTRUM = (1024, LANES), (512, LANES), (512, LANES)
ENDS, KEPT = (2, 16, LANES), (16, 32, LANES)


def call(kernel, outs, scratch, **more):
    return pl.pallas_call(
        kernel,
        out_shape=[jax.ShapeDtypeStruct(s, jnp.float32) for s in outs],
        scratch_shapes=scratch,
        compiler_params=pltpu.CompilerParams(vmem_limit_bytes=32 * 1024 * 1024),
        **more,
    )


def far(*arrays):
    return [pltpu.with_memory_space_constraint(a, pltpu.HBM) for a in arrays]


def exchange(flat, axes, *shape):
    moved = lax.all_to_all(flat.reshape(*shape, LANES), axes, 0, 0, tiled=True)
    return moved.reshape(flat.shape)


def per_device(sources, metric, helm):
    table, waves = (jnp.asarray(a) for a in tables())
    line, column = ("half", "pair", "core"), ("gy", "pair", "core")
    here = lax.axis_index("gy") * lax.axis_size("pair") + lax.axis_index("pair")
    here = jnp.full((1, LANES), here, jnp.float32)
    core = jnp.full((1, LANES), lax.axis_index("core"), jnp.float32)
    block = pltpu.VMEM(metric.shape, metric.dtype)
    hbm, vmem = pl.BlockSpec(memory_space=pl.ANY), pl.BlockSpec(memory_space=pltpu.VMEM)

    def swap(ends):
        return lax.ppermute(ends, "core", [(0, 1), (1, 0)])

    (sent,) = call(
        leave_block,
        [BLOCKS_SENT],
        [pltpu.VMEM(sources.shape, sources.dtype), block, block, pltpu.SemaphoreType.DMA((4,))],
        in_specs=[hbm] * 5 + [vmem] * 2,
    )(*far(sources, metric, helm, table, waves), here, core)
    blocks = exchange(sent, line, 8, 128)
    first, ends = call(pencil_first, [SPECTRUM, ENDS], [RS])(blocks, table, waves)
    sibling = swap(ends)
    (sent,) = call(leave_lines, [SENT], [])(ends, sibling, waves, here, core)
    received = exchange(sent, column, 64, 8)
    second, more, kept = call(pencil_middle, [SPECTRUM, ENDS, KEPT], [RS, LINES])(
        received, blocks, first, ends, sibling, table, waves, here, core
    )
    twin = swap(more)
    (sent,) = call(leave_lines, [SENT], [])(more, twin, waves, here, core)
    received = exchange(sent, column, 64, 8)
    (sent,) = call(pencil_last, [(8 * 136, LANES)], [RS, LINES])(
        received, blocks, second, more, twin, kept, table, waves, here, core
    )
    received = exchange(sent, line, 8, 136)
    (parts,) = call(gather_sums, [(32, LANES)], [])(received)
    parts = exchange(parts, "gy", 16, 2)
    outs = call(
        enter_block,
        [sources.shape] * 2,
        [pltpu.VMEM((2, *sources.shape), jnp.float32), pltpu.SemaphoreType.DMA((8,))],
        in_specs=[vmem] * 5,
        out_specs=[hbm] * 2,
    )(received, parts, sources, metric, helm)
    return tuple(outs)


def solution(mesh):
    devices = mesh.devices.reshape(2, 2, 2, 16)
    finer = jax.sharding.Mesh(devices, ("half", "pair", "core", "gy"))
    line = ("half", "pair", "core")
    in_specs = (P(None, line, "gy"), P(line, "gy"), P(line, "gy"))
    out_specs = (P(None, line, "gy"), P(None, line, "gy"))
    return jax.shard_map(
        per_device, mesh=finer, in_specs=in_specs, out_specs=out_specs, check_vma=False
    )
```

```python
import functools
import math

import jax
import jax.numpy as jnp
import ml_dtypes
import numpy as np
from jax import lax
from jax.experimental import pallas as pl
from jax.experimental.pallas import tpu as pltpu
from jax.sharding import PartitionSpec as P

SHIFT = 0.001
ROWS = 16
BLOCK = 32
BLOCKS = 32
LANES = 128
LENGTH = ROWS * LANES


def frequency():
    t = np.arange(16)[:, None]
    k2 = np.arange(64)[None, :]
    first = t + 32 * k2
    second = np.where(t == 0, 16, 32 - t) + 32 * k2
    return np.concatenate([first, second], axis=1)


def tables():
    freq = frequency()
    b = np.arange(LANES)
    phase = (freq[:, None, :] * (2 * b[None, :, None] + 1)) % (4 * LENGTH)
    angle = phase * (math.pi / (2 * LENGTH))
    scale = np.where(freq == 0, math.sqrt(1.0 / LENGTH), math.sqrt(2.0 / LENGTH))[:, None, :]
    even, odd = scale * np.cos(angle), scale * np.sin(angle)
    sign = np.where(np.arange(LANES) < 64, -1.0, 1.0)
    full = np.concatenate([even, odd * sign], axis=1)
    full[0, :LANES, 64:] = 0.0
    full[0, LANES:, :64] = 0.0
    full[0, LANES:, 64:] = even[0, :, 64:]
    high = full.astype(ml_dtypes.bfloat16)
    low = (full - high.astype(np.float64)).astype(ml_dtypes.bfloat16)
    forward = np.concatenate([high, low], axis=2)
    sigma = 4.0 * np.sin(math.pi * freq / (2 * LENGTH)) ** 2 + SHIFT
    mu = 2.0 * np.arcsinh(np.sqrt(sigma) / 2.0)
    waves = [np.exp(-mu), BLOCK * mu, 0.5 / np.sinh(mu), 1.0 / (1.0 - np.exp(-4.0 * BLOCK * BLOCKS * mu))]
    return np.stack([forward, np.swapaxes(forward, 1, 2)], axis=1), np.stack(waves).astype(np.float32)


def cos16(n):
    return float(math.cos(math.pi * n / 16))


def sin16(n):
    return float(math.sin(math.pi * n / 16))


def combine(terms):
    total = None
    for c, v in terms:
        if abs(c) < 1e-12:
            continue
        if abs(abs(c) - 1.0) < 1e-12:
            if total is None:
                total = v if c > 0 else -v
            else:
                total = total + v if c > 0 else total - v
        else:
            total = c * v if total is None else total + c * v
    return total


def first_stage(x):
    p = {a: x[a] + x[16 - a] for a in range(1, 8)}
    m = {a: x[a] - x[16 - a] for a in range(1, 8)}
    R, S = {}, {}
    for j in range(1, 8):
        c, s = (m, p) if j % 2 else (p, m)
        ev = combine([(1.0, x[0])] + [(cos16(j * a), c[a]) for a in (2, 4, 6)] + [(cos16(8 * j), x[8])])
        od = combine([(cos16(j * a), c[a]) for a in (1, 3, 5, 7)])
        R[j], R[16 - j] = ev + od, ev - od
        ev = combine([(sin16(j * a), s[a]) for a in (2, 4, 6)] + [(sin16(8 * j), x[8])])
        od = combine([(sin16(j * a), s[a]) for a in (1, 3, 5, 7)])
        S[j], S[16 - j] = od + ev, od - ev
    outer, inner = x[0] + x[8], p[2] + p[6]
    R[8] = outer + p[4] - inner
    S[8] = (m[1] + m[5]) - (m[3] + m[7])
    even, odd = outer + p[4] + inner, (p[1] + p[7]) + (p[3] + p[5])
    R[0], R[16] = even + odd, even - odd
    return R, S


def first_stage_transposed(R, S):
    rp = {j: R[j] + R[16 - j] for j in range(1, 8)}
    rm = {j: R[j] - R[16 - j] for j in range(1, 8)}
    sp = {j: S[j] + S[16 - j] for j in range(1, 8)}
    sm = {j: S[j] - S[16 - j] for j in range(1, 8)}
    ends, wide = R[0] + R[16], R[0] - R[16]
    x = {}
    for a in range(1, 8):
        r, s = (rm, sp) if a % 2 else (rp, sm)
        ce = combine([(1.0, wide if a % 2 else ends), (cos16(8 * a), R[8])] + [(cos16(j * a), r[j]) for j in (2, 4, 6)])
        co = combine([(cos16(j * a), r[j]) for j in (1, 3, 5, 7)])
        se = combine([(sin16(8 * a), S[8])] + [(sin16(j * a), s[j]) for j in (2, 4, 6)])
        so = combine([(sin16(j * a), s[j]) for j in (1, 3, 5, 7)])
        x[a], x[16 - a] = (ce + so) + (co + se), (ce + so) - (co + se)
    even = ends + R[8] + rp[2] + rp[4] + rp[6]
    x[0] = even + (rp[1] + rp[7]) + (rp[3] + rp[5])
    x[8] = ends + R[8] - rp[2] + rp[4] - rp[6] + (sm[1] - sm[3]) + (sm[5] - sm[7])
    return x


def split(value):
    high = value.astype(jnp.bfloat16)
    return high, (value - high.astype(jnp.float32)).astype(jnp.bfloat16)


def forward_dot(value, table, t):
    high, low = split(value)
    both = jnp.dot(jnp.concatenate([high, low], axis=0), table[t, 0, :, :LANES], preferred_element_type=jnp.float32)
    third = jnp.dot(high, table[t, 0, :, LANES:], preferred_element_type=jnp.float32)
    return both[:32] + (both[32:] + third)


def backward_dot(value, table, t):
    high, low = split(value)
    both = jnp.dot(jnp.concatenate([high, low], axis=0), table[t, 1, :LANES, :], preferred_element_type=jnp.float32)
    third = jnp.dot(high, table[t, 1, LANES:, :], preferred_element_type=jnp.float32)
    return both[:32] + (both[32:] + third)


def put_first(R, S, rs, chunk):
    rows = pl.ds(8 * chunk, 8)
    for t in range(16):
        rs[t, rows, 0:LANES] = R[t]
        rs[t, rows, LANES : 2 * LANES] = R[16] if t == 0 else S[t]


def get_first(rs, chunk):
    rows = pl.ds(8 * chunk, 8)
    R = {t: rs[t, rows, 0:LANES] for t in range(16)}
    S = {t: rs[t, rows, LANES : 2 * LANES] for t in range(1, 16)}
    R[16] = rs[0, rows, LANES : 2 * LANES]
    return R, S


def leave_block(sources, metric, helm, table, waves, here, core, sent, source_here, metric_here, helm_here, arrived):
    moves = [(metric, metric_here)]
    moves += [(sources.at[f], source_here.at[f]) for f in range(2)] + [(helm, helm_here)]
    copies = [pltpu.make_async_copy(a, b, arrived.at[n]) for n, (a, b) in enumerate(moves)]
    for copy in copies:
        copy.start()
    copies[0].wait()
    inverse = 1.0 / metric_here[...]
    for f in range(2):
        copies[1 + f].wait()
        field = source_here[f] * inverse
        for h in range(2):
            across = field[LANES * h : LANES * (h + 1), :].T
            for quarter in range(4):
                rows = pl.ds(LANES * (4 * f + quarter) + h, BLOCK, stride=2)
                sent[rows, :] = across[BLOCK * quarter : BLOCK * (quarter + 1)]
    copies[3].wait()
    weight = helm_here[...] * (inverse * inverse) - SHIFT
    for h in range(2):
        across = weight[LANES * h : LANES * (h + 1), :].T
        for quarter in range(4):
            for f in range(2):
                rows = pl.ds(LANES * (4 * f + quarter) + 64 + h, BLOCK, stride=2)
                sent[rows, :] = across[BLOCK * quarter : BLOCK * (quarter + 1)]


def from_block(blocks, a, chunk, field):
    return blocks[pl.ds(LANES * (a // 2) + 64 * field + 16 * chunk + a % 2, 8, stride=2), :]


def lines(spectrum, y):
    return spectrum[pl.ds(16 * y, 16), :]


def forward_x(table, rs, spectrum):
    for t in range(16):
        spectrum[pl.ds(t, BLOCK, stride=16), :] = forward_dot(rs[t], table, t)


def backward_x(spectrum, table, rs):
    for t in range(16):
        rs[t] = backward_dot(spectrum[pl.ds(t, BLOCK, stride=16), :], table, t)


def local_sums(spectrum, waves, ends):
    rho = waves[0]
    p = lines(spectrum, 0)
    q = lines(spectrum, BLOCK - 1)
    for y in range(1, BLOCK):
        p = rho * p + lines(spectrum, y)
        q = rho * q + lines(spectrum, BLOCK - 1 - y)
    ends[0], ends[1] = p, q


def both_cores(ends, sibling, whole, upper):
    p = jnp.where(upper, ends[0] + whole * sibling[0], sibling[0] + whole * ends[0])
    q = jnp.where(upper, sibling[1] + whole * ends[1], ends[1] + whole * sibling[1])
    return p, q


def leave_lines(ends, sibling, waves, here, core, sent):
    decay = waves[1]
    upper = core[...] > 0
    p, q = both_cores(ends, sibling, jnp.exp(-decay), upper)
    b = here[...]
    above = p + jnp.exp(-decay * (4.0 * b + 2.0)) * q
    below = q + jnp.exp(-decay * (4.0 * (BLOCKS - 1.0 - b) + 2.0)) * p
    above = jnp.where(upper, above[8:], above[:8])
    below = jnp.where(upper, below[8:], below[:8])
    for n in range(BLOCKS):
        value = jnp.where(b < n, above, below)
        for twin in range(2):
            sent[pl.ds(16 * n + 8 * twin, 8), :] = value


def solve_lines(received, spectrum, waves, here, core, ends, sibling, solved):
    rho, decay, scale, rounds = waves[0], waves[1], waves[2], waves[3]
    whole, double = jnp.exp(-decay), jnp.exp(-2.0 * decay)
    b = here[...]
    low = jnp.zeros((16, LANES), jnp.float32)
    high = jnp.zeros((16, LANES), jnp.float32)
    for n in range(BLOCKS):
        low = jnp.where(b > n, received[pl.ds(16 * n, 16), :] + double * low, low)
        m = BLOCKS - 1 - n
        high = jnp.where(b < m, received[pl.ds(16 * m, 16), :] + double * high, high)
    upper = core[...] > 0
    p, q = both_cores(ends, sibling, whole, upper)
    left = jnp.exp(-decay * (4.0 * b))
    right = jnp.exp(-decay * (4.0 * (BLOCKS - 1.0 - b)))
    up = (low + left * (q + double * (high + right * p))) * rounds
    down = high + right * (p + double * up)
    up = jnp.where(upper, sibling[0] + whole * up, up)
    down = jnp.where(upper, down, sibling[1] + whole * down)
    for y in range(BLOCK):
        up = rho * up + lines(spectrum, y)
        solved[pl.ds(16 * y, 16), :] = up
    for y in range(BLOCK - 1, -1, -1):
        down = rho * down
        solved[pl.ds(16 * y, 16), :] = scale * (lines(solved, y) + down)
        down = down + lines(spectrum, y)


def pencil_first(blocks, table, waves, spectrum, ends, rs):
    for chunk in range(4):
        x = [from_block(blocks, a, chunk, 0) for a in range(16)]
        put_first(*first_stage(x), rs, chunk)
    forward_x(table, rs, spectrum)
    local_sums(spectrum, waves, ends)


def pencil_middle(
    received, blocks, old, old_ends, sibling, table, waves, here, core, spectrum, ends, kept, sums, rs, solved
):
    solve_lines(received, old, waves, here, core, old_ends, sibling, solved)
    backward_x(solved, table, rs)
    totals = [jnp.zeros((8, LANES), jnp.float32) for _ in range(2)]
    for chunk in range(4):
        x = first_stage_transposed(*get_first(rs, chunk))
        scaled = [x[a] * from_block(blocks, a, chunk, 1) for a in range(16)]
        for a in range(16):
            kept[a, pl.ds(8 * chunk, 8), :] = x[a]
            totals[0] += from_block(blocks, a, chunk, 0) * x[a]
            totals[1] += scaled[a] * x[a]
        put_first(*first_stage(scaled), rs, chunk)
    sums[0], sums[1] = totals
    forward_x(table, rs, spectrum)
    local_sums(spectrum, waves, ends)


def pencil_last(received, blocks, old, old_ends, sibling, kept, first, table, waves, here, core, sent, rs, solved):
    solve_lines(received, old, waves, here, core, old_ends, sibling, solved)
    backward_x(solved, table, rs)
    n0, n1 = (jnp.sum(first[n], axis=(0, 1), keepdims=True) for n in range(2))
    positive = n0 + n1 > 0.0
    step = jnp.where(positive, n0 / jnp.where(positive, n0 + n1, 1.0), 0.0)
    step = jnp.clip(step, 0.0, 2.0)
    sums = [jnp.zeros((8, LANES), jnp.float32) for _ in range(7)]
    for chunk in range(4):
        x = first_stage_transposed(*get_first(rs, chunk))
        for a in range(16):
            before, new = kept[a, pl.ds(8 * chunk, 8), :], x[a]
            weight, source = from_block(blocks, a, chunk, 1), from_block(blocks, a, chunk, 0)
            g, h = source + weight * before, before + new
            u1, z1 = source - step * g, before - step * h
            wz, wh = weight * z1, weight * h
            for q, (one, two) in enumerate(((u1, z1), (u1, h), (g, z1), (g, h), (wz, z1), (wz, h), (wh, h))):
                sums[q] += one * two
            place = 136 * (a // 2) + 16 * chunk + a % 2
            sent[pl.ds(place, 8, stride=2), :] = before
            sent[pl.ds(place + 64, 8, stride=2), :] = new
    lane = lax.broadcasted_iota(jnp.int32, (8, LANES), 1)
    line = jnp.where(lane == 7, n0, jnp.where(lane == 8, n1, jnp.where(lane == 9, step, 0.0)))
    for q in range(7):
        line = jnp.where(lane == q, jnp.sum(sums[q], axis=(0, 1), keepdims=True), line)
    for i in range(8):
        sent[pl.ds(136 * i + 128, 8), :] = line


def gather_sums(received, sent):
    row = lax.broadcasted_iota(jnp.int32, (8, LANES), 0)
    rows = received[pl.ds(128, 8), :]
    for i in range(1, 8):
        rows = jnp.where(row == i, received[pl.ds(136 * i + 128, 8), :], rows)
    for n in range(16):
        sent[pl.ds(8 * n, 8), :] = rows


def enter_block(received, parts, sources, metric, helm, solution, resid, near, done):
    copies = []
    lane = lax.broadcasted_iota(jnp.int32, (1, LANES), 1)
    row = lax.broadcasted_iota(jnp.int32, (LANES, LANES), 0)
    every = parts[...]
    steps = jnp.sum(jnp.where(lane == 9, every, 0.0), axis=1, keepdims=True)

    def pick(line, q):
        return jnp.sum(jnp.where(lane == q, line, 0.0), axis=1, keepdims=True)

    m = metric[...]
    inverse = 1.0 / m
    weight = helm[...] * inverse - SHIFT * m
    for f in range(2):
        mine = jnp.where(row % 8 // 4 == f, every, 0.0)
        zeroth = jnp.sum(mine, axis=0, keepdims=True)
        n0, n1 = pick(zeroth, 7), pick(zeroth, 8)
        delta = n0 + n1
        alpha, rest = n0 / delta, n1 / delta
        away = alpha - steps
        moved = away * mine
        first = jnp.sum(moved, axis=0, keepdims=True)
        second = jnp.sum(away * moved, axis=0, keepdims=True)
        gamma = pick(zeroth, 0) - (pick(first, 1) + pick(first, 2)) + pick(second, 3)
        inner = pick(zeroth, 4) - 2.0 * pick(first, 5) + pick(second, 6)
        cross = pick(zeroth, 2) - pick(first, 3)
        beta = gamma / n0
        size = gamma / (gamma + inner + 2.0 * beta * cross + beta * beta * delta)
        c0, c1 = alpha + size * (rest + beta), -size * alpha
        for h in range(2):
            pair = []
            for field in range(2):
                places = [136 * (4 * f + quarter) + 64 * field + h for quarter in range(4)]
                columns = [received[pl.ds(place, BLOCK, stride=2), :] for place in places]
                pair.append(jnp.concatenate(columns, axis=0).T)
            old, new = pair
            rows = slice(LANES * h, LANES * (h + 1))
            near[0, f, rows, :] = (c0 * old + c1 * new) * inverse[rows]
            near[1, f, rows, :] = (1.0 - c0) * sources[f, rows, :] - ((c0 + c1) * old + c1 * new) * weight[rows]
            for n, out in enumerate((solution, resid)):
                place = (f, pl.ds(LANES * h, LANES))
                copies.append(pltpu.make_async_copy(near.at[n, *place], out.at[*place], done.at[4 * n + 2 * f + h]))
                copies[-1].start()
    for copy in copies:
        copy.wait()


RS = pltpu.VMEM((16, 32, 2 * LANES), jnp.float32)
LINES = pltpu.VMEM((512, LANES), jnp.float32)
BLOCKS_SENT, SENT, SPECTRUM = (1024, LANES), (512, LANES), (512, LANES)
ENDS, KEPT = (2, 16, LANES), (16, 32, LANES)


def call(kernel, outs, scratch, **more):
    return pl.pallas_call(
        kernel,
        out_shape=[jax.ShapeDtypeStruct(s, jnp.float32) for s in outs],
        scratch_shapes=scratch,
        compiler_params=pltpu.CompilerParams(vmem_limit_bytes=32 * 1024 * 1024),
        **more,
    )


def far(*arrays):
    return [pltpu.with_memory_space_constraint(a, pltpu.HBM) for a in arrays]


def exchange(flat, axes, *shape):
    moved = lax.all_to_all(flat.reshape(*shape, LANES), axes, 0, 0, tiled=True)
    return moved.reshape(flat.shape)


def per_device(sources, metric, helm):
    table, waves = (jnp.asarray(a) for a in tables())
    line, column = ("half", "pair", "core"), ("gy", "pair", "core")
    here = lax.axis_index("gy") * lax.axis_size("pair") + lax.axis_index("pair")
    here = jnp.full((1, LANES), here, jnp.float32)
    core = jnp.full((1, LANES), lax.axis_index("core"), jnp.float32)
    block = pltpu.VMEM(metric.shape, metric.dtype)
    hbm, vmem = pl.BlockSpec(memory_space=pl.ANY), pl.BlockSpec(memory_space=pltpu.VMEM)

    def swap(ends):
        return lax.ppermute(ends, "core", [(0, 1), (1, 0)])

    (sent,) = call(
        leave_block,
        [BLOCKS_SENT],
        [pltpu.VMEM(sources.shape, sources.dtype), block, block, pltpu.SemaphoreType.DMA((4,))],
        in_specs=[hbm] * 5 + [vmem] * 2,
    )(*far(sources, metric, helm, table, waves), here, core)
    blocks = exchange(sent, line, 8, 128)
    first, ends = call(pencil_first, [SPECTRUM, ENDS], [RS])(blocks, table, waves)
    sibling = swap(ends)
    (sent,) = call(leave_lines, [SENT], [])(ends, sibling, waves, here, core)
    received = exchange(sent, column, 64, 8)
    second, more, kept, sums = call(pencil_middle, [SPECTRUM, ENDS, KEPT, (2, 8, LANES)], [RS, LINES])(
        received, blocks, first, ends, sibling, table, waves, here, core
    )
    twin = swap(more)
    (sent,) = call(leave_lines, [SENT], [])(more, twin, waves, here, core)
    received = exchange(sent, column, 64, 8)
    (sent,) = call(pencil_last, [(8 * 136, LANES)], [RS, LINES])(
        received, blocks, second, more, twin, kept, sums, table, waves, here, core
    )
    received = exchange(sent, line, 8, 136)
    (parts,) = call(gather_sums, [(LANES, LANES)], [])(received)
    parts = exchange(parts, "gy", 16, 8)
    outs = call(
        enter_block,
        [sources.shape] * 2,
        [pltpu.VMEM((2, *sources.shape), jnp.float32), pltpu.SemaphoreType.DMA((8,))],
        in_specs=[vmem] * 5,
        out_specs=[hbm] * 2,
    )(received, parts, sources, metric, helm)
    return tuple(outs)


def solution(mesh):
    devices = mesh.devices.reshape(2, 2, 2, 16)
    finer = jax.sharding.Mesh(devices, ("half", "pair", "core", "gy"))
    line = ("half", "pair", "core")
    in_specs = (P(None, line, "gy"), P(line, "gy"), P(line, "gy"))
    out_specs = (P(None, line, "gy"), P(None, line, "gy"))
    return jax.shard_map(
        per_device, mesh=finer, in_specs=in_specs, out_specs=out_specs, check_vma=False
    )
```

```python
import functools
import math

import jax
import jax.numpy as jnp
import ml_dtypes
import numpy as np
from jax import lax
from jax.experimental import pallas as pl
from jax.experimental.pallas import tpu as pltpu
from jax.sharding import PartitionSpec as P

SHIFT = 0.001
ROWS = 16
BLOCK = 32
BLOCKS = 32
LANES = 128
LENGTH = ROWS * LANES


def frequency():
    t = np.arange(16)[:, None]
    k2 = np.arange(64)[None, :]
    first = t + 32 * k2
    second = np.where(t == 0, 16, 32 - t) + 32 * k2
    return np.concatenate([first, second], axis=1)


def tables():
    freq = frequency()
    b = np.arange(LANES)
    phase = (freq[:, None, :] * (2 * b[None, :, None] + 1)) % (4 * LENGTH)
    angle = phase * (math.pi / (2 * LENGTH))
    scale = np.where(freq == 0, math.sqrt(1.0 / LENGTH), math.sqrt(2.0 / LENGTH))[:, None, :]
    even, odd = scale * np.cos(angle), scale * np.sin(angle)
    sign = np.where(np.arange(LANES) < 64, -1.0, 1.0)
    full = np.concatenate([even, odd * sign], axis=1)
    full[0, :LANES, 64:] = 0.0
    full[0, LANES:, :64] = 0.0
    full[0, LANES:, 64:] = even[0, :, 64:]
    high = full.astype(ml_dtypes.bfloat16)
    low = (full - high.astype(np.float64)).astype(ml_dtypes.bfloat16)
    forward = np.concatenate([high, low], axis=2)
    sigma = 4.0 * np.sin(math.pi * freq / (2 * LENGTH)) ** 2 + SHIFT
    mu = 2.0 * np.arcsinh(np.sqrt(sigma) / 2.0)
    waves = [np.exp(-mu), BLOCK * mu, 0.5 / np.sinh(mu), 1.0 / (1.0 - np.exp(-4.0 * BLOCK * BLOCKS * mu))]
    return np.stack([forward, np.swapaxes(forward, 1, 2)], axis=1), np.stack(waves).astype(np.float32)


def cos16(n):
    return float(math.cos(math.pi * n / 16))


def sin16(n):
    return float(math.sin(math.pi * n / 16))


def combine(terms):
    total = None
    for c, v in terms:
        if abs(c) < 1e-12:
            continue
        if abs(abs(c) - 1.0) < 1e-12:
            if total is None:
                total = v if c > 0 else -v
            else:
                total = total + v if c > 0 else total - v
        else:
            total = c * v if total is None else total + c * v
    return total


def first_stage(x):
    p = {a: x[a] + x[16 - a] for a in range(1, 8)}
    m = {a: x[a] - x[16 - a] for a in range(1, 8)}
    R, S = {}, {}
    for j in range(1, 8):
        c, s = (m, p) if j % 2 else (p, m)
        ev = combine([(1.0, x[0])] + [(cos16(j * a), c[a]) for a in (2, 4, 6)] + [(cos16(8 * j), x[8])])
        od = combine([(cos16(j * a), c[a]) for a in (1, 3, 5, 7)])
        R[j], R[16 - j] = ev + od, ev - od
        ev = combine([(sin16(j * a), s[a]) for a in (2, 4, 6)] + [(sin16(8 * j), x[8])])
        od = combine([(sin16(j * a), s[a]) for a in (1, 3, 5, 7)])
        S[j], S[16 - j] = od + ev, od - ev
    outer, inner = x[0] + x[8], p[2] + p[6]
    R[8] = outer + p[4] - inner
    S[8] = (m[1] + m[5]) - (m[3] + m[7])
    even, odd = outer + p[4] + inner, (p[1] + p[7]) + (p[3] + p[5])
    R[0], R[16] = even + odd, even - odd
    return R, S


def first_stage_transposed(R, S):
    rp = {j: R[j] + R[16 - j] for j in range(1, 8)}
    rm = {j: R[j] - R[16 - j] for j in range(1, 8)}
    sp = {j: S[j] + S[16 - j] for j in range(1, 8)}
    sm = {j: S[j] - S[16 - j] for j in range(1, 8)}
    ends, wide = R[0] + R[16], R[0] - R[16]
    x = {}
    for a in range(1, 8):
        r, s = (rm, sp) if a % 2 else (rp, sm)
        ce = combine([(1.0, wide if a % 2 else ends), (cos16(8 * a), R[8])] + [(cos16(j * a), r[j]) for j in (2, 4, 6)])
        co = combine([(cos16(j * a), r[j]) for j in (1, 3, 5, 7)])
        se = combine([(sin16(8 * a), S[8])] + [(sin16(j * a), s[j]) for j in (2, 4, 6)])
        so = combine([(sin16(j * a), s[j]) for j in (1, 3, 5, 7)])
        x[a], x[16 - a] = (ce + so) + (co + se), (ce + so) - (co + se)
    even = ends + R[8] + rp[2] + rp[4] + rp[6]
    x[0] = even + (rp[1] + rp[7]) + (rp[3] + rp[5])
    x[8] = ends + R[8] - rp[2] + rp[4] - rp[6] + (sm[1] - sm[3]) + (sm[5] - sm[7])
    return x


def split(value):
    high = value.astype(jnp.bfloat16)
    return high, (value - high.astype(jnp.float32)).astype(jnp.bfloat16)


def forward_dot(value, table, t):
    high, low = split(value)
    both = jnp.dot(jnp.concatenate([high, low], axis=0), table[t, 0, :, :LANES], preferred_element_type=jnp.float32)
    third = jnp.dot(high, table[t, 0, :, LANES:], preferred_element_type=jnp.float32)
    return both[:32] + (both[32:] + third)


def backward_dot(value, table, t):
    high, low = split(value)
    both = jnp.dot(jnp.concatenate([high, low], axis=0), table[t, 1, :LANES, :], preferred_element_type=jnp.float32)
    third = jnp.dot(high, table[t, 1, LANES:, :], preferred_element_type=jnp.float32)
    return both[:32] + (both[32:] + third)


def put_first(R, S, rs, chunk):
    rows = pl.ds(8 * chunk, 8)
    for t in range(16):
        rs[t, rows, 0:LANES] = R[t]
        rs[t, rows, LANES : 2 * LANES] = R[16] if t == 0 else S[t]


def get_first(rs, chunk):
    rows = pl.ds(8 * chunk, 8)
    R = {t: rs[t, rows, 0:LANES] for t in range(16)}
    S = {t: rs[t, rows, LANES : 2 * LANES] for t in range(1, 16)}
    R[16] = rs[0, rows, LANES : 2 * LANES]
    return R, S


def leave_block(sources, metric, helm, table, waves, here, core, sent, source_here, metric_here, helm_here, arrived):
    moves = [(metric, metric_here)]
    moves += [(sources, source_here), (helm, helm_here)]
    copies = [pltpu.make_async_copy(a, b, arrived.at[n]) for n, (a, b) in enumerate(moves)]
    for copy in copies:
        copy.start()
    copies[0].wait()
    inverse = 1.0 / metric_here[...]
    for f in range(2):
        if f == 0:
            copies[1].wait()
        field = source_here[f] * inverse
        for h in range(2):
            across = field[LANES * h : LANES * (h + 1), :].T
            for quarter in range(4):
                rows = pl.ds(LANES * (4 * f + quarter) + h, BLOCK, stride=2)
                sent[rows, :] = across[BLOCK * quarter : BLOCK * (quarter + 1)]
    copies[2].wait()
    weight = helm_here[...] * (inverse * inverse) - SHIFT
    for h in range(2):
        across = weight[LANES * h : LANES * (h + 1), :].T
        for quarter in range(4):
            for f in range(2):
                rows = pl.ds(LANES * (4 * f + quarter) + 64 + h, BLOCK, stride=2)
                sent[rows, :] = across[BLOCK * quarter : BLOCK * (quarter + 1)]


def from_block(blocks, a, chunk, field):
    return blocks[pl.ds(LANES * (a // 2) + 64 * field + 16 * chunk + a % 2, 8, stride=2), :]


def lines(spectrum, y):
    return spectrum[pl.ds(16 * y, 16), :]


def forward_x(table, rs, spectrum):
    for t in range(16):
        spectrum[pl.ds(t, BLOCK, stride=16), :] = forward_dot(rs[t], table, t)


def backward_x(spectrum, table, rs):
    for t in range(16):
        rs[t] = backward_dot(spectrum[pl.ds(t, BLOCK, stride=16), :], table, t)


def local_sums(spectrum, waves, ends):
    rho = waves[0]
    p = lines(spectrum, 0)
    q = lines(spectrum, BLOCK - 1)
    for y in range(1, BLOCK):
        p = rho * p + lines(spectrum, y)
        q = rho * q + lines(spectrum, BLOCK - 1 - y)
    ends[0], ends[1] = p, q


def both_cores(ends, sibling, whole, upper):
    p = jnp.where(upper, ends[0] + whole * sibling[0], sibling[0] + whole * ends[0])
    q = jnp.where(upper, sibling[1] + whole * ends[1], ends[1] + whole * sibling[1])
    return p, q


def leave_lines(ends, sibling, waves, here, core, sent):
    decay = waves[1]
    upper = core[...] > 0
    p, q = both_cores(ends, sibling, jnp.exp(-decay), upper)
    b = here[...]
    above = p + jnp.exp(-decay * (4.0 * b + 2.0)) * q
    below = q + jnp.exp(-decay * (4.0 * (BLOCKS - 1.0 - b) + 2.0)) * p
    above = jnp.where(upper, above[8:], above[:8])
    below = jnp.where(upper, below[8:], below[:8])
    for n in range(BLOCKS):
        value = jnp.where(b < n, above, below)
        for twin in range(2):
            sent[pl.ds(16 * n + 8 * twin, 8), :] = value


def solve_lines(received, spectrum, waves, here, core, ends, sibling, solved):
    rho, decay, scale, rounds = waves[0], waves[1], waves[2], waves[3]
    whole, double = jnp.exp(-decay), jnp.exp(-2.0 * decay)
    b = here[...]
    low = jnp.zeros((16, LANES), jnp.float32)
    high = jnp.zeros((16, LANES), jnp.float32)
    for n in range(BLOCKS):
        low = jnp.where(b > n, received[pl.ds(16 * n, 16), :] + double * low, low)
        m = BLOCKS - 1 - n
        high = jnp.where(b < m, received[pl.ds(16 * m, 16), :] + double * high, high)
    upper = core[...] > 0
    p, q = both_cores(ends, sibling, whole, upper)
    left = jnp.exp(-decay * (4.0 * b))
    right = jnp.exp(-decay * (4.0 * (BLOCKS - 1.0 - b)))
    up = (low + left * (q + double * (high + right * p))) * rounds
    down = high + right * (p + double * up)
    up = jnp.where(upper, sibling[0] + whole * up, up)
    down = jnp.where(upper, down, sibling[1] + whole * down)
    for y in range(BLOCK):
        up = rho * up + lines(spectrum, y)
        solved[pl.ds(16 * y, 16), :] = up
    for y in range(BLOCK - 1, -1, -1):
        down = rho * down
        solved[pl.ds(16 * y, 16), :] = scale * (lines(solved, y) + down)
        down = down + lines(spectrum, y)


def pencil_first(blocks, table, waves, spectrum, ends, rs):
    for chunk in range(4):
        x = [from_block(blocks, a, chunk, 0) for a in range(16)]
        put_first(*first_stage(x), rs, chunk)
    forward_x(table, rs, spectrum)
    local_sums(spectrum, waves, ends)


def pencil_middle(
    received, blocks, old, old_ends, sibling, table, waves, here, core, spectrum, ends, kept, sums, rs, solved
):
    solve_lines(received, old, waves, here, core, old_ends, sibling, solved)
    backward_x(solved, table, rs)
    totals = [jnp.zeros((8, LANES), jnp.float32) for _ in range(2)]
    for chunk in range(4):
        x = first_stage_transposed(*get_first(rs, chunk))
        scaled = [x[a] * from_block(blocks, a, chunk, 1) for a in range(16)]
        for a in range(16):
            kept[a, pl.ds(8 * chunk, 8), :] = x[a]
            totals[0] += from_block(blocks, a, chunk, 0) * x[a]
            totals[1] += scaled[a] * x[a]
        put_first(*first_stage(scaled), rs, chunk)
    sums[0], sums[1] = totals
    forward_x(table, rs, spectrum)
    local_sums(spectrum, waves, ends)


def pencil_last(received, blocks, old, old_ends, sibling, kept, first, table, waves, here, core, sent, rs, solved):
    solve_lines(received, old, waves, here, core, old_ends, sibling, solved)
    backward_x(solved, table, rs)
    n0, n1 = (jnp.sum(first[n], axis=(0, 1), keepdims=True) for n in range(2))
    positive = n0 + n1 > 0.0
    step = jnp.where(positive, n0 / jnp.where(positive, n0 + n1, 1.0), 0.0)
    step = jnp.clip(step, 0.0, 2.0)
    sums = [jnp.zeros((8, LANES), jnp.float32) for _ in range(7)]
    for chunk in range(4):
        x = first_stage_transposed(*get_first(rs, chunk))
        for a in range(16):
            before, new = kept[a, pl.ds(8 * chunk, 8), :], x[a]
            weight, source = from_block(blocks, a, chunk, 1), from_block(blocks, a, chunk, 0)
            g, h = source + weight * before, before + new
            u1, z1 = source - step * g, before - step * h
            wz, wh = weight * z1, weight * h
            for q, (one, two) in enumerate(((u1, z1), (u1, h), (g, z1), (g, h), (wz, z1), (wz, h), (wh, h))):
                sums[q] += one * two
            place = 130 * (a // 2) + 16 * chunk + a % 2
            sent[pl.ds(place, 8, stride=2), :] = before
            sent[pl.ds(place + 64, 8, stride=2), :] = new
    lane = lax.broadcasted_iota(jnp.int32, (2, LANES), 1)
    line = jnp.where(lane == 7, n0, jnp.where(lane == 8, n1, jnp.where(lane == 9, step, 0.0)))
    for q in range(7):
        line = jnp.where(lane == q, jnp.sum(sums[q], axis=(0, 1), keepdims=True), line)
    for i in range(8):
        sent[pl.ds(130 * i + 128, 2), :] = line


def gather_sums(received, sent):
    rows = received[pl.ds(128, 8, stride=130), :]
    for n in range(16):
        sent[pl.ds(8 * n, 8), :] = rows


def enter_block(received, parts, sources, metric, helm, solution, resid, near, done):
    copies = []
    lane = lax.broadcasted_iota(jnp.int32, (1, LANES), 1)
    row = lax.broadcasted_iota(jnp.int32, (LANES, LANES), 0)
    every = parts[...]
    steps = jnp.sum(jnp.where(lane == 9, every, 0.0), axis=1, keepdims=True)

    def pick(line, q):
        return jnp.sum(jnp.where(lane == q, line, 0.0), axis=1, keepdims=True)

    m = metric[...]
    inverse = 1.0 / m
    weight = helm[...] * inverse - SHIFT * m
    for f in range(2):
        mine = jnp.where(row % 8 // 4 == f, every, 0.0)
        zeroth = jnp.sum(mine, axis=0, keepdims=True)
        n0, n1 = pick(zeroth, 7), pick(zeroth, 8)
        delta = n0 + n1
        alpha, rest = n0 / delta, n1 / delta
        away = alpha - steps
        moved = away * mine
        first = jnp.sum(moved, axis=0, keepdims=True)
        second = jnp.sum(away * moved, axis=0, keepdims=True)
        gamma = pick(zeroth, 0) - (pick(first, 1) + pick(first, 2)) + pick(second, 3)
        inner = pick(zeroth, 4) - 2.0 * pick(first, 5) + pick(second, 6)
        cross = pick(zeroth, 2) - pick(first, 3)
        beta = gamma / n0
        size = gamma / (gamma + inner + 2.0 * beta * cross + beta * beta * delta)
        c0, c1 = alpha + size * (rest + beta), -size * alpha
        for h in range(2):
            pair = []
            for field in range(2):
                places = [130 * (4 * f + quarter) + 64 * field + h for quarter in range(4)]
                columns = [received[pl.ds(place, BLOCK, stride=2), :] for place in places]
                pair.append(jnp.concatenate(columns, axis=0).T)
            old, new = pair
            rows = slice(LANES * h, LANES * (h + 1))
            near[0, f, rows, :] = (c0 * old + c1 * new) * inverse[rows]
            near[1, f, rows, :] = (1.0 - c0) * sources[f, rows, :] - ((c0 + c1) * old + c1 * new) * weight[rows]
        for n, out in enumerate((solution, resid)):
            copies.append(pltpu.make_async_copy(near.at[n, f], out.at[f], done.at[2 * n + f]))
            copies[-1].start()
    for copy in copies:
        copy.wait()


RS = pltpu.VMEM((16, 32, 2 * LANES), jnp.float32)
LINES = pltpu.VMEM((512, LANES), jnp.float32)
BLOCKS_SENT, SENT, SPECTRUM = (1024, LANES), (512, LANES), (512, LANES)
ENDS, KEPT = (2, 16, LANES), (16, 32, LANES)


def call(kernel, outs, scratch, **more):
    return pl.pallas_call(
        kernel,
        out_shape=[jax.ShapeDtypeStruct(s, jnp.float32) for s in outs],
        scratch_shapes=scratch,
        compiler_params=pltpu.CompilerParams(vmem_limit_bytes=32 * 1024 * 1024),
        **more,
    )


def far(*arrays):
    return [pltpu.with_memory_space_constraint(a, pltpu.HBM) for a in arrays]


def exchange(flat, axes, *shape):
    moved = lax.all_to_all(flat.reshape(*shape, LANES), axes, 0, 0, tiled=True)
    return moved.reshape(flat.shape)


def per_device(sources, metric, helm):
    table, waves = (jnp.asarray(a) for a in tables())
    line, column = ("half", "pair", "core"), ("gy", "pair", "core")
    here = lax.axis_index("gy") * lax.axis_size("pair") + lax.axis_index("pair")
    here = jnp.full((1, LANES), here, jnp.float32)
    core = jnp.full((1, LANES), lax.axis_index("core"), jnp.float32)
    block = pltpu.VMEM(metric.shape, metric.dtype)
    hbm, vmem = pl.BlockSpec(memory_space=pl.ANY), pl.BlockSpec(memory_space=pltpu.VMEM)

    def swap(ends):
        return lax.ppermute(ends, "core", [(0, 1), (1, 0)])

    (sent,) = call(
        leave_block,
        [BLOCKS_SENT],
        [pltpu.VMEM(sources.shape, sources.dtype), block, block, pltpu.SemaphoreType.DMA((4,))],
        in_specs=[hbm] * 5 + [vmem] * 2,
    )(*far(sources, metric, helm, table, waves), here, core)
    blocks = exchange(sent, line, 8, 128)
    first, ends = call(pencil_first, [SPECTRUM, ENDS], [RS])(blocks, table, waves)
    sibling = swap(ends)
    (sent,) = call(leave_lines, [SENT], [])(ends, sibling, waves, here, core)
    received = exchange(sent, column, 64, 8)
    second, more, kept, sums = call(pencil_middle, [SPECTRUM, ENDS, KEPT, (2, 8, LANES)], [RS, LINES])(
        received, blocks, first, ends, sibling, table, waves, here, core
    )
    twin = swap(more)
    (sent,) = call(leave_lines, [SENT], [])(more, twin, waves, here, core)
    received = exchange(sent, column, 64, 8)
    (sent,) = call(pencil_last, [(8 * 130, LANES)], [RS, LINES])(
        received, blocks, second, more, twin, kept, sums, table, waves, here, core
    )
    received = exchange(sent, line, 8, 65, 2)
    (parts,) = call(gather_sums, [(LANES, LANES)], [])(received)
    parts = exchange(parts, "gy", 16, 8)
    outs = call(
        enter_block,
        [sources.shape] * 2,
        [pltpu.VMEM((2, *sources.shape), jnp.float32), pltpu.SemaphoreType.DMA((4,))],
        in_specs=[vmem] * 5,
        out_specs=[hbm] * 2,
    )(received, parts, sources, metric, helm)
    return tuple(outs)


def solution(mesh):
    devices = mesh.devices.reshape(2, 2, 2, 16)
    finer = jax.sharding.Mesh(devices, ("half", "pair", "core", "gy"))
    line = ("half", "pair", "core")
    in_specs = (P(None, line, "gy"), P(line, "gy"), P(line, "gy"))
    out_specs = (P(None, line, "gy"), P(None, line, "gy"))
    return jax.shard_map(
        per_device, mesh=finer, in_specs=in_specs, out_specs=out_specs, check_vma=False
    )
```

```python
import functools
import math

import jax
import jax.numpy as jnp
import ml_dtypes
import numpy as np
from jax import lax
from jax.experimental import pallas as pl
from jax.experimental.pallas import tpu as pltpu
from jax.sharding import PartitionSpec as P

SHIFT = 0.001
ROWS = 16
BLOCK = 32
BLOCKS = 32
LANES = 128
LENGTH = ROWS * LANES


def frequency():
    t = np.arange(16)[:, None]
    k2 = np.arange(64)[None, :]
    first = t + 32 * k2
    second = np.where(t == 0, 16, 32 - t) + 32 * k2
    return np.concatenate([first, second], axis=1)


def tables():
    freq = frequency()
    b = np.arange(LANES)
    phase = (freq[:, None, :] * (2 * b[None, :, None] + 1)) % (4 * LENGTH)
    angle = phase * (math.pi / (2 * LENGTH))
    scale = np.where(freq == 0, math.sqrt(1.0 / LENGTH), math.sqrt(2.0 / LENGTH))[:, None, :]
    even, odd = scale * np.cos(angle), scale * np.sin(angle)
    sign = np.where(np.arange(LANES) < 64, -1.0, 1.0)
    full = np.concatenate([even, odd * sign], axis=1)
    full[0, :LANES, 64:] = 0.0
    full[0, LANES:, :64] = 0.0
    full[0, LANES:, 64:] = even[0, :, 64:]
    high = full.astype(ml_dtypes.bfloat16)
    low = (full - high.astype(np.float64)).astype(ml_dtypes.bfloat16)
    forward = np.concatenate([high, low], axis=2)
    sigma = 4.0 * np.sin(math.pi * freq / (2 * LENGTH)) ** 2 + SHIFT
    mu = 2.0 * np.arcsinh(np.sqrt(sigma) / 2.0)
    waves = [np.exp(-mu), BLOCK * mu, 0.5 / np.sinh(mu), 1.0 / (1.0 - np.exp(-4.0 * BLOCK * BLOCKS * mu))]
    return np.stack([forward, np.swapaxes(forward, 1, 2)], axis=1), np.stack(waves).astype(np.float32)


def cos16(n):
    return float(math.cos(math.pi * n / 16))


def sin16(n):
    return float(math.sin(math.pi * n / 16))


def combine(terms):
    total = None
    for c, v in terms:
        if abs(c) < 1e-12:
            continue
        if abs(abs(c) - 1.0) < 1e-12:
            if total is None:
                total = v if c > 0 else -v
            else:
                total = total + v if c > 0 else total - v
        else:
            total = c * v if total is None else total + c * v
    return total


def first_stage(x):
    p = {a: x[a] + x[16 - a] for a in range(1, 8)}
    m = {a: x[a] - x[16 - a] for a in range(1, 8)}
    R, S = {}, {}
    for j in range(1, 8):
        c, s = (m, p) if j % 2 else (p, m)
        ev = combine([(1.0, x[0])] + [(cos16(j * a), c[a]) for a in (2, 4, 6)] + [(cos16(8 * j), x[8])])
        od = combine([(cos16(j * a), c[a]) for a in (1, 3, 5, 7)])
        R[j], R[16 - j] = ev + od, ev - od
        ev = combine([(sin16(j * a), s[a]) for a in (2, 4, 6)] + [(sin16(8 * j), x[8])])
        od = combine([(sin16(j * a), s[a]) for a in (1, 3, 5, 7)])
        S[j], S[16 - j] = od + ev, od - ev
    outer, inner = x[0] + x[8], p[2] + p[6]
    R[8] = outer + p[4] - inner
    S[8] = (m[1] + m[5]) - (m[3] + m[7])
    even, odd = outer + p[4] + inner, (p[1] + p[7]) + (p[3] + p[5])
    R[0], R[16] = even + odd, even - odd
    return R, S


def first_stage_transposed(R, S):
    rp = {j: R[j] + R[16 - j] for j in range(1, 8)}
    rm = {j: R[j] - R[16 - j] for j in range(1, 8)}
    sp = {j: S[j] + S[16 - j] for j in range(1, 8)}
    sm = {j: S[j] - S[16 - j] for j in range(1, 8)}
    ends, wide = R[0] + R[16], R[0] - R[16]
    x = {}
    for a in range(1, 8):
        r, s = (rm, sp) if a % 2 else (rp, sm)
        ce = combine([(1.0, wide if a % 2 else ends), (cos16(8 * a), R[8])] + [(cos16(j * a), r[j]) for j in (2, 4, 6)])
        co = combine([(cos16(j * a), r[j]) for j in (1, 3, 5, 7)])
        se = combine([(sin16(8 * a), S[8])] + [(sin16(j * a), s[j]) for j in (2, 4, 6)])
        so = combine([(sin16(j * a), s[j]) for j in (1, 3, 5, 7)])
        x[a], x[16 - a] = (ce + so) + (co + se), (ce + so) - (co + se)
    even = ends + R[8] + rp[2] + rp[4] + rp[6]
    x[0] = even + (rp[1] + rp[7]) + (rp[3] + rp[5])
    x[8] = ends + R[8] - rp[2] + rp[4] - rp[6] + (sm[1] - sm[3]) + (sm[5] - sm[7])
    return x


def split(value):
    high = value.astype(jnp.bfloat16)
    return high, (value - high.astype(jnp.float32)).astype(jnp.bfloat16)


def forward_dot(value, table, t):
    high, low = split(value)
    both = jnp.dot(jnp.concatenate([high, low], axis=0), table[t, 0, :, :LANES], preferred_element_type=jnp.float32)
    third = jnp.dot(high, table[t, 0, :, LANES:], preferred_element_type=jnp.float32)
    return both[:32] + (both[32:] + third)


def backward_dot(value, table, t):
    high, low = split(value)
    both = jnp.dot(jnp.concatenate([high, low], axis=0), table[t, 1, :LANES, :], preferred_element_type=jnp.float32)
    third = jnp.dot(high, table[t, 1, LANES:, :], preferred_element_type=jnp.float32)
    return both[:32] + (both[32:] + third)


def put_first(R, S, rs, chunk):
    rows = pl.ds(8 * chunk, 8)
    for t in range(16):
        rs[t, rows, 0:LANES] = R[t]
        rs[t, rows, LANES : 2 * LANES] = R[16] if t == 0 else S[t]


def get_first(rs, chunk):
    rows = pl.ds(8 * chunk, 8)
    R = {t: rs[t, rows, 0:LANES] for t in range(16)}
    S = {t: rs[t, rows, LANES : 2 * LANES] for t in range(1, 16)}
    R[16] = rs[0, rows, LANES : 2 * LANES]
    return R, S


def place_of(half, quarter):
    return 2 * quarter + half


def leave_block(sources, metric, helm, table, waves, here, core, sent, source_here, metric_here, helm_here, arrived):
    moves = [(metric, metric_here), (helm, helm_here), (sources, source_here)]
    copies = [pltpu.make_async_copy(a, b, arrived.at[n]) for n, (a, b) in enumerate(moves)]
    for copy in copies:
        copy.start()
    copies[0].wait()
    inverse = 1.0 / metric_here[...]
    copies[1].wait()
    weight = helm_here[...] * (inverse * inverse) - SHIFT
    for h in range(2):
        across = weight[LANES * h : LANES * (h + 1), :].T
        for quarter in range(4):
            for f in range(2):
                rows = pl.ds(LANES * place_of(f, quarter) + 64 + h, BLOCK, stride=2)
                sent[rows, :] = across[BLOCK * quarter : BLOCK * (quarter + 1)]
    copies[2].wait()
    for f in range(2):
        field = source_here[f] * inverse
        for h in range(2):
            across = field[LANES * h : LANES * (h + 1), :].T
            for quarter in range(4):
                rows = pl.ds(LANES * place_of(f, quarter) + h, BLOCK, stride=2)
                sent[rows, :] = across[BLOCK * quarter : BLOCK * (quarter + 1)]


def from_block(blocks, a, chunk, field):
    return blocks[pl.ds(LANES * place_of(a // 8, a // 2 % 4) + 64 * field + 16 * chunk + a % 2, 8, stride=2), :]


def lines(spectrum, y):
    return spectrum[pl.ds(16 * y, 16), :]


def forward_x(table, rs, spectrum):
    for t in range(16):
        spectrum[pl.ds(t, BLOCK, stride=16), :] = forward_dot(rs[t], table, t)


def backward_x(spectrum, table, rs):
    for t in range(16):
        rs[t] = backward_dot(spectrum[pl.ds(t, BLOCK, stride=16), :], table, t)


def local_sums(spectrum, waves, ends):
    rho = waves[0]
    p = lines(spectrum, 0)
    q = lines(spectrum, BLOCK - 1)
    for y in range(1, BLOCK):
        p = rho * p + lines(spectrum, y)
        q = rho * q + lines(spectrum, BLOCK - 1 - y)
    ends[0], ends[1] = p, q


def both_cores(ends, sibling, whole, upper):
    p = jnp.where(upper, ends[0] + whole * sibling[0], sibling[0] + whole * ends[0])
    q = jnp.where(upper, sibling[1] + whole * ends[1], ends[1] + whole * sibling[1])
    return p, q


def leave_lines(ends, sibling, waves, here, core, sent):
    decay = waves[1]
    upper = core[...] > 0
    p, q = both_cores(ends, sibling, jnp.exp(-decay), upper)
    b = here[...]
    above = p + jnp.exp(-decay * (4.0 * b + 2.0)) * q
    below = q + jnp.exp(-decay * (4.0 * (BLOCKS - 1.0 - b) + 2.0)) * p
    above = jnp.where(upper, above[8:], above[:8])
    below = jnp.where(upper, below[8:], below[:8])
    for n in range(BLOCKS):
        value = jnp.where(b < n, above, below)
        for twin in range(2):
            sent[pl.ds(16 * n + 8 * twin, 8), :] = value


def solve_lines(received, spectrum, waves, here, core, ends, sibling, solved):
    rho, decay, scale, rounds = waves[0], waves[1], waves[2], waves[3]
    whole, double = jnp.exp(-decay), jnp.exp(-2.0 * decay)
    b = here[...]
    middle = BLOCKS // 2
    low, high = [[jnp.zeros((16, LANES), jnp.float32)] * 2 for _ in range(2)]
    for n in range(middle):
        for part in range(2):
            k = n + middle * part
            low[part] = jnp.where(b > k, received[pl.ds(16 * k, 16), :] + double * low[part], low[part])
            m = BLOCKS - 1 - k
            high[part] = jnp.where(b < m, received[pl.ds(16 * m, 16), :] + double * high[part], high[part])
    low = low[1] + jnp.exp(-2.0 * decay * jnp.maximum(b - middle, 0.0)) * low[0]
    high = high[1] + jnp.exp(-2.0 * decay * jnp.maximum(middle - 1.0 - b, 0.0)) * high[0]
    upper = core[...] > 0
    p, q = both_cores(ends, sibling, whole, upper)
    left = jnp.exp(-decay * (4.0 * b))
    right = jnp.exp(-decay * (4.0 * (BLOCKS - 1.0 - b)))
    up = (low + left * (q + double * (high + right * p))) * rounds
    down = high + right * (p + double * up)
    up = jnp.where(upper, sibling[0] + whole * up, up)
    down = jnp.where(upper, down, sibling[1] + whole * down)
    for y in range(BLOCK):
        up = rho * up + lines(spectrum, y)
        solved[pl.ds(16 * y, 16), :] = up
    for y in range(BLOCK - 1, -1, -1):
        down = rho * down
        solved[pl.ds(16 * y, 16), :] = scale * (lines(solved, y) + down)
        down = down + lines(spectrum, y)


def pencil_first(blocks, table, waves, spectrum, ends, rs):
    for chunk in range(4):
        x = [from_block(blocks, a, chunk, 0) for a in range(16)]
        put_first(*first_stage(x), rs, chunk)
    forward_x(table, rs, spectrum)
    local_sums(spectrum, waves, ends)


def pencil_middle(
    received, blocks, old, old_ends, sibling, table, waves, here, core, spectrum, ends, kept, sums, rs, solved
):
    solve_lines(received, old, waves, here, core, old_ends, sibling, solved)
    backward_x(solved, table, rs)
    totals = [jnp.zeros((8, LANES), jnp.float32) for _ in range(2)]
    for chunk in range(4):
        x = first_stage_transposed(*get_first(rs, chunk))
        scaled = [x[a] * from_block(blocks, a, chunk, 1) for a in range(16)]
        for a in range(16):
            kept[a, pl.ds(8 * chunk, 8), :] = x[a]
            totals[0] += from_block(blocks, a, chunk, 0) * x[a]
            totals[1] += scaled[a] * x[a]
        put_first(*first_stage(scaled), rs, chunk)
    sums[0], sums[1] = totals
    forward_x(table, rs, spectrum)
    local_sums(spectrum, waves, ends)


def pencil_last(received, blocks, old, old_ends, sibling, kept, first, table, waves, here, core, sent, rs, solved):
    solve_lines(received, old, waves, here, core, old_ends, sibling, solved)
    backward_x(solved, table, rs)
    n0, n1 = (jnp.sum(first[n], axis=(0, 1), keepdims=True) for n in range(2))
    positive = n0 + n1 > 0.0
    step = jnp.where(positive, n0 / jnp.where(positive, n0 + n1, 1.0), 0.0)
    step = jnp.clip(step, 0.0, 2.0)
    sums = [jnp.zeros((8, LANES), jnp.float32) for _ in range(7)]
    for chunk in range(4):
        x = first_stage_transposed(*get_first(rs, chunk))
        for a in range(16):
            before, new = kept[a, pl.ds(8 * chunk, 8), :], x[a]
            weight, source = from_block(blocks, a, chunk, 1), from_block(blocks, a, chunk, 0)
            g, h = source + weight * before, before + new
            u1, z1 = source - step * g, before - step * h
            wz, wh = weight * z1, weight * h
            for q, (one, two) in enumerate(((u1, z1), (u1, h), (g, z1), (g, h), (wz, z1), (wz, h), (wh, h))):
                sums[q] += one * two
            place = 130 * place_of(a // 8, a // 2 % 4) + 16 * chunk + a % 2
            sent[pl.ds(place, 8, stride=2), :] = before
            sent[pl.ds(place + 64, 8, stride=2), :] = new
    lane = lax.broadcasted_iota(jnp.int32, (2, LANES), 1)
    line = jnp.where(lane == 7, n0, jnp.where(lane == 8, n1, jnp.where(lane >= 64, step, 0.0)))
    for q in range(7):
        line = jnp.where(lane == q, jnp.sum(sums[q], axis=(0, 1), keepdims=True), line)
    for i in range(8):
        sent[pl.ds(130 * i + 128, 2), :] = line


def gather_sums(received, sent):
    rows = received[pl.ds(128, 8, stride=130), :]
    for n in range(16):
        sent[pl.ds(8 * n, 8), :] = rows


def enter_block(received, parts, sources, metric, helm, solution, resid, near, done):
    copies = []
    lane = lax.broadcasted_iota(jnp.int32, (1, LANES), 1)
    row = lax.broadcasted_iota(jnp.int32, (LANES, LANES), 0)
    every = parts[...]
    steps = pltpu.roll(every, 64, 1)

    def pick(line, q):
        return jnp.sum(jnp.where(lane == q, line, 0.0), axis=1, keepdims=True)

    m = metric[...]
    inverse = 1.0 / m
    weight = helm[...] * inverse - SHIFT * m
    for f in range(2):
        mine = jnp.where(row % 2 == f, every, 0.0)
        zeroth = jnp.sum(mine, axis=0, keepdims=True)
        n0, n1 = pick(zeroth, 7), pick(zeroth, 8)
        delta = n0 + n1
        alpha, rest = n0 / delta, n1 / delta
        away = alpha - steps
        moved = away * mine
        first = jnp.sum(moved, axis=0, keepdims=True)
        second = jnp.sum(away * moved, axis=0, keepdims=True)
        gamma = pick(zeroth, 0) - (pick(first, 1) + pick(first, 2)) + pick(second, 3)
        inner = pick(zeroth, 4) - 2.0 * pick(first, 5) + pick(second, 6)
        cross = pick(zeroth, 2) - pick(first, 3)
        beta = gamma / n0
        size = gamma / (gamma + inner + 2.0 * beta * cross + beta * beta * delta)
        c0, c1 = alpha + size * (rest + beta), -size * alpha
        for h in range(2):
            pair = []
            for field in range(2):
                places = [130 * place_of(f, quarter) + 64 * field + h for quarter in range(4)]
                columns = [received[pl.ds(place, BLOCK, stride=2), :] for place in places]
                pair.append(jnp.concatenate(columns, axis=0).T)
            old, new = pair
            rows = slice(LANES * h, LANES * (h + 1))
            near[0, f, rows, :] = (c0 * old + c1 * new) * inverse[rows]
            near[1, f, rows, :] = (1.0 - c0) * sources[f, rows, :] - ((c0 + c1) * old + c1 * new) * weight[rows]
        for n, out in enumerate((solution, resid)):
            copies.append(pltpu.make_async_copy(near.at[n, f], out.at[f], done.at[2 * n + f]))
            copies[-1].start()
    for copy in copies:
        copy.wait()


RS = pltpu.VMEM((16, 32, 2 * LANES), jnp.float32)
LINES = pltpu.VMEM((512, LANES), jnp.float32)
BLOCKS_SENT, SENT, SPECTRUM = (1024, LANES), (512, LANES), (512, LANES)
ENDS, KEPT = (2, 16, LANES), (16, 32, LANES)


def call(kernel, outs, scratch, **more):
    return pl.pallas_call(
        kernel,
        out_shape=[jax.ShapeDtypeStruct(s, jnp.float32) for s in outs],
        scratch_shapes=scratch,
        compiler_params=pltpu.CompilerParams(vmem_limit_bytes=32 * 1024 * 1024),
        **more,
    )


def far(*arrays):
    return [pltpu.with_memory_space_constraint(a, pltpu.HBM) for a in arrays]


def exchange(flat, axes, *shape):
    moved = lax.all_to_all(flat.reshape(*shape, LANES), axes, 0, 0, tiled=True)
    return moved.reshape(flat.shape)


def per_device(sources, metric, helm):
    table, waves = (jnp.asarray(a) for a in tables())
    line, column = ("pair", "core", "half"), ("gy", "pair", "core")
    here = lax.axis_index("gy") * lax.axis_size("pair") + lax.axis_index("pair")
    here = jnp.full((1, LANES), here, jnp.float32)
    core = jnp.full((1, LANES), lax.axis_index("core"), jnp.float32)
    block = pltpu.VMEM(metric.shape, metric.dtype)
    hbm, vmem = pl.BlockSpec(memory_space=pl.ANY), pl.BlockSpec(memory_space=pltpu.VMEM)

    def swap(ends):
        return lax.ppermute(ends, "core", [(0, 1), (1, 0)])

    (sent,) = call(
        leave_block,
        [BLOCKS_SENT],
        [pltpu.VMEM(sources.shape, sources.dtype), block, block, pltpu.SemaphoreType.DMA((4,))],
        in_specs=[hbm] * 5 + [vmem] * 2,
    )(*far(sources, metric, helm, table, waves), here, core)
    blocks = exchange(sent, line, 8, 128)
    first, ends = call(pencil_first, [SPECTRUM, ENDS], [RS])(blocks, table, waves)
    sibling = swap(ends)
    (sent,) = call(leave_lines, [SENT], [])(ends, sibling, waves, here, core)
    received = exchange(sent, column, 64, 8)
    second, more, kept, sums = call(pencil_middle, [SPECTRUM, ENDS, KEPT, (2, 8, LANES)], [RS, LINES])(
        received, blocks, first, ends, sibling, table, waves, here, core
    )
    twin = swap(more)
    (sent,) = call(leave_lines, [SENT], [])(more, twin, waves, here, core)
    received = exchange(sent, column, 64, 8)
    (sent,) = call(pencil_last, [(8 * 130, LANES)], [RS, LINES])(
        received, blocks, second, more, twin, kept, sums, table, waves, here, core
    )
    received = exchange(sent, line, 8, 65, 2)
    (parts,) = call(gather_sums, [(LANES, LANES)], [])(received)
    parts = exchange(parts, "gy", 16, 8)
    outs = call(
        enter_block,
        [sources.shape] * 2,
        [pltpu.VMEM((2, *sources.shape), jnp.float32), pltpu.SemaphoreType.DMA((4,))],
        in_specs=[vmem] * 5,
        out_specs=[hbm] * 2,
    )(received, parts, sources, metric, helm)
    return tuple(outs)


def solution(mesh):
    devices = mesh.devices.reshape(2, 2, 2, 16)
    finer = jax.sharding.Mesh(devices, ("half", "pair", "core", "gy"))
    line = ("half", "pair", "core")
    in_specs = (P(None, line, "gy"), P(line, "gy"), P(line, "gy"))
    out_specs = (P(None, line, "gy"), P(None, line, "gy"))
    return jax.shard_map(
        per_device, mesh=finer, in_specs=in_specs, out_specs=out_specs, check_vma=False
    )
```

```python
import functools
import math

import jax
import jax.numpy as jnp
import ml_dtypes
import numpy as np
from jax import lax
from jax.experimental import pallas as pl
from jax.experimental.pallas import tpu as pltpu
from jax.sharding import PartitionSpec as P

SHIFT = 0.001
ROWS = 16
BLOCK = 32
BLOCKS = 32
LANES = 128
LENGTH = ROWS * LANES


def frequency():
    t = np.arange(16)[:, None]
    k2 = np.arange(64)[None, :]
    first = t + 32 * k2
    second = np.where(t == 0, 16, 32 - t) + 32 * k2
    return np.concatenate([first, second], axis=1)


def tables():
    freq = frequency()
    b = np.arange(LANES)
    phase = (freq[:, None, :] * (2 * b[None, :, None] + 1)) % (4 * LENGTH)
    angle = phase * (math.pi / (2 * LENGTH))
    scale = np.where(freq == 0, math.sqrt(1.0 / LENGTH), math.sqrt(2.0 / LENGTH))[:, None, :]
    even, odd = scale * np.cos(angle), scale * np.sin(angle)
    sign = np.where(np.arange(LANES) < 64, -1.0, 1.0)
    full = np.concatenate([even, odd * sign], axis=1)
    full[0, :LANES, 64:] = 0.0
    full[0, LANES:, :64] = 0.0
    full[0, LANES:, 64:] = even[0, :, 64:]
    high = full.astype(ml_dtypes.bfloat16)
    low = (full - high.astype(np.float64)).astype(ml_dtypes.bfloat16)
    forward = np.concatenate([high, low], axis=2)
    sigma = 4.0 * np.sin(math.pi * freq / (2 * LENGTH)) ** 2 + SHIFT
    mu = 2.0 * np.arcsinh(np.sqrt(sigma) / 2.0)
    waves = [np.exp(-mu), BLOCK * mu, 0.5 / np.sinh(mu), 1.0 / (1.0 - np.exp(-4.0 * BLOCK * BLOCKS * mu))]
    return np.stack([forward, np.swapaxes(forward, 1, 2)], axis=1), np.stack(waves).astype(np.float32)


def cos16(n):
    return float(math.cos(math.pi * n / 16))


def sin16(n):
    return float(math.sin(math.pi * n / 16))


def combine(terms):
    total = None
    for c, v in terms:
        if abs(c) < 1e-12:
            continue
        if abs(abs(c) - 1.0) < 1e-12:
            if total is None:
                total = v if c > 0 else -v
            else:
                total = total + v if c > 0 else total - v
        else:
            total = c * v if total is None else total + c * v
    return total


def first_stage(x):
    p = {a: x[a] + x[16 - a] for a in range(1, 8)}
    m = {a: x[a] - x[16 - a] for a in range(1, 8)}
    R, S = {}, {}
    for j in range(1, 8):
        c, s = (m, p) if j % 2 else (p, m)
        ev = combine([(1.0, x[0])] + [(cos16(j * a), c[a]) for a in (2, 4, 6)] + [(cos16(8 * j), x[8])])
        od = combine([(cos16(j * a), c[a]) for a in (1, 3, 5, 7)])
        R[j], R[16 - j] = ev + od, ev - od
        ev = combine([(sin16(j * a), s[a]) for a in (2, 4, 6)] + [(sin16(8 * j), x[8])])
        od = combine([(sin16(j * a), s[a]) for a in (1, 3, 5, 7)])
        S[j], S[16 - j] = od + ev, od - ev
    outer, inner = x[0] + x[8], p[2] + p[6]
    R[8] = outer + p[4] - inner
    S[8] = (m[1] + m[5]) - (m[3] + m[7])
    even, odd = outer + p[4] + inner, (p[1] + p[7]) + (p[3] + p[5])
    R[0], R[16] = even + odd, even - odd
    return R, S


def first_stage_transposed(R, S):
    rp = {j: R[j] + R[16 - j] for j in range(1, 8)}
    rm = {j: R[j] - R[16 - j] for j in range(1, 8)}
    sp = {j: S[j] + S[16 - j] for j in range(1, 8)}
    sm = {j: S[j] - S[16 - j] for j in range(1, 8)}
    ends, wide = R[0] + R[16], R[0] - R[16]
    x = {}
    for a in range(1, 8):
        r, s = (rm, sp) if a % 2 else (rp, sm)
        ce = combine([(1.0, wide if a % 2 else ends), (cos16(8 * a), R[8])] + [(cos16(j * a), r[j]) for j in (2, 4, 6)])
        co = combine([(cos16(j * a), r[j]) for j in (1, 3, 5, 7)])
        se = combine([(sin16(8 * a), S[8])] + [(sin16(j * a), s[j]) for j in (2, 4, 6)])
        so = combine([(sin16(j * a), s[j]) for j in (1, 3, 5, 7)])
        x[a], x[16 - a] = (ce + so) + (co + se), (ce + so) - (co + se)
    even = ends + R[8] + rp[2] + rp[4] + rp[6]
    x[0] = even + (rp[1] + rp[7]) + (rp[3] + rp[5])
    x[8] = ends + R[8] - rp[2] + rp[4] - rp[6] + (sm[1] - sm[3]) + (sm[5] - sm[7])
    return x


def split(value):
    high = value.astype(jnp.bfloat16)
    return high, (value - high.astype(jnp.float32)).astype(jnp.bfloat16)


def forward_dot(value, table, t):
    high, low = split(value)
    both = jnp.dot(jnp.concatenate([high, low], axis=0), table[t, 0, :, :LANES], preferred_element_type=jnp.float32)
    third = jnp.dot(high, table[t, 0, :, LANES:], preferred_element_type=jnp.float32)
    return both[:32] + (both[32:] + third)


def backward_dot(value, table, t):
    high, low = split(value)
    both = jnp.dot(jnp.concatenate([high, low], axis=0), table[t, 1, :LANES, :], preferred_element_type=jnp.float32)
    third = jnp.dot(high, table[t, 1, LANES:, :], preferred_element_type=jnp.float32)
    return both[:32] + (both[32:] + third)


def put_first(R, S, rs, chunk):
    rows = pl.ds(8 * chunk, 8)
    for t in range(16):
        rs[t, rows, 0:LANES] = R[t]
        rs[t, rows, LANES : 2 * LANES] = R[16] if t == 0 else S[t]


def get_first(rs, chunk):
    rows = pl.ds(8 * chunk, 8)
    R = {t: rs[t, rows, 0:LANES] for t in range(16)}
    S = {t: rs[t, rows, LANES : 2 * LANES] for t in range(1, 16)}
    R[16] = rs[0, rows, LANES : 2 * LANES]
    return R, S


def place_of(half, quarter):
    return 2 * quarter + half


def leave_block(sources, metric, helm, table, waves, here, core, sent, source_here, metric_here, helm_here, arrived):
    moves = [(metric, metric_here), (helm, helm_here), (sources, source_here)]
    copies = [pltpu.make_async_copy(a, b, arrived.at[n]) for n, (a, b) in enumerate(moves)]
    for copy in copies:
        copy.start()
    copies[0].wait()
    inverse = 1.0 / metric_here[...]
    copies[1].wait()
    weight = helm_here[...] * (inverse * inverse) - SHIFT
    for h in range(2):
        across = weight[LANES * h : LANES * (h + 1), :].T
        for quarter in range(4):
            for f in range(2):
                rows = pl.ds(LANES * place_of(f, quarter) + 64 + h, BLOCK, stride=2)
                sent[rows, :] = across[BLOCK * quarter : BLOCK * (quarter + 1)]
    copies[2].wait()
    for f in range(2):
        field = source_here[f] * inverse
        for h in range(2):
            across = field[LANES * h : LANES * (h + 1), :].T
            for quarter in range(4):
                rows = pl.ds(LANES * place_of(f, quarter) + h, BLOCK, stride=2)
                sent[rows, :] = across[BLOCK * quarter : BLOCK * (quarter + 1)]


def from_block(blocks, a, chunk, field):
    return blocks[pl.ds(LANES * place_of(a // 8, a // 2 % 4) + 64 * field + 16 * chunk + a % 2, 8, stride=2), :]


def lines(spectrum, y):
    return spectrum[pl.ds(16 * y, 16), :]


def forward_x(table, rs, spectrum):
    for t in range(16):
        spectrum[pl.ds(t, BLOCK, stride=16), :] = forward_dot(rs[t], table, t)


def backward_x(spectrum, table, rs):
    for t in range(16):
        rs[t] = backward_dot(spectrum[pl.ds(t, BLOCK, stride=16), :], table, t)


def local_sums(spectrum, waves, ends):
    rho = waves[0]
    p = lines(spectrum, 0)
    q = lines(spectrum, BLOCK - 1)
    for y in range(1, BLOCK):
        p = rho * p + lines(spectrum, y)
        q = rho * q + lines(spectrum, BLOCK - 1 - y)
    ends[0], ends[1] = p, q


def both_cores(ends, sibling, whole, upper):
    p = jnp.where(upper, ends[0] + whole * sibling[0], sibling[0] + whole * ends[0])
    q = jnp.where(upper, sibling[1] + whole * ends[1], ends[1] + whole * sibling[1])
    return p, q


def leave_lines(ends, sibling, waves, here, core, sent):
    decay = waves[1]
    upper = core[...] > 0
    p, q = both_cores(ends, sibling, jnp.exp(-decay), upper)
    b = here[...]
    above = p + jnp.exp(-decay * (4.0 * b + 2.0)) * q
    below = q + jnp.exp(-decay * (4.0 * (BLOCKS - 1.0 - b) + 2.0)) * p
    above = jnp.where(upper, above[8:], above[:8])
    below = jnp.where(upper, below[8:], below[:8])
    for n in range(BLOCKS):
        value = jnp.where(b < n, above, below)
        for twin in range(2):
            sent[pl.ds(16 * n + 8 * twin, 8), :] = value


def solve_lines(received, spectrum, waves, here, core, ends, sibling, solved):
    rho, decay, scale, rounds = waves[0], waves[1], waves[2], waves[3]
    whole, double = jnp.exp(-decay), jnp.exp(-2.0 * decay)
    b = here[...]
    middle = BLOCKS // 2
    low, high = [[jnp.zeros((16, LANES), jnp.float32)] * 2 for _ in range(2)]
    for n in range(middle):
        for part in range(2):
            k = n + middle * part
            low[part] = jnp.where(b > k, received[pl.ds(16 * k, 16), :] + double * low[part], low[part])
            m = BLOCKS - 1 - k
            high[part] = jnp.where(b < m, received[pl.ds(16 * m, 16), :] + double * high[part], high[part])
    low = low[1] + jnp.exp(-2.0 * decay * jnp.maximum(b - middle, 0.0)) * low[0]
    high = high[1] + jnp.exp(-2.0 * decay * jnp.maximum(middle - 1.0 - b, 0.0)) * high[0]
    upper = core[...] > 0
    p, q = both_cores(ends, sibling, whole, upper)
    left = jnp.exp(-decay * (4.0 * b))
    right = jnp.exp(-decay * (4.0 * (BLOCKS - 1.0 - b)))
    up = (low + left * (q + double * (high + right * p))) * rounds
    down = high + right * (p + double * up)
    up = jnp.where(upper, sibling[0] + whole * up, up)
    down = jnp.where(upper, down, sibling[1] + whole * down)
    for y in range(BLOCK):
        up = rho * up + lines(spectrum, y)
        solved[pl.ds(16 * y, 16), :] = up
    for y in range(BLOCK - 1, -1, -1):
        down = rho * down
        solved[pl.ds(16 * y, 16), :] = scale * (lines(solved, y) + down)
        down = down + lines(spectrum, y)


def pencil_first(blocks, table, waves, spectrum, ends, rs):
    for chunk in range(4):
        x = [from_block(blocks, a, chunk, 0) for a in range(16)]
        put_first(*first_stage(x), rs, chunk)
    forward_x(table, rs, spectrum)
    local_sums(spectrum, waves, ends)


def pencil_middle(
    received, blocks, old, old_ends, sibling, table, waves, here, core, spectrum, ends, kept, sums, rs, solved
):
    solve_lines(received, old, waves, here, core, old_ends, sibling, solved)
    backward_x(solved, table, rs)
    totals = [jnp.zeros((8, LANES), jnp.float32) for _ in range(2)]
    for chunk in range(4):
        x = first_stage_transposed(*get_first(rs, chunk))
        scaled = [x[a] * from_block(blocks, a, chunk, 1) for a in range(16)]
        for a in range(16):
            kept[a, pl.ds(8 * chunk, 8), :] = x[a]
            totals[0] += from_block(blocks, a, chunk, 0) * x[a]
            totals[1] += scaled[a] * x[a]
        put_first(*first_stage(scaled), rs, chunk)
    sums[0], sums[1] = totals
    forward_x(table, rs, spectrum)
    local_sums(spectrum, waves, ends)


def pencil_last(received, blocks, old, old_ends, sibling, kept, first, table, waves, here, core, sent, rs, solved):
    solve_lines(received, old, waves, here, core, old_ends, sibling, solved)
    backward_x(solved, table, rs)
    n0, n1 = (jnp.sum(first[n], axis=(0, 1), keepdims=True) for n in range(2))
    positive = n0 + n1 > 0.0
    step = jnp.where(positive, n0 / jnp.where(positive, n0 + n1, 1.0), 0.0)
    step = jnp.clip(step, 0.0, 2.0)
    sums = [jnp.zeros((8, LANES), jnp.float32) for _ in range(7)]
    for chunk in range(4):
        x = first_stage_transposed(*get_first(rs, chunk))
        for a in range(16):
            before, new = kept[a, pl.ds(8 * chunk, 8), :], x[a]
            weight, source = from_block(blocks, a, chunk, 1), from_block(blocks, a, chunk, 0)
            g, h = source + weight * before, before + new
            u1, z1 = source - step * g, before - step * h
            wz, wh = weight * z1, weight * h
            for q, (one, two) in enumerate(((u1, z1), (u1, h), (g, z1), (g, h), (wz, z1), (wz, h), (wh, h))):
                sums[q] += one * two
            place = 130 * place_of(a // 8, a // 2 % 4) + 16 * chunk + a % 2
            sent[pl.ds(place, 8, stride=2), :] = before
            sent[pl.ds(place + 64, 8, stride=2), :] = new
    lane = lax.broadcasted_iota(jnp.int32, (2, LANES), 1)
    line = jnp.where(lane == 7, n0, jnp.where(lane == 8, n1, jnp.where(lane >= 64, step, 0.0)))
    for q in range(7):
        line = jnp.where(lane == q, jnp.sum(sums[q], axis=(0, 1), keepdims=True), line)
    for i in range(8):
        sent[pl.ds(130 * i + 128, 2), :] = line


def gather_sums(received, sent):
    rows = received[pl.ds(128, 8, stride=130), :]
    for n in range(16):
        sent[pl.ds(8 * n, 8), :] = rows


def enter_block(received, parts, sources, metric, helm, solution, resid, near, done):
    copies = []
    lane = lax.broadcasted_iota(jnp.int32, (1, LANES), 1)
    row = lax.broadcasted_iota(jnp.int32, (LANES, LANES), 0)
    every = parts[...]
    steps = pltpu.roll(every, 64, 1)

    def total(line):
        return jnp.sum(line, axis=1, keepdims=True)

    def pick(line, q):
        return total(jnp.where(lane == q, line, 0.0))

    m = metric[...]
    inverse = 1.0 / m
    weight = helm[...] * inverse - SHIFT * m
    for f in range(2):
        mine = jnp.where(row % 2 == f, every, 0.0)
        zeroth = jnp.sum(mine, axis=0, keepdims=True)
        n0, n1 = pick(zeroth, 7), pick(zeroth, 8)
        delta = n0 + n1
        alpha, rest = n0 / delta, n1 / delta
        away = alpha - steps
        moved = away * mine
        first = jnp.sum(moved, axis=0, keepdims=True)
        second = jnp.sum(away * moved, axis=0, keepdims=True)
        once = (lane == 1) | (lane == 2)
        gamma = total(jnp.where(lane == 0, zeroth, jnp.where(once, -first, jnp.where(lane == 3, second, 0.0))))
        inner = total(jnp.where(lane == 4, zeroth, jnp.where(lane == 5, -2.0 * first, jnp.where(lane == 6, second, 0.0))))
        cross = total(jnp.where(lane == 2, zeroth, jnp.where(lane == 3, -first, 0.0)))
        beta = gamma / n0
        size = gamma / (gamma + inner + 2.0 * beta * cross + beta * beta * delta)
        c0, c1 = alpha + size * (rest + beta), -size * alpha
        for h in range(2):
            pair = []
            for field in range(2):
                places = [130 * place_of(f, quarter) + 64 * field + h for quarter in range(4)]
                columns = [received[pl.ds(place, BLOCK, stride=2), :] for place in places]
                pair.append(jnp.concatenate(columns, axis=0).T)
            old, new = pair
            rows = slice(LANES * h, LANES * (h + 1))
            near[0, f, rows, :] = (c0 * old + c1 * new) * inverse[rows]
            near[1, f, rows, :] = (1.0 - c0) * sources[f, rows, :] - ((c0 + c1) * old + c1 * new) * weight[rows]
        for n, out in enumerate((solution, resid)):
            copies.append(pltpu.make_async_copy(near.at[n, f], out.at[f], done.at[2 * n + f]))
            copies[-1].start()
    for copy in copies:
        copy.wait()


RS = pltpu.VMEM((16, 32, 2 * LANES), jnp.float32)
LINES = pltpu.VMEM((512, LANES), jnp.float32)
BLOCKS_SENT, SENT, SPECTRUM = (1024, LANES), (512, LANES), (512, LANES)
ENDS, KEPT = (2, 16, LANES), (16, 32, LANES)


def call(kernel, outs, scratch, **more):
    return pl.pallas_call(
        kernel,
        out_shape=[jax.ShapeDtypeStruct(s, jnp.float32) for s in outs],
        scratch_shapes=scratch,
        compiler_params=pltpu.CompilerParams(vmem_limit_bytes=32 * 1024 * 1024),
        **more,
    )


def far(*arrays):
    return [pltpu.with_memory_space_constraint(a, pltpu.HBM) for a in arrays]


def exchange(flat, axes, *shape):
    moved = lax.all_to_all(flat.reshape(*shape, LANES), axes, 0, 0, tiled=True)
    return moved.reshape(flat.shape)


def per_device(sources, metric, helm):
    table, waves = (jnp.asarray(a) for a in tables())
    line, column = ("pair", "core", "half"), ("gy", "pair", "core")
    here = lax.axis_index("gy") * lax.axis_size("pair") + lax.axis_index("pair")
    here = jnp.full((1, LANES), here, jnp.float32)
    core = jnp.full((1, LANES), lax.axis_index("core"), jnp.float32)
    block = pltpu.VMEM(metric.shape, metric.dtype)
    hbm, vmem = pl.BlockSpec(memory_space=pl.ANY), pl.BlockSpec(memory_space=pltpu.VMEM)

    def swap(ends):
        return lax.ppermute(ends, "core", [(0, 1), (1, 0)])

    (sent,) = call(
        leave_block,
        [BLOCKS_SENT],
        [pltpu.VMEM(sources.shape, sources.dtype), block, block, pltpu.SemaphoreType.DMA((4,))],
        in_specs=[hbm] * 5 + [vmem] * 2,
    )(*far(sources, metric, helm, table, waves), here, core)
    blocks = exchange(sent, line, 8, 128)
    first, ends = call(pencil_first, [SPECTRUM, ENDS], [RS])(blocks, table, waves)
    sibling = swap(ends)
    (sent,) = call(leave_lines, [SENT], [])(ends, sibling, waves, here, core)
    received = exchange(sent, column, 64, 8)
    second, more, kept, sums = call(pencil_middle, [SPECTRUM, ENDS, KEPT, (2, 8, LANES)], [RS, LINES])(
        received, blocks, first, ends, sibling, table, waves, here, core
    )
    twin = swap(more)
    (sent,) = call(leave_lines, [SENT], [])(more, twin, waves, here, core)
    received = exchange(sent, column, 64, 8)
    (sent,) = call(pencil_last, [(8 * 130, LANES)], [RS, LINES])(
        received, blocks, second, more, twin, kept, sums, table, waves, here, core
    )
    received = exchange(sent, line, 8, 65, 2)
    (parts,) = call(gather_sums, [(LANES, LANES)], [])(received)
    parts = exchange(parts, "gy", 16, 8)
    outs = call(
        enter_block,
        [sources.shape] * 2,
        [pltpu.VMEM((2, *sources.shape), jnp.float32), pltpu.SemaphoreType.DMA((4,))],
        in_specs=[vmem] * 5,
        out_specs=[hbm] * 2,
    )(received, parts, sources, metric, helm)
    return tuple(outs)


def solution(mesh):
    devices = mesh.devices.reshape(2, 2, 2, 16)
    finer = jax.sharding.Mesh(devices, ("half", "pair", "core", "gy"))
    line = ("half", "pair", "core")
    in_specs = (P(None, line, "gy"), P(line, "gy"), P(line, "gy"))
    out_specs = (P(None, line, "gy"), P(None, line, "gy"))
    return jax.shard_map(
        per_device, mesh=finer, in_specs=in_specs, out_specs=out_specs, check_vma=False
    )
```

```python
import functools
import math

import jax
import jax.numpy as jnp
import ml_dtypes
import numpy as np
from jax import lax
from jax.experimental import pallas as pl
from jax.experimental.pallas import tpu as pltpu
from jax.sharding import PartitionSpec as P

SHIFT = 0.001
ROWS = 16
BLOCK = 32
BLOCKS = 32
LANES = 128
LENGTH = ROWS * LANES


def frequency():
    t = np.arange(16)[:, None]
    k2 = np.arange(64)[None, :]
    first = t + 32 * k2
    second = np.where(t == 0, 16, 32 - t) + 32 * k2
    return np.concatenate([first, second], axis=1)


def tables():
    freq = frequency()
    b = np.arange(LANES)
    phase = (freq[:, None, :] * (2 * b[None, :, None] + 1)) % (4 * LENGTH)
    angle = phase * (math.pi / (2 * LENGTH))
    scale = np.where(freq == 0, math.sqrt(1.0 / LENGTH), math.sqrt(2.0 / LENGTH))[:, None, :]
    even, odd = scale * np.cos(angle), scale * np.sin(angle)
    sign = np.where(np.arange(LANES) < 64, -1.0, 1.0)
    full = np.concatenate([even, odd * sign], axis=1)
    full[0, :LANES, 64:] = 0.0
    full[0, LANES:, :64] = 0.0
    full[0, LANES:, 64:] = even[0, :, 64:]
    high = full.astype(ml_dtypes.bfloat16)
    low = (full - high.astype(np.float64)).astype(ml_dtypes.bfloat16)
    forward = np.concatenate([high, low], axis=2)
    sigma = 4.0 * np.sin(math.pi * freq / (2 * LENGTH)) ** 2 + SHIFT
    mu = 2.0 * np.arcsinh(np.sqrt(sigma) / 2.0)
    waves = [np.exp(-mu), BLOCK * mu, 0.5 / np.sinh(mu), 1.0 / (1.0 - np.exp(-4.0 * BLOCK * BLOCKS * mu))]
    return np.stack([forward, np.swapaxes(forward, 1, 2)], axis=1), np.stack(waves).astype(np.float32)


def cos16(n):
    return float(math.cos(math.pi * n / 16))


def sin16(n):
    return float(math.sin(math.pi * n / 16))


def combine(terms):
    total = None
    for c, v in terms:
        if abs(c) < 1e-12:
            continue
        if abs(abs(c) - 1.0) < 1e-12:
            if total is None:
                total = v if c > 0 else -v
            else:
                total = total + v if c > 0 else total - v
        else:
            total = c * v if total is None else total + c * v
    return total


def first_stage(x):
    p = {a: x[a] + x[16 - a] for a in range(1, 8)}
    m = {a: x[a] - x[16 - a] for a in range(1, 8)}
    R, S = {}, {}
    for j in range(1, 8):
        c, s = (m, p) if j % 2 else (p, m)
        ev = combine([(1.0, x[0])] + [(cos16(j * a), c[a]) for a in (2, 4, 6)] + [(cos16(8 * j), x[8])])
        od = combine([(cos16(j * a), c[a]) for a in (1, 3, 5, 7)])
        R[j], R[16 - j] = ev + od, ev - od
        ev = combine([(sin16(j * a), s[a]) for a in (2, 4, 6)] + [(sin16(8 * j), x[8])])
        od = combine([(sin16(j * a), s[a]) for a in (1, 3, 5, 7)])
        S[j], S[16 - j] = od + ev, od - ev
    outer, inner = x[0] + x[8], p[2] + p[6]
    R[8] = outer + p[4] - inner
    S[8] = (m[1] + m[5]) - (m[3] + m[7])
    even, odd = outer + p[4] + inner, (p[1] + p[7]) + (p[3] + p[5])
    R[0], R[16] = even + odd, even - odd
    return R, S


def first_stage_transposed(R, S):
    rp = {j: R[j] + R[16 - j] for j in range(1, 8)}
    rm = {j: R[j] - R[16 - j] for j in range(1, 8)}
    sp = {j: S[j] + S[16 - j] for j in range(1, 8)}
    sm = {j: S[j] - S[16 - j] for j in range(1, 8)}
    ends, wide = R[0] + R[16], R[0] - R[16]
    x = {}
    for a in range(1, 8):
        r, s = (rm, sp) if a % 2 else (rp, sm)
        ce = combine([(1.0, wide if a % 2 else ends), (cos16(8 * a), R[8])] + [(cos16(j * a), r[j]) for j in (2, 4, 6)])
        co = combine([(cos16(j * a), r[j]) for j in (1, 3, 5, 7)])
        se = combine([(sin16(8 * a), S[8])] + [(sin16(j * a), s[j]) for j in (2, 4, 6)])
        so = combine([(sin16(j * a), s[j]) for j in (1, 3, 5, 7)])
        x[a], x[16 - a] = (ce + so) + (co + se), (ce + so) - (co + se)
    even = ends + R[8] + rp[2] + rp[4] + rp[6]
    x[0] = even + (rp[1] + rp[7]) + (rp[3] + rp[5])
    x[8] = ends + R[8] - rp[2] + rp[4] - rp[6] + (sm[1] - sm[3]) + (sm[5] - sm[7])
    return x


def split(value):
    high = value.astype(jnp.bfloat16)
    return high, (value - high.astype(jnp.float32)).astype(jnp.bfloat16)


def forward_dot(value, table, t):
    high, low = split(value)
    both = jnp.dot(jnp.concatenate([high, low], axis=0), table[t, 0, :, :LANES], preferred_element_type=jnp.float32)
    third = jnp.dot(high, table[t, 0, :, LANES:], preferred_element_type=jnp.float32)
    return both[:32] + (both[32:] + third)


def backward_dot(value, table, t):
    high, low = split(value)
    both = jnp.dot(jnp.concatenate([high, low], axis=0), table[t, 1, :LANES, :], preferred_element_type=jnp.float32)
    third = jnp.dot(high, table[t, 1, LANES:, :], preferred_element_type=jnp.float32)
    return both[:32] + (both[32:] + third)


def put_first(R, S, rs, chunk):
    rows = pl.ds(8 * chunk, 8)
    for t in range(16):
        rs[t, rows, 0:LANES] = R[t]
        rs[t, rows, LANES : 2 * LANES] = R[16] if t == 0 else S[t]


def get_first(rs, chunk):
    rows = pl.ds(8 * chunk, 8)
    R = {t: rs[t, rows, 0:LANES] for t in range(16)}
    S = {t: rs[t, rows, LANES : 2 * LANES] for t in range(1, 16)}
    R[16] = rs[0, rows, LANES : 2 * LANES]
    return R, S


def place_of(half, quarter):
    return 2 * quarter + half


def leave_block(sources, metric, helm, table, waves, here, core, sent, source_here, metric_here, helm_here, arrived):
    moves = [(metric, metric_here), (helm, helm_here), (sources, source_here)]
    copies = [pltpu.make_async_copy(a, b, arrived.at[n]) for n, (a, b) in enumerate(moves)]
    for copy in copies:
        copy.start()
    copies[0].wait()
    inverse = 1.0 / metric_here[...]
    copies[1].wait()
    weight = helm_here[...] * (inverse * inverse) - SHIFT
    for h in range(2):
        across = weight[LANES * h : LANES * (h + 1), :].T
        for quarter in range(4):
            for f in range(2):
                rows = pl.ds(LANES * place_of(f, quarter) + 64 + h, BLOCK, stride=2)
                sent[rows, :] = across[BLOCK * quarter : BLOCK * (quarter + 1)]
    copies[2].wait()
    for f in range(2):
        field = source_here[f] * inverse
        for h in range(2):
            across = field[LANES * h : LANES * (h + 1), :].T
            for quarter in range(4):
                rows = pl.ds(LANES * place_of(f, quarter) + h, BLOCK, stride=2)
                sent[rows, :] = across[BLOCK * quarter : BLOCK * (quarter + 1)]


def from_block(blocks, a, chunk, field):
    return blocks[pl.ds(LANES * place_of(a // 8, a // 2 % 4) + 64 * field + 16 * chunk + a % 2, 8, stride=2), :]


def lines(spectrum, y):
    return spectrum[pl.ds(16 * y, 16), :]


def forward_x(table, rs, spectrum):
    for t in range(16):
        spectrum[pl.ds(t, BLOCK, stride=16), :] = forward_dot(rs[t], table, t)


def backward_x(spectrum, table, rs):
    for t in range(16):
        rs[t] = backward_dot(spectrum[pl.ds(t, BLOCK, stride=16), :], table, t)


def local_sums(spectrum, waves, ends):
    rho = waves[0]
    p = lines(spectrum, 0)
    q = lines(spectrum, BLOCK - 1)
    for y in range(1, BLOCK):
        p = rho * p + lines(spectrum, y)
        q = rho * q + lines(spectrum, BLOCK - 1 - y)
    ends[0], ends[1] = p, q


def both_cores(ends, sibling, whole, upper):
    p = jnp.where(upper, ends[0] + whole * sibling[0], sibling[0] + whole * ends[0])
    q = jnp.where(upper, sibling[1] + whole * ends[1], ends[1] + whole * sibling[1])
    return p, q


def leave_lines(ends, sibling, waves, here, core, sent):
    decay = waves[1]
    upper = core[...] > 0
    p, q = both_cores(ends, sibling, jnp.exp(-decay), upper)
    b = here[...]
    above = p + jnp.exp(-decay * (4.0 * b + 2.0)) * q
    below = q + jnp.exp(-decay * (4.0 * (BLOCKS - 1.0 - b) + 2.0)) * p
    above = jnp.where(upper, above[8:], above[:8])
    below = jnp.where(upper, below[8:], below[:8])
    for n in range(BLOCKS):
        value = jnp.where(b < n, above, below)
        for twin in range(2):
            sent[pl.ds(16 * n + 8 * twin, 8), :] = value


def solve_lines(received, spectrum, waves, here, core, ends, sibling, solved):
    rho, decay, scale, rounds = waves[0], waves[1], waves[2], waves[3]
    whole, double = jnp.exp(-decay), jnp.exp(-2.0 * decay)
    b = here[...]
    middle = BLOCKS // 2
    low, high = [[jnp.zeros((16, LANES), jnp.float32)] * 2 for _ in range(2)]
    for n in range(middle):
        for part in range(2):
            k = n + middle * part
            low[part] = jnp.where(b > k, received[pl.ds(16 * k, 16), :] + double * low[part], low[part])
            m = BLOCKS - 1 - k
            high[part] = jnp.where(b < m, received[pl.ds(16 * m, 16), :] + double * high[part], high[part])
    low = low[1] + jnp.exp(-2.0 * decay * jnp.maximum(b - middle, 0.0)) * low[0]
    high = high[1] + jnp.exp(-2.0 * decay * jnp.maximum(middle - 1.0 - b, 0.0)) * high[0]
    upper = core[...] > 0
    p, q = both_cores(ends, sibling, whole, upper)
    left = jnp.exp(-decay * (4.0 * b))
    right = jnp.exp(-decay * (4.0 * (BLOCKS - 1.0 - b)))
    up = (low + left * (q + double * (high + right * p))) * rounds
    down = high + right * (p + double * up)
    up = jnp.where(upper, sibling[0] + whole * up, up)
    down = jnp.where(upper, down, sibling[1] + whole * down)
    for y in range(BLOCK):
        up = rho * up + lines(spectrum, y)
        solved[pl.ds(16 * y, 16), :] = up
    for y in range(BLOCK - 1, -1, -1):
        down = rho * down
        solved[pl.ds(16 * y, 16), :] = scale * (lines(solved, y) + down)
        down = down + lines(spectrum, y)


def pencil_first(blocks, table, waves, spectrum, ends, rs):
    for chunk in range(4):
        x = [from_block(blocks, a, chunk, 0) for a in range(16)]
        put_first(*first_stage(x), rs, chunk)
    forward_x(table, rs, spectrum)
    local_sums(spectrum, waves, ends)


def pencil_middle(
    received, blocks, old, old_ends, sibling, table, waves, here, core, spectrum, ends, kept, sums, rs, solved
):
    solve_lines(received, old, waves, here, core, old_ends, sibling, solved)
    backward_x(solved, table, rs)
    totals = [jnp.zeros((8, LANES), jnp.float32) for _ in range(2)]
    for chunk in range(4):
        x = first_stage_transposed(*get_first(rs, chunk))
        scaled = [x[a] * from_block(blocks, a, chunk, 1) for a in range(16)]
        for a in range(16):
            kept[a, pl.ds(8 * chunk, 8), :] = x[a]
            totals[0] += from_block(blocks, a, chunk, 0) * x[a]
            totals[1] += scaled[a] * x[a]
        put_first(*first_stage(scaled), rs, chunk)
    sums[0], sums[1] = totals
    forward_x(table, rs, spectrum)
    local_sums(spectrum, waves, ends)


def pencil_last(received, blocks, old, old_ends, sibling, kept, first, table, waves, here, core, sent, rs, solved):
    solve_lines(received, old, waves, here, core, old_ends, sibling, solved)
    backward_x(solved, table, rs)
    n0, n1 = (jnp.sum(first[n], axis=(0, 1), keepdims=True) for n in range(2))
    positive = n0 + n1 > 0.0
    step = jnp.where(positive, n0 / jnp.where(positive, n0 + n1, 1.0), 0.0)
    step = jnp.clip(step, 0.0, 2.0)
    sums = [jnp.zeros((8, LANES), jnp.float32) for _ in range(7)]
    for chunk in range(4):
        x = first_stage_transposed(*get_first(rs, chunk))
        for a in range(16):
            before, new = kept[a, pl.ds(8 * chunk, 8), :], x[a]
            weight, source = from_block(blocks, a, chunk, 1), from_block(blocks, a, chunk, 0)
            g, h = source + weight * before, before + new
            u1, z1 = source - step * g, before - step * h
            wz, wh = weight * z1, weight * h
            for q, (one, two) in enumerate(((u1, z1), (u1, h), (g, z1), (g, h), (wz, z1), (wz, h), (wh, h))):
                sums[q] += one * two
            place = 130 * (a // 2) + 16 * chunk + a % 2
            sent[pl.ds(place, 8, stride=2), :] = before
            sent[pl.ds(place + 64, 8, stride=2), :] = new
    lane = lax.broadcasted_iota(jnp.int32, (2, LANES), 1)
    line = jnp.where(lane == 7, n0, jnp.where(lane == 8, n1, jnp.where(lane >= 64, step, 0.0)))
    for q in range(7):
        line = jnp.where(lane == q, jnp.sum(sums[q], axis=(0, 1), keepdims=True), line)
    for i in range(8):
        sent[pl.ds(130 * i + 128, 2), :] = line


def gather_sums(received, sent):
    rows = received[pl.ds(128, 8, stride=130), :]
    for n in range(16):
        sent[pl.ds(8 * n, 8), :] = rows


def enter_block(received, parts, sources, metric, helm, solution, resid, near, done):
    copies = []
    lane = lax.broadcasted_iota(jnp.int32, (1, LANES), 1)
    row = lax.broadcasted_iota(jnp.int32, (LANES, LANES), 0)
    every = parts[...]
    steps = pltpu.roll(every, 64, 1)

    def total(line):
        return jnp.sum(line, axis=1, keepdims=True)

    def pick(line, q):
        return total(jnp.where(lane == q, line, 0.0))

    m = metric[...]
    inverse = 1.0 / m
    weight = helm[...] * inverse - SHIFT * m
    for f in range(2):
        mine = jnp.where(row % 8 // 4 == f, every, 0.0)
        zeroth = jnp.sum(mine, axis=0, keepdims=True)
        n0, n1 = pick(zeroth, 7), pick(zeroth, 8)
        delta = n0 + n1
        alpha, rest = n0 / delta, n1 / delta
        away = alpha - steps
        moved = away * mine
        first = jnp.sum(moved, axis=0, keepdims=True)
        second = jnp.sum(away * moved, axis=0, keepdims=True)
        once = (lane == 1) | (lane == 2)
        gamma = total(jnp.where(lane == 0, zeroth, jnp.where(once, -first, jnp.where(lane == 3, second, 0.0))))
        inner = total(jnp.where(lane == 4, zeroth, jnp.where(lane == 5, -2.0 * first, jnp.where(lane == 6, second, 0.0))))
        cross = total(jnp.where(lane == 2, zeroth, jnp.where(lane == 3, -first, 0.0)))
        beta = gamma / n0
        size = gamma / (gamma + inner + 2.0 * beta * cross + beta * beta * delta)
        c0, c1 = alpha + size * (rest + beta), -size * alpha
        for h in range(2):
            pair = []
            for field in range(2):
                places = [130 * (4 * f + quarter) + 64 * field + h for quarter in range(4)]
                columns = [received[pl.ds(place, BLOCK, stride=2), :] for place in places]
                pair.append(jnp.concatenate(columns, axis=0).T)
            old, new = pair
            rows = slice(LANES * h, LANES * (h + 1))
            near[0, f, rows, :] = (c0 * old + c1 * new) * inverse[rows]
            near[1, f, rows, :] = (1.0 - c0) * sources[f, rows, :] - ((c0 + c1) * old + c1 * new) * weight[rows]
        for n, out in enumerate((solution, resid)):
            copies.append(pltpu.make_async_copy(near.at[n, f], out.at[f], done.at[2 * n + f]))
            copies[-1].start()
    for copy in copies:
        copy.wait()


RS = pltpu.VMEM((16, 32, 2 * LANES), jnp.float32)
LINES = pltpu.VMEM((512, LANES), jnp.float32)
BLOCKS_SENT, SENT, SPECTRUM = (1024, LANES), (512, LANES), (512, LANES)
ENDS, KEPT = (2, 16, LANES), (16, 32, LANES)


def call(kernel, outs, scratch, **more):
    return pl.pallas_call(
        kernel,
        out_shape=[jax.ShapeDtypeStruct(s, jnp.float32) for s in outs],
        scratch_shapes=scratch,
        compiler_params=pltpu.CompilerParams(vmem_limit_bytes=32 * 1024 * 1024),
        **more,
    )


def far(*arrays):
    return [pltpu.with_memory_space_constraint(a, pltpu.HBM) for a in arrays]


def exchange(flat, axes, *shape):
    moved = lax.all_to_all(flat.reshape(*shape, LANES), axes, 0, 0, tiled=True)
    return moved.reshape(flat.shape)


def per_device(sources, metric, helm):
    table, waves = (jnp.asarray(a) for a in tables())
    line, column = ("half", "pair", "core"), ("gy", "pair", "core")
    here = lax.axis_index("gy") * lax.axis_size("pair") + lax.axis_index("pair")
    here = jnp.full((1, LANES), here, jnp.float32)
    core = jnp.full((1, LANES), lax.axis_index("core"), jnp.float32)
    block = pltpu.VMEM(metric.shape, metric.dtype)
    hbm, vmem = pl.BlockSpec(memory_space=pl.ANY), pl.BlockSpec(memory_space=pltpu.VMEM)

    def swap(ends):
        return lax.ppermute(ends, "core", [(0, 1), (1, 0)])

    (sent,) = call(
        leave_block,
        [BLOCKS_SENT],
        [pltpu.VMEM(sources.shape, sources.dtype), block, block, pltpu.SemaphoreType.DMA((4,))],
        in_specs=[hbm] * 5 + [vmem] * 2,
    )(*far(sources, metric, helm, table, waves), here, core)
    blocks = exchange(sent, ("pair", "core", "half"), 8, 128)
    first, ends = call(pencil_first, [SPECTRUM, ENDS], [RS])(blocks, table, waves)
    sibling = swap(ends)
    (sent,) = call(leave_lines, [SENT], [])(ends, sibling, waves, here, core)
    received = exchange(sent, column, 64, 8)
    second, more, kept, sums = call(pencil_middle, [SPECTRUM, ENDS, KEPT, (2, 8, LANES)], [RS, LINES])(
        received, blocks, first, ends, sibling, table, waves, here, core
    )
    twin = swap(more)
    (sent,) = call(leave_lines, [SENT], [])(more, twin, waves, here, core)
    received = exchange(sent, column, 64, 8)
    (sent,) = call(pencil_last, [(8 * 130, LANES)], [RS, LINES])(
        received, blocks, second, more, twin, kept, sums, table, waves, here, core
    )
    received = exchange(sent, line, 8, 65, 2)
    (parts,) = call(gather_sums, [(LANES, LANES)], [])(received)
    parts = exchange(parts, "gy", 16, 8)
    outs = call(
        enter_block,
        [sources.shape] * 2,
        [pltpu.VMEM((2, *sources.shape), jnp.float32), pltpu.SemaphoreType.DMA((4,))],
        in_specs=[vmem] * 5,
        out_specs=[hbm] * 2,
    )(received, parts, sources, metric, helm)
    return tuple(outs)


def solution(mesh):
    devices = mesh.devices.reshape(2, 2, 2, 16)
    finer = jax.sharding.Mesh(devices, ("half", "pair", "core", "gy"))
    line = ("half", "pair", "core")
    in_specs = (P(None, line, "gy"), P(line, "gy"), P(line, "gy"))
    out_specs = (P(None, line, "gy"), P(None, line, "gy"))
    return jax.shard_map(
        per_device, mesh=finer, in_specs=in_specs, out_specs=out_specs, check_vma=False
    )
```

```python
import functools
import math

import jax
import jax.numpy as jnp
import ml_dtypes
import numpy as np
from jax import lax
from jax.experimental import pallas as pl
from jax.experimental.pallas import tpu as pltpu
from jax.sharding import PartitionSpec as P

SHIFT = 0.001
ROWS = 16
BLOCK = 32
BLOCKS = 32
LANES = 128
LENGTH = ROWS * LANES


def frequency():
    t = np.arange(16)[:, None]
    k2 = np.arange(64)[None, :]
    first = t + 32 * k2
    second = np.where(t == 0, 16, 32 - t) + 32 * k2
    return np.concatenate([first, second], axis=1)


def tables():
    freq = frequency()
    b = np.arange(LANES)
    phase = (freq[:, None, :] * (2 * b[None, :, None] + 1)) % (4 * LENGTH)
    angle = phase * (math.pi / (2 * LENGTH))
    scale = np.where(freq == 0, math.sqrt(1.0 / LENGTH), math.sqrt(2.0 / LENGTH))[:, None, :]
    even, odd = scale * np.cos(angle), scale * np.sin(angle)
    sign = np.where(np.arange(LANES) < 64, -1.0, 1.0)
    full = np.concatenate([even, odd * sign], axis=1)
    full[0, :LANES, 64:] = 0.0
    full[0, LANES:, :64] = 0.0
    full[0, LANES:, 64:] = even[0, :, 64:]
    high = full.astype(ml_dtypes.bfloat16)
    low = (full - high.astype(np.float64)).astype(ml_dtypes.bfloat16)
    forward = np.concatenate([high, low], axis=2)
    sigma = 4.0 * np.sin(math.pi * freq / (2 * LENGTH)) ** 2 + SHIFT
    mu = 2.0 * np.arcsinh(np.sqrt(sigma) / 2.0)
    waves = [np.exp(-mu), BLOCK * mu, 0.5 / np.sinh(mu), 1.0 / (1.0 - np.exp(-4.0 * BLOCK * BLOCKS * mu))]
    return np.stack([forward, np.swapaxes(forward, 1, 2)], axis=1), np.stack(waves).astype(np.float32)


def cos16(n):
    return float(math.cos(math.pi * n / 16))


def sin16(n):
    return float(math.sin(math.pi * n / 16))


def combine(terms):
    total = None
    for c, v in terms:
        if abs(c) < 1e-12:
            continue
        if abs(abs(c) - 1.0) < 1e-12:
            if total is None:
                total = v if c > 0 else -v
            else:
                total = total + v if c > 0 else total - v
        else:
            total = c * v if total is None else total + c * v
    return total


def first_stage(x):
    p = {a: x[a] + x[16 - a] for a in range(1, 8)}
    m = {a: x[a] - x[16 - a] for a in range(1, 8)}
    R, S = {}, {}
    for j in range(1, 8):
        c, s = (m, p) if j % 2 else (p, m)
        ev = combine([(1.0, x[0])] + [(cos16(j * a), c[a]) for a in (2, 4, 6)] + [(cos16(8 * j), x[8])])
        od = combine([(cos16(j * a), c[a]) for a in (1, 3, 5, 7)])
        R[j], R[16 - j] = ev + od, ev - od
        ev = combine([(sin16(j * a), s[a]) for a in (2, 4, 6)] + [(sin16(8 * j), x[8])])
        od = combine([(sin16(j * a), s[a]) for a in (1, 3, 5, 7)])
        S[j], S[16 - j] = od + ev, od - ev
    outer, inner = x[0] + x[8], p[2] + p[6]
    R[8] = outer + p[4] - inner
    S[8] = (m[1] + m[5]) - (m[3] + m[7])
    even, odd = outer + p[4] + inner, (p[1] + p[7]) + (p[3] + p[5])
    R[0], R[16] = even + odd, even - odd
    return R, S


def first_stage_transposed(R, S):
    rp = {j: R[j] + R[16 - j] for j in range(1, 8)}
    rm = {j: R[j] - R[16 - j] for j in range(1, 8)}
    sp = {j: S[j] + S[16 - j] for j in range(1, 8)}
    sm = {j: S[j] - S[16 - j] for j in range(1, 8)}
    ends, wide = R[0] + R[16], R[0] - R[16]
    x = {}
    for a in range(1, 8):
        r, s = (rm, sp) if a % 2 else (rp, sm)
        ce = combine([(1.0, wide if a % 2 else ends), (cos16(8 * a), R[8])] + [(cos16(j * a), r[j]) for j in (2, 4, 6)])
        co = combine([(cos16(j * a), r[j]) for j in (1, 3, 5, 7)])
        se = combine([(sin16(8 * a), S[8])] + [(sin16(j * a), s[j]) for j in (2, 4, 6)])
        so = combine([(sin16(j * a), s[j]) for j in (1, 3, 5, 7)])
        x[a], x[16 - a] = (ce + so) + (co + se), (ce + so) - (co + se)
    even = ends + R[8] + rp[2] + rp[4] + rp[6]
    x[0] = even + (rp[1] + rp[7]) + (rp[3] + rp[5])
    x[8] = ends + R[8] - rp[2] + rp[4] - rp[6] + (sm[1] - sm[3]) + (sm[5] - sm[7])
    return x


def split(value):
    high = value.astype(jnp.bfloat16)
    return high, (value - high.astype(jnp.float32)).astype(jnp.bfloat16)


def forward_dot(value, table, t):
    high, low = split(value)
    both = jnp.dot(jnp.concatenate([high, low], axis=0), table[t, 0, :, :LANES], preferred_element_type=jnp.float32)
    third = jnp.dot(high, table[t, 0, :, LANES:], preferred_element_type=jnp.float32)
    return both[:32] + (both[32:] + third)


def backward_dot(value, table, t):
    high, low = split(value)
    both = jnp.dot(jnp.concatenate([high, low], axis=0), table[t, 1, :LANES, :], preferred_element_type=jnp.float32)
    third = jnp.dot(high, table[t, 1, LANES:, :], preferred_element_type=jnp.float32)
    return both[:32] + (both[32:] + third)


def put_first(R, S, rs, chunk):
    rows = pl.ds(8 * chunk, 8)
    for t in range(16):
        rs[t, rows, 0:LANES] = R[t]
        rs[t, rows, LANES : 2 * LANES] = R[16] if t == 0 else S[t]


def get_first(rs, chunk):
    rows = pl.ds(8 * chunk, 8)
    R = {t: rs[t, rows, 0:LANES] for t in range(16)}
    S = {t: rs[t, rows, LANES : 2 * LANES] for t in range(1, 16)}
    R[16] = rs[0, rows, LANES : 2 * LANES]
    return R, S


def place_of(half, quarter):
    return 2 * quarter + half


def leave_block(sources, metric, helm, table, waves, here, core, sent, source_here, metric_here, helm_here, arrived):
    moves = [(metric, metric_here), (helm, helm_here), (sources, source_here)]
    copies = [pltpu.make_async_copy(a, b, arrived.at[n]) for n, (a, b) in enumerate(moves)]
    for copy in copies:
        copy.start(priority=1)
    copies[0].wait()
    inverse = 1.0 / metric_here[...]
    copies[1].wait()
    weight = helm_here[...] * (inverse * inverse) - SHIFT
    for h in range(2):
        across = weight[LANES * h : LANES * (h + 1), :].T
        for quarter in range(4):
            for f in range(2):
                rows = pl.ds(LANES * place_of(f, quarter) + 64 + h, BLOCK, stride=2)
                sent[rows, :] = across[BLOCK * quarter : BLOCK * (quarter + 1)]
    copies[2].wait()
    for f in range(2):
        field = source_here[f] * inverse
        for h in range(2):
            across = field[LANES * h : LANES * (h + 1), :].T
            for quarter in range(4):
                rows = pl.ds(LANES * place_of(f, quarter) + h, BLOCK, stride=2)
                sent[rows, :] = across[BLOCK * quarter : BLOCK * (quarter + 1)]


def from_block(blocks, a, chunk, field):
    return blocks[pl.ds(LANES * place_of(a // 8, a // 2 % 4) + 64 * field + 16 * chunk + a % 2, 8, stride=2), :]


def lines(spectrum, y):
    return spectrum[pl.ds(16 * y, 16), :]


def forward_x(table, rs, spectrum):
    for t in range(16):
        spectrum[pl.ds(t, BLOCK, stride=16), :] = forward_dot(rs[t], table, t)


def backward_x(spectrum, table, rs):
    for t in range(16):
        rs[t] = backward_dot(spectrum[pl.ds(t, BLOCK, stride=16), :], table, t)


def local_sums(spectrum, waves, ends):
    rho = waves[0]
    p = lines(spectrum, 0)
    q = lines(spectrum, BLOCK - 1)
    for y in range(1, BLOCK):
        p = rho * p + lines(spectrum, y)
        q = rho * q + lines(spectrum, BLOCK - 1 - y)
    ends[0], ends[1] = p, q


def both_cores(ends, sibling, whole, upper):
    p = jnp.where(upper, ends[0] + whole * sibling[0], sibling[0] + whole * ends[0])
    q = jnp.where(upper, sibling[1] + whole * ends[1], ends[1] + whole * sibling[1])
    return p, q


def leave_lines(ends, sibling, waves, here, core, sent):
    decay = waves[1]
    upper = core[...] > 0
    p, q = both_cores(ends, sibling, jnp.exp(-decay), upper)
    b = here[...]
    above = p + jnp.exp(-decay * (4.0 * b + 2.0)) * q
    below = q + jnp.exp(-decay * (4.0 * (BLOCKS - 1.0 - b) + 2.0)) * p
    above = jnp.where(upper, above[8:], above[:8])
    below = jnp.where(upper, below[8:], below[:8])
    for n in range(BLOCKS):
        value = jnp.where(b < n, above, below)
        for twin in range(2):
            sent[pl.ds(16 * n + 8 * twin, 8), :] = value


def solve_lines(received, spectrum, waves, here, core, ends, sibling, solved):
    rho, decay, scale, rounds = waves[0], waves[1], waves[2], waves[3]
    whole, double = jnp.exp(-decay), jnp.exp(-2.0 * decay)
    b = here[...]
    middle = BLOCKS // 2
    low, high = [[jnp.zeros((16, LANES), jnp.float32)] * 2 for _ in range(2)]
    for n in range(middle):
        for part in range(2):
            k = n + middle * part
            low[part] = jnp.where(b > k, received[pl.ds(16 * k, 16), :] + double * low[part], low[part])
            m = BLOCKS - 1 - k
            high[part] = jnp.where(b < m, received[pl.ds(16 * m, 16), :] + double * high[part], high[part])
    low = low[1] + jnp.exp(-2.0 * decay * jnp.maximum(b - middle, 0.0)) * low[0]
    high = high[1] + jnp.exp(-2.0 * decay * jnp.maximum(middle - 1.0 - b, 0.0)) * high[0]
    upper = core[...] > 0
    p, q = both_cores(ends, sibling, whole, upper)
    left = jnp.exp(-decay * (4.0 * b))
    right = jnp.exp(-decay * (4.0 * (BLOCKS - 1.0 - b)))
    up = (low + left * (q + double * (high + right * p))) * rounds
    down = high + right * (p + double * up)
    up = jnp.where(upper, sibling[0] + whole * up, up)
    down = jnp.where(upper, down, sibling[1] + whole * down)
    for y in range(BLOCK):
        up = rho * up + lines(spectrum, y)
        solved[pl.ds(16 * y, 16), :] = up
    for y in range(BLOCK - 1, -1, -1):
        down = rho * down
        solved[pl.ds(16 * y, 16), :] = scale * (lines(solved, y) + down)
        down = down + lines(spectrum, y)


def pencil_first(blocks, table, waves, spectrum, ends, rs):
    for chunk in range(4):
        x = [from_block(blocks, a, chunk, 0) for a in range(16)]
        put_first(*first_stage(x), rs, chunk)
    forward_x(table, rs, spectrum)
    local_sums(spectrum, waves, ends)


def pencil_middle(
    received, blocks, old, old_ends, sibling, table, waves, here, core, spectrum, ends, kept, sums, rs, solved
):
    solve_lines(received, old, waves, here, core, old_ends, sibling, solved)
    backward_x(solved, table, rs)
    totals = [jnp.zeros((8, LANES), jnp.float32) for _ in range(2)]
    for chunk in range(4):
        x = first_stage_transposed(*get_first(rs, chunk))
        scaled = [x[a] * from_block(blocks, a, chunk, 1) for a in range(16)]
        for a in range(16):
            kept[a, pl.ds(8 * chunk, 8), :] = x[a]
            totals[0] += from_block(blocks, a, chunk, 0) * x[a]
            totals[1] += scaled[a] * x[a]
        put_first(*first_stage(scaled), rs, chunk)
    sums[0], sums[1] = totals
    forward_x(table, rs, spectrum)
    local_sums(spectrum, waves, ends)


def pencil_last(received, blocks, old, old_ends, sibling, kept, first, table, waves, here, core, sent, rs, solved):
    solve_lines(received, old, waves, here, core, old_ends, sibling, solved)
    backward_x(solved, table, rs)
    n0, n1 = (jnp.sum(first[n], axis=(0, 1), keepdims=True) for n in range(2))
    positive = n0 + n1 > 0.0
    step = jnp.where(positive, n0 / jnp.where(positive, n0 + n1, 1.0), 0.0)
    step = jnp.clip(step, 0.0, 2.0)
    sums = [jnp.zeros((8, LANES), jnp.float32) for _ in range(7)]
    for chunk in range(4):
        x = first_stage_transposed(*get_first(rs, chunk))
        for a in range(16):
            before, new = kept[a, pl.ds(8 * chunk, 8), :], x[a]
            weight, source = from_block(blocks, a, chunk, 1), from_block(blocks, a, chunk, 0)
            g, h = source + weight * before, before + new
            u1, z1 = source - step * g, before - step * h
            wz, wh = weight * z1, weight * h
            for q, (one, two) in enumerate(((u1, z1), (u1, h), (g, z1), (g, h), (wz, z1), (wz, h), (wh, h))):
                sums[q] += one * two
            place = 130 * place_of(a // 8, a // 2 % 4) + 16 * chunk + a % 2
            sent[pl.ds(place, 8, stride=2), :] = before
            sent[pl.ds(place + 64, 8, stride=2), :] = new
    lane = lax.broadcasted_iota(jnp.int32, (2, LANES), 1)
    line = jnp.where(lane == 7, n0, jnp.where(lane == 8, n1, jnp.where(lane >= 64, step, 0.0)))
    for q in range(7):
        line = jnp.where(lane == q, jnp.sum(sums[q], axis=(0, 1), keepdims=True), line)
    for i in range(8):
        sent[pl.ds(130 * i + 128, 2), :] = line


def gather_sums(received, sent):
    rows = received[pl.ds(128, 8, stride=130), :]
    for n in range(16):
        sent[pl.ds(8 * n, 8), :] = rows


def enter_block(received, parts, sources, metric, helm, solution, resid, near, done):
    copies = []
    lane = lax.broadcasted_iota(jnp.int32, (1, LANES), 1)
    row = lax.broadcasted_iota(jnp.int32, (LANES, LANES), 0)
    every = parts[...]
    steps = pltpu.roll(every, 64, 1)

    def total(line):
        return jnp.sum(line, axis=1, keepdims=True)

    def pick(line, q):
        return total(jnp.where(lane == q, line, 0.0))

    m = metric[...]
    inverse = 1.0 / m
    weight = helm[...] * inverse - SHIFT * m
    for f in range(2):
        mine = jnp.where(row % 2 == f, every, 0.0)
        zeroth = jnp.sum(mine, axis=0, keepdims=True)
        n0, n1 = pick(zeroth, 7), pick(zeroth, 8)
        delta = n0 + n1
        alpha, rest = n0 / delta, n1 / delta
        away = alpha - steps
        moved = away * mine
        first = jnp.sum(moved, axis=0, keepdims=True)
        second = jnp.sum(away * moved, axis=0, keepdims=True)
        once = (lane == 1) | (lane == 2)
        gamma = total(jnp.where(lane == 0, zeroth, jnp.where(once, -first, jnp.where(lane == 3, second, 0.0))))
        inner = total(jnp.where(lane == 4, zeroth, jnp.where(lane == 5, -2.0 * first, jnp.where(lane == 6, second, 0.0))))
        cross = total(jnp.where(lane == 2, zeroth, jnp.where(lane == 3, -first, 0.0)))
        beta = gamma / n0
        size = gamma / (gamma + inner + 2.0 * beta * cross + beta * beta * delta)
        c0, c1 = alpha + size * (rest + beta), -size * alpha
        for h in range(2):
            pair = []
            for field in range(2):
                places = [130 * place_of(f, quarter) + 64 * field + h for quarter in range(4)]
                columns = [received[pl.ds(place, BLOCK, stride=2), :] for place in places]
                pair.append(jnp.concatenate(columns, axis=0).T)
            old, new = pair
            rows = slice(LANES * h, LANES * (h + 1))
            near[0, f, rows, :] = (c0 * old + c1 * new) * inverse[rows]
            near[1, f, rows, :] = (1.0 - c0) * sources[f, rows, :] - ((c0 + c1) * old + c1 * new) * weight[rows]
        for n, out in enumerate((solution, resid)):
            copies.append(pltpu.make_async_copy(near.at[n, f], out.at[f], done.at[2 * n + f]))
            copies[-1].start()
    for copy in copies:
        copy.wait()


RS = pltpu.VMEM((16, 32, 2 * LANES), jnp.float32)
LINES = pltpu.VMEM((512, LANES), jnp.float32)
BLOCKS_SENT, SENT, SPECTRUM = (1024, LANES), (512, LANES), (512, LANES)
ENDS, KEPT = (2, 16, LANES), (16, 32, LANES)


def call(kernel, outs, scratch, **more):
    return pl.pallas_call(
        kernel,
        out_shape=[jax.ShapeDtypeStruct(s, jnp.float32) for s in outs],
        scratch_shapes=scratch,
        compiler_params=pltpu.CompilerParams(vmem_limit_bytes=32 * 1024 * 1024),
        **more,
    )


def far(*arrays):
    return [pltpu.with_memory_space_constraint(a, pltpu.HBM) for a in arrays]


def exchange(flat, axes, *shape):
    moved = lax.all_to_all(flat.reshape(*shape, LANES), axes, 0, 0, tiled=True)
    return moved.reshape(flat.shape)


def per_device(sources, metric, helm):
    table, waves = (jnp.asarray(a) for a in tables())
    line, column = ("pair", "core", "half"), ("gy", "pair", "core")
    here = lax.axis_index("gy") * lax.axis_size("pair") + lax.axis_index("pair")
    here = jnp.full((1, LANES), here, jnp.float32)
    core = jnp.full((1, LANES), lax.axis_index("core"), jnp.float32)
    block = pltpu.VMEM(metric.shape, metric.dtype)
    hbm, vmem = pl.BlockSpec(memory_space=pl.ANY), pl.BlockSpec(memory_space=pltpu.VMEM)

    def swap(ends):
        return lax.ppermute(ends, "core", [(0, 1), (1, 0)])

    (sent,) = call(
        leave_block,
        [BLOCKS_SENT],
        [pltpu.VMEM(sources.shape, sources.dtype), block, block, pltpu.SemaphoreType.DMA((4,))],
        in_specs=[hbm] * 5 + [vmem] * 2,
    )(*far(sources, metric, helm, table, waves), here, core)
    blocks = exchange(sent, line, 8, 128)
    first, ends = call(pencil_first, [SPECTRUM, ENDS], [RS])(blocks, table, waves)
    sibling = swap(ends)
    (sent,) = call(leave_lines, [SENT], [])(ends, sibling, waves, here, core)
    received = exchange(sent, column, 64, 8)
    second, more, kept, sums = call(pencil_middle, [SPECTRUM, ENDS, KEPT, (2, 8, LANES)], [RS, LINES])(
        received, blocks, first, ends, sibling, table, waves, here, core
    )
    twin = swap(more)
    (sent,) = call(leave_lines, [SENT], [])(more, twin, waves, here, core)
    received = exchange(sent, column, 64, 8)
    (sent,) = call(pencil_last, [(8 * 130, LANES)], [RS, LINES])(
        received, blocks, second, more, twin, kept, sums, table, waves, here, core
    )
    received = exchange(sent, line, 8, 65, 2)
    (parts,) = call(gather_sums, [(LANES, LANES)], [])(received)
    parts = exchange(parts, "gy", 16, 8)
    outs = call(
        enter_block,
        [sources.shape] * 2,
        [pltpu.VMEM((2, *sources.shape), jnp.float32), pltpu.SemaphoreType.DMA((4,))],
        in_specs=[vmem] * 5,
        out_specs=[hbm] * 2,
    )(received, parts, sources, metric, helm)
    return tuple(outs)


def solution(mesh):
    devices = mesh.devices.reshape(2, 2, 2, 16)
    finer = jax.sharding.Mesh(devices, ("half", "pair", "core", "gy"))
    line = ("half", "pair", "core")
    in_specs = (P(None, line, "gy"), P(line, "gy"), P(line, "gy"))
    out_specs = (P(None, line, "gy"), P(None, line, "gy"))
    return jax.shard_map(
        per_device, mesh=finer, in_specs=in_specs, out_specs=out_specs, check_vma=False
    )
```

```python
import functools
import math

import jax
import jax.numpy as jnp
import ml_dtypes
import numpy as np
from jax import lax
from jax.experimental import pallas as pl
from jax.experimental.pallas import tpu as pltpu
from jax.sharding import PartitionSpec as P

SHIFT = 0.001
ROWS = 16
BLOCK = 32
BLOCKS = 32
LANES = 128
LENGTH = ROWS * LANES


def frequency():
    t = np.arange(16)[:, None]
    k2 = np.arange(64)[None, :]
    first = t + 32 * k2
    second = np.where(t == 0, 16, 32 - t) + 32 * k2
    return np.concatenate([first, second], axis=1)


def tables():
    freq = frequency()
    b = np.arange(LANES)
    phase = (freq[:, None, :] * (2 * b[None, :, None] + 1)) % (4 * LENGTH)
    angle = phase * (math.pi / (2 * LENGTH))
    scale = np.where(freq == 0, math.sqrt(1.0 / LENGTH), math.sqrt(2.0 / LENGTH))[:, None, :]
    even, odd = scale * np.cos(angle), scale * np.sin(angle)
    sign = np.where(np.arange(LANES) < 64, -1.0, 1.0)
    full = np.concatenate([even, odd * sign], axis=1)
    full[0, :LANES, 64:] = 0.0
    full[0, LANES:, :64] = 0.0
    full[0, LANES:, 64:] = even[0, :, 64:]
    high = full.astype(ml_dtypes.bfloat16)
    low = (full - high.astype(np.float64)).astype(ml_dtypes.bfloat16)
    forward = np.concatenate([high, low], axis=2)
    sigma = 4.0 * np.sin(math.pi * freq / (2 * LENGTH)) ** 2 + SHIFT
    mu = 2.0 * np.arcsinh(np.sqrt(sigma) / 2.0)
    waves = [np.exp(-mu), BLOCK * mu, 0.5 / np.sinh(mu), 1.0 / (1.0 - np.exp(-4.0 * BLOCK * BLOCKS * mu))]
    return np.stack([forward, np.swapaxes(forward, 1, 2)], axis=1), np.stack(waves).astype(np.float32)


def cos16(n):
    return float(math.cos(math.pi * n / 16))


def sin16(n):
    return float(math.sin(math.pi * n / 16))


def combine(terms):
    total = None
    for c, v in terms:
        if abs(c) < 1e-12:
            continue
        if abs(abs(c) - 1.0) < 1e-12:
            if total is None:
                total = v if c > 0 else -v
            else:
                total = total + v if c > 0 else total - v
        else:
            total = c * v if total is None else total + c * v
    return total


def first_stage(x):
    p = {a: x[a] + x[16 - a] for a in range(1, 8)}
    m = {a: x[a] - x[16 - a] for a in range(1, 8)}
    R, S = {}, {}
    for j in range(1, 8):
        c, s = (m, p) if j % 2 else (p, m)
        ev = combine([(1.0, x[0])] + [(cos16(j * a), c[a]) for a in (2, 4, 6)] + [(cos16(8 * j), x[8])])
        od = combine([(cos16(j * a), c[a]) for a in (1, 3, 5, 7)])
        R[j], R[16 - j] = ev + od, ev - od
        ev = combine([(sin16(j * a), s[a]) for a in (2, 4, 6)] + [(sin16(8 * j), x[8])])
        od = combine([(sin16(j * a), s[a]) for a in (1, 3, 5, 7)])
        S[j], S[16 - j] = od + ev, od - ev
    outer, inner = x[0] + x[8], p[2] + p[6]
    R[8] = outer + p[4] - inner
    S[8] = (m[1] + m[5]) - (m[3] + m[7])
    even, odd = outer + p[4] + inner, (p[1] + p[7]) + (p[3] + p[5])
    R[0], R[16] = even + odd, even - odd
    return R, S


def first_stage_transposed(R, S):
    rp = {j: R[j] + R[16 - j] for j in range(1, 8)}
    rm = {j: R[j] - R[16 - j] for j in range(1, 8)}
    sp = {j: S[j] + S[16 - j] for j in range(1, 8)}
    sm = {j: S[j] - S[16 - j] for j in range(1, 8)}
    ends, wide = R[0] + R[16], R[0] - R[16]
    x = {}
    for a in range(1, 8):
        r, s = (rm, sp) if a % 2 else (rp, sm)
        ce = combine([(1.0, wide if a % 2 else ends), (cos16(8 * a), R[8])] + [(cos16(j * a), r[j]) for j in (2, 4, 6)])
        co = combine([(cos16(j * a), r[j]) for j in (1, 3, 5, 7)])
        se = combine([(sin16(8 * a), S[8])] + [(sin16(j * a), s[j]) for j in (2, 4, 6)])
        so = combine([(sin16(j * a), s[j]) for j in (1, 3, 5, 7)])
        x[a], x[16 - a] = (ce + so) + (co + se), (ce + so) - (co + se)
    even = ends + R[8] + rp[2] + rp[4] + rp[6]
    x[0] = even + (rp[1] + rp[7]) + (rp[3] + rp[5])
    x[8] = ends + R[8] - rp[2] + rp[4] - rp[6] + (sm[1] - sm[3]) + (sm[5] - sm[7])
    return x


def split(value):
    high = value.astype(jnp.bfloat16)
    return high, (value - high.astype(jnp.float32)).astype(jnp.bfloat16)


def forward_dot(value, table, t):
    high, low = split(value)
    both = jnp.dot(jnp.concatenate([high, low], axis=0), table[t, 0, :, :LANES], preferred_element_type=jnp.float32)
    third = jnp.dot(high, table[t, 0, :, LANES:], preferred_element_type=jnp.float32)
    return both[:32] + (both[32:] + third)


def backward_dot(value, table, t):
    high, low = split(value)
    both = jnp.dot(jnp.concatenate([high, low], axis=0), table[t, 1, :LANES, :], preferred_element_type=jnp.float32)
    third = jnp.dot(high, table[t, 1, LANES:, :], preferred_element_type=jnp.float32)
    return both[:32] + (both[32:] + third)


def put_first(R, S, rs, chunk):
    rows = pl.ds(8 * chunk, 8)
    for t in range(16):
        rs[t, rows, 0:LANES] = R[t]
        rs[t, rows, LANES : 2 * LANES] = R[16] if t == 0 else S[t]


def get_first(rs, chunk):
    rows = pl.ds(8 * chunk, 8)
    R = {t: rs[t, rows, 0:LANES] for t in range(16)}
    S = {t: rs[t, rows, LANES : 2 * LANES] for t in range(1, 16)}
    R[16] = rs[0, rows, LANES : 2 * LANES]
    return R, S


def place_of(half, quarter):
    return 2 * quarter + half


def leave_block(sources, metric, helm, table, waves, here, core, sent, source_here, metric_here, helm_here, arrived):
    moves = [(metric, metric_here), (helm, helm_here), (sources, source_here)]
    copies = [pltpu.make_async_copy(a, b, arrived.at[n]) for n, (a, b) in enumerate(moves)]
    for copy in copies:
        copy.start()
    copies[0].wait()
    inverse = 1.0 / metric_here[...]
    copies[1].wait()
    weight = helm_here[...] * (inverse * inverse) - SHIFT
    for h in range(2):
        across = weight[LANES * h : LANES * (h + 1), :].T
        for quarter in range(4):
            for f in range(2):
                rows = pl.ds(LANES * place_of(f, quarter) + 64 + h, BLOCK, stride=2)
                sent[rows, :] = across[BLOCK * quarter : BLOCK * (quarter + 1)]
    copies[2].wait()
    for f in range(2):
        field = source_here[f] * inverse
        for h in range(2):
            across = field[LANES * h : LANES * (h + 1), :].T
            for quarter in range(4):
                rows = pl.ds(LANES * place_of(f, quarter) + h, BLOCK, stride=2)
                sent[rows, :] = across[BLOCK * quarter : BLOCK * (quarter + 1)]


def from_block(blocks, a, chunk, field):
    return blocks[pl.ds(LANES * place_of(a // 8, a // 2 % 4) + 64 * field + 16 * chunk + a % 2, 8, stride=2), :]


def lines(spectrum, y):
    return spectrum[pl.ds(16 * y, 16), :]


def forward_x(table, rs, spectrum):
    for t in range(16):
        spectrum[pl.ds(t, BLOCK, stride=16), :] = forward_dot(rs[t], table, t)


def backward_x(spectrum, table, rs):
    for t in range(16):
        rs[t] = backward_dot(spectrum[pl.ds(t, BLOCK, stride=16), :], table, t)


def local_sums(spectrum, waves, ends):
    rho = waves[0]
    part = BLOCK // 2
    p = [lines(spectrum, 0), lines(spectrum, part)]
    q = [lines(spectrum, part - 1), lines(spectrum, BLOCK - 1)]
    for y in range(1, part):
        for n in range(2):
            p[n] = rho * p[n] + lines(spectrum, part * n + y)
            q[n] = rho * q[n] + lines(spectrum, part * (n + 1) - 1 - y)
    through = jnp.exp(-0.5 * waves[1])
    ends[0], ends[1] = p[1] + through * p[0], q[0] + through * q[1]


def both_cores(ends, sibling, whole, upper):
    p = jnp.where(upper, ends[0] + whole * sibling[0], sibling[0] + whole * ends[0])
    q = jnp.where(upper, sibling[1] + whole * ends[1], ends[1] + whole * sibling[1])
    return p, q


def leave_lines(ends, sibling, waves, here, core, sent):
    decay = waves[1]
    upper = core[...] > 0
    p, q = both_cores(ends, sibling, jnp.exp(-decay), upper)
    b = here[...]
    above = p + jnp.exp(-decay * (4.0 * b + 2.0)) * q
    below = q + jnp.exp(-decay * (4.0 * (BLOCKS - 1.0 - b) + 2.0)) * p
    above = jnp.where(upper, above[8:], above[:8])
    below = jnp.where(upper, below[8:], below[:8])
    for n in range(BLOCKS):
        value = jnp.where(b < n, above, below)
        for twin in range(2):
            sent[pl.ds(16 * n + 8 * twin, 8), :] = value


def solve_lines(received, spectrum, waves, here, core, ends, sibling, solved):
    rho, decay, scale, rounds = waves[0], waves[1], waves[2], waves[3]
    whole, double = jnp.exp(-decay), jnp.exp(-2.0 * decay)
    b = here[...]
    middle = BLOCKS // 2
    low, high = [[jnp.zeros((16, LANES), jnp.float32)] * 2 for _ in range(2)]
    for n in range(middle):
        for part in range(2):
            k = n + middle * part
            low[part] = jnp.where(b > k, received[pl.ds(16 * k, 16), :] + double * low[part], low[part])
            m = BLOCKS - 1 - k
            high[part] = jnp.where(b < m, received[pl.ds(16 * m, 16), :] + double * high[part], high[part])
    low = low[1] + jnp.exp(-2.0 * decay * jnp.maximum(b - middle, 0.0)) * low[0]
    high = high[1] + jnp.exp(-2.0 * decay * jnp.maximum(middle - 1.0 - b, 0.0)) * high[0]
    upper = core[...] > 0
    p, q = both_cores(ends, sibling, whole, upper)
    left = jnp.exp(-decay * (4.0 * b))
    right = jnp.exp(-decay * (4.0 * (BLOCKS - 1.0 - b)))
    up = (low + left * (q + double * (high + right * p))) * rounds
    down = high + right * (p + double * up)
    up = jnp.where(upper, sibling[0] + whole * up, up)
    down = jnp.where(upper, down, sibling[1] + whole * down)
    for y in range(BLOCK):
        up = rho * up + lines(spectrum, y)
        solved[pl.ds(16 * y, 16), :] = up
    for y in range(BLOCK - 1, -1, -1):
        down = rho * down
        solved[pl.ds(16 * y, 16), :] = scale * (lines(solved, y) + down)
        down = down + lines(spectrum, y)


def pencil_first(blocks, table, waves, spectrum, ends, rs):
    for chunk in range(4):
        x = [from_block(blocks, a, chunk, 0) for a in range(16)]
        put_first(*first_stage(x), rs, chunk)
    forward_x(table, rs, spectrum)
    local_sums(spectrum, waves, ends)


def pencil_middle(
    received, blocks, old, old_ends, sibling, table, waves, here, core, spectrum, ends, kept, sums, rs, solved
):
    solve_lines(received, old, waves, here, core, old_ends, sibling, solved)
    backward_x(solved, table, rs)
    totals = [jnp.zeros((8, LANES), jnp.float32) for _ in range(2)]
    for chunk in range(4):
        x = first_stage_transposed(*get_first(rs, chunk))
        scaled = [x[a] * from_block(blocks, a, chunk, 1) for a in range(16)]
        for a in range(16):
            kept[a, pl.ds(8 * chunk, 8), :] = x[a]
            totals[0] += from_block(blocks, a, chunk, 0) * x[a]
            totals[1] += scaled[a] * x[a]
        put_first(*first_stage(scaled), rs, chunk)
    sums[0], sums[1] = totals
    forward_x(table, rs, spectrum)
    local_sums(spectrum, waves, ends)


def pencil_last(received, blocks, old, old_ends, sibling, kept, first, table, waves, here, core, sent, rs, solved):
    solve_lines(received, old, waves, here, core, old_ends, sibling, solved)
    backward_x(solved, table, rs)
    n0, n1 = (jnp.sum(first[n], axis=(0, 1), keepdims=True) for n in range(2))
    positive = n0 + n1 > 0.0
    step = jnp.where(positive, n0 / jnp.where(positive, n0 + n1, 1.0), 0.0)
    step = jnp.clip(step, 0.0, 2.0)
    sums = [jnp.zeros((8, LANES), jnp.float32) for _ in range(7)]
    for chunk in range(4):
        x = first_stage_transposed(*get_first(rs, chunk))
        for a in range(16):
            before, new = kept[a, pl.ds(8 * chunk, 8), :], x[a]
            weight, source = from_block(blocks, a, chunk, 1), from_block(blocks, a, chunk, 0)
            g, h = source + weight * before, before + new
            u1, z1 = source - step * g, before - step * h
            wz, wh = weight * z1, weight * h
            for q, (one, two) in enumerate(((u1, z1), (u1, h), (g, z1), (g, h), (wz, z1), (wz, h), (wh, h))):
                sums[q] += one * two
            place = 130 * place_of(a // 8, a // 2 % 4) + 16 * chunk + a % 2
            sent[pl.ds(place, 8, stride=2), :] = before
            sent[pl.ds(place + 64, 8, stride=2), :] = new
    lane = lax.broadcasted_iota(jnp.int32, (2, LANES), 1)
    line = jnp.where(lane == 7, n0, jnp.where(lane == 8, n1, jnp.where(lane >= 64, step, 0.0)))
    for q in range(7):
        line = jnp.where(lane == q, jnp.sum(sums[q], axis=(0, 1), keepdims=True), line)
    for i in range(8):
        sent[pl.ds(130 * i + 128, 2), :] = line


def gather_sums(received, sent):
    rows = received[pl.ds(128, 8, stride=130), :]
    for n in range(16):
        sent[pl.ds(8 * n, 8), :] = rows


def enter_block(received, parts, sources, metric, helm, solution, resid, near, done):
    copies = []
    lane = lax.broadcasted_iota(jnp.int32, (1, LANES), 1)
    row = lax.broadcasted_iota(jnp.int32, (LANES, LANES), 0)
    every = parts[...]
    steps = pltpu.roll(every, 64, 1)

    def total(line):
        return jnp.sum(line, axis=1, keepdims=True)

    def pick(line, q):
        return total(jnp.where(lane == q, line, 0.0))

    m = metric[...]
    inverse = 1.0 / m
    weight = helm[...] * inverse - SHIFT * m
    for f in range(2):
        mine = jnp.where(row % 2 == f, every, 0.0)
        zeroth = jnp.sum(mine, axis=0, keepdims=True)
        n0, n1 = pick(zeroth, 7), pick(zeroth, 8)
        delta = n0 + n1
        alpha, rest = n0 / delta, n1 / delta
        away = alpha - steps
        moved = away * mine
        first = jnp.sum(moved, axis=0, keepdims=True)
        second = jnp.sum(away * moved, axis=0, keepdims=True)
        once = (lane == 1) | (lane == 2)
        gamma = total(jnp.where(lane == 0, zeroth, jnp.where(once, -first, jnp.where(lane == 3, second, 0.0))))
        inner = total(jnp.where(lane == 4, zeroth, jnp.where(lane == 5, -2.0 * first, jnp.where(lane == 6, second, 0.0))))
        cross = total(jnp.where(lane == 2, zeroth, jnp.where(lane == 3, -first, 0.0)))
        beta = gamma / n0
        size = gamma / (gamma + inner + 2.0 * beta * cross + beta * beta * delta)
        c0, c1 = alpha + size * (rest + beta), -size * alpha
        for h in range(2):
            pair = []
            for field in range(2):
                places = [130 * place_of(f, quarter) + 64 * field + h for quarter in range(4)]
                columns = [received[pl.ds(place, BLOCK, stride=2), :] for place in places]
                pair.append(jnp.concatenate(columns, axis=0).T)
            old, new = pair
            rows = slice(LANES * h, LANES * (h + 1))
            near[0, f, rows, :] = (c0 * old + c1 * new) * inverse[rows]
            near[1, f, rows, :] = (1.0 - c0) * sources[f, rows, :] - ((c0 + c1) * old + c1 * new) * weight[rows]
        for n, out in enumerate((solution, resid)):
            copies.append(pltpu.make_async_copy(near.at[n, f], out.at[f], done.at[2 * n + f]))
            copies[-1].start()
    for copy in copies:
        copy.wait()


RS = pltpu.VMEM((16, 32, 2 * LANES), jnp.float32)
LINES = pltpu.VMEM((512, LANES), jnp.float32)
BLOCKS_SENT, SENT, SPECTRUM = (1024, LANES), (512, LANES), (512, LANES)
ENDS, KEPT = (2, 16, LANES), (16, 32, LANES)


def call(kernel, outs, scratch, **more):
    return pl.pallas_call(
        kernel,
        out_shape=[jax.ShapeDtypeStruct(s, jnp.float32) for s in outs],
        scratch_shapes=scratch,
        compiler_params=pltpu.CompilerParams(vmem_limit_bytes=32 * 1024 * 1024),
        **more,
    )


def far(*arrays):
    return [pltpu.with_memory_space_constraint(a, pltpu.HBM) for a in arrays]


def exchange(flat, axes, *shape):
    moved = lax.all_to_all(flat.reshape(*shape, LANES), axes, 0, 0, tiled=True)
    return moved.reshape(flat.shape)


def per_device(sources, metric, helm):
    table, waves = (jnp.asarray(a) for a in tables())
    line, column = ("pair", "core", "half"), ("gy", "pair", "core")
    here = lax.axis_index("gy") * lax.axis_size("pair") + lax.axis_index("pair")
    here = jnp.full((1, LANES), here, jnp.float32)
    core = jnp.full((1, LANES), lax.axis_index("core"), jnp.float32)
    block = pltpu.VMEM(metric.shape, metric.dtype)
    hbm, vmem = pl.BlockSpec(memory_space=pl.ANY), pl.BlockSpec(memory_space=pltpu.VMEM)

    def swap(ends):
        return lax.ppermute(ends, "core", [(0, 1), (1, 0)])

    (sent,) = call(
        leave_block,
        [BLOCKS_SENT],
        [pltpu.VMEM(sources.shape, sources.dtype), block, block, pltpu.SemaphoreType.DMA((4,))],
        in_specs=[hbm] * 5 + [vmem] * 2,
    )(*far(sources, metric, helm, table, waves), here, core)
    blocks = exchange(sent, line, 8, 128)
    first, ends = call(pencil_first, [SPECTRUM, ENDS], [RS])(blocks, table, waves)
    sibling = swap(ends)
    (sent,) = call(leave_lines, [SENT], [])(ends, sibling, waves, here, core)
    received = exchange(sent, column, 64, 8)
    second, more, kept, sums = call(pencil_middle, [SPECTRUM, ENDS, KEPT, (2, 8, LANES)], [RS, LINES])(
        received, blocks, first, ends, sibling, table, waves, here, core
    )
    twin = swap(more)
    (sent,) = call(leave_lines, [SENT], [])(more, twin, waves, here, core)
    received = exchange(sent, column, 64, 8)
    (sent,) = call(pencil_last, [(8 * 130, LANES)], [RS, LINES])(
        received, blocks, second, more, twin, kept, sums, table, waves, here, core
    )
    received = exchange(sent, line, 8, 65, 2)
    (parts,) = call(gather_sums, [(LANES, LANES)], [])(received)
    parts = exchange(parts, "gy", 16, 8)
    outs = call(
        enter_block,
        [sources.shape] * 2,
        [pltpu.VMEM((2, *sources.shape), jnp.float32), pltpu.SemaphoreType.DMA((4,))],
        in_specs=[vmem] * 5,
        out_specs=[hbm] * 2,
    )(received, parts, sources, metric, helm)
    return tuple(outs)


def solution(mesh):
    devices = mesh.devices.reshape(2, 2, 2, 16)
    finer = jax.sharding.Mesh(devices, ("half", "pair", "core", "gy"))
    line = ("half", "pair", "core")
    in_specs = (P(None, line, "gy"), P(line, "gy"), P(line, "gy"))
    out_specs = (P(None, line, "gy"), P(None, line, "gy"))
    return jax.shard_map(
        per_device, mesh=finer, in_specs=in_specs, out_specs=out_specs, check_vma=False
    )
```
